32 devices in a mesh: groups: 2 (over y), ctx: 4 (over z), head: 4 (over x, core).
Axes of the slice: x: 2, y: 2, z: 4, core: 2. Of those that a mesh axis runs over, the one named last changes fastest.
Arguments:
- queries: bfloat16 [1024, 6144], P(('groups', 'ctx'), 'head'), parts along dimension 0, may hold values from -128 to 128
- latent: bfloat16 [1024, 576], P(('groups', 'ctx')), parts along dimension 0, may hold values from -8 to 8
- w_keys: bfloat16 [512, 4096], P(None, 'head'), may hold values from -0.25 to 0.25
- w_values: bfloat16 [512, 4096], P(None, 'head'), may hold values from -0.25 to 0.25
- w_out: bfloat16 [4096, 3584], P('head'), may hold values from -0.375 to 0.375
- block_order: int32 [16], P('groups'), parts along dimension 0, may hold values from 0 to 7, as said below
- valid_lengths: int32 [16], P('groups'), parts along dimension 0, may hold values from 1 to 64, as said below
Outputs:
- mixed: bfloat16 [1024, 3584], P(('groups', 'ctx'), 'head'), parts along dimension 0
The draws below stay inside these ranges and needn't reach their ends.
There are 2 independent parts, one for each index of `groups`. The reference program is written for one: setup_inputs(seed, part) draws one part's arguments, and reference() takes and returns one part's arrays. A program takes and returns all parts, laid end to end along the dimension named above; an argument that names none is the same for every part. Nothing has to cross between parts.
Inputs may be any that keep to these rules, and one draw needn't show every extreme that they name: `block_order`: a permutation of 0 to 7. `valid_lengths`: the half-block at place 0 of the prompt is always whole.
All inputs are finite; a program needn't handle non-finite values.
Results may differ from the reference program's by a relative error of at most 0.012.
Values may be sent and summed in bfloat16 or wider, within the bound.
No kernel may reach another device: no remote copies, remote signals or barrier semaphores. Data moves between devices by JAX's collectives and lax.ppermute only.
A program may use at most 64 MiB of HBM per device.

```python
import jax
import jax.numpy as jnp
from jax import lax

LATENT = 512
ROPE = 64
HEAD_DIM = 128
HEADS = 32
D_OUT = 3584
HALF = 64
SLOTS = 8
TOKENS = 512


def shared_order(key):
    return jax.random.permutation(jax.random.fold_in(key, 5), SLOTS).astype(jnp.int32)


def shared_latent(key):
    return jax.random.normal(jax.random.fold_in(key, 21), (TOKENS, LATENT + ROPE), jnp.float32)


def draw_block_order(key, part):
    return shared_order(key)


def draw_valid_lengths(key, part):
    order = shared_order(key)
    key = jax.random.fold_in(key, 13)
    drawn = jax.random.randint(key, (SLOTS,), 1, HALF + 1, dtype=jnp.int32)
    return jnp.where(order == 0, HALF, drawn).astype(jnp.int32)


def draw_latent(key, part):
    base = shared_latent(key)
    values = jnp.clip(base, -6.0, 6.0)
    return values.astype(jnp.bfloat16)


def draw_queries(key, part):
    key = jax.random.fold_in(key, 41)
    width = HEAD_DIM + ROPE
    values = jnp.clip(2.5 * jax.random.normal(key, (TOKENS, HEADS, width), jnp.float32), -15.0, 15.0)
    return values.reshape(TOKENS, HEADS * width).astype(jnp.bfloat16)


def levels(stream_key, extent, shards, least, largest):
    loudness = 1.0
    for axis_at, blocks in shards:
        draws = jax.random.uniform(jax.random.fold_in(jax.random.fold_in(stream_key, 6), axis_at), (blocks,), jnp.float32, least / len(shards), largest / len(shards))
        loudness = loudness * jnp.repeat(jnp.exp(draws), extent[axis_at] // blocks).reshape((-1,) + (1,) * (len(extent) - 1 - axis_at))
    return loudness


def bell_draw(key, dims, scale, limit, cuts=(), kind=jnp.bfloat16):
    result = scale * jax.random.normal(key, dims, jnp.float32)
    if cuts:
        result = result * levels(key, dims, cuts, -0.22, 0.18)
    return jnp.clip(result, -limit, limit).astype(kind)


def setup_inputs(seed: int = 0, part: int = 0) -> dict:
    streams_of = jax.random.split(jax.random.key(seed), 8)
    part_keys = jax.random.split(jax.random.fold_in(streams_of[7], part), 8)
    return {
        "queries": draw_queries(jax.random.fold_in(jax.random.fold_in(streams_of[7], part), 71), part),
        "latent": draw_latent(jax.random.fold_in(jax.random.fold_in(streams_of[7], part), 71), part),
        "w_keys": bell_draw(streams_of[2], (LATENT, HEADS * HEAD_DIM), LATENT ** -0.5, 0.25, ((1, 4),)),
        "w_values": bell_draw(streams_of[3], (LATENT, HEADS * HEAD_DIM), LATENT ** -0.5, 0.25, ((1, 4),)),
        "w_out": bell_draw(streams_of[4], (HEADS * HEAD_DIM, D_OUT), (HEADS * HEAD_DIM // 16) ** -0.5, 0.375, ((0, 4),)),
        "block_order": draw_block_order(jax.random.fold_in(jax.random.fold_in(streams_of[7], part), 71), part),
        "valid_lengths": draw_valid_lengths(jax.random.fold_in(jax.random.fold_in(streams_of[7], part), 71), part),
    }


def reference(queries, latent, w_keys, w_values, w_out, block_order, valid_lengths):
    tok_count = latent.shape[0]
    head_count = w_keys.shape[1] // HEAD_DIM
    score_scale = (HEAD_DIM + ROPE) ** -0.5
    compressed = latent[:, :LATENT]
    key_rope = latent[:, LATENT:]
    key_nope = jnp.dot(compressed, w_keys, preferred_element_type=jnp.float32).astype(jnp.bfloat16)
    value_heads = jnp.dot(compressed, w_values, preferred_element_type=jnp.float32).astype(jnp.bfloat16)
    key_nope = key_nope.reshape(tok_count, head_count, HEAD_DIM).transpose(1, 0, 2)
    value_heads = value_heads.reshape(tok_count, head_count, HEAD_DIM).transpose(1, 0, 2)
    shaped = queries.reshape(tok_count, head_count, HEAD_DIM + ROPE).transpose(1, 0, 2)
    index_all = jnp.arange(tok_count, dtype=jnp.int32)
    slot_of = (index_all // HALF).astype(jnp.int32)
    offset_of = (index_all % HALF).astype(jnp.int32)
    position = block_order[slot_of] * HALF + offset_of
    valid_key = offset_of < valid_lengths[slot_of]
    visible = (position[None, :] <= position[:, None]) & valid_key[None, :]

    def one_head(pieces):
        query_head, keys_head, values_head = pieces
        scores = jnp.dot(query_head[:, :HEAD_DIM], keys_head.T, preferred_element_type=jnp.float32)
        scores = scores + jnp.dot(query_head[:, HEAD_DIM:], key_rope.T, preferred_element_type=jnp.float32)
        scores = jnp.where(visible, scores * score_scale, jnp.float32(-1e30))
        row_peak = jnp.max(scores, axis=1, keepdims=True)
        weights = jnp.where(visible, jnp.exp(scores - row_peak), jnp.float32(0.0))
        denom = jnp.sum(weights, axis=1, keepdims=True)
        summed = jnp.dot(weights.astype(jnp.bfloat16), values_head, preferred_element_type=jnp.float32)
        return (summed / denom).astype(jnp.bfloat16)

    attended = lax.map(one_head, (shaped, key_nope, value_heads))
    attended = attended.transpose(1, 0, 2).reshape(tok_count, head_count * HEAD_DIM)
    return jnp.dot(attended, w_out, preferred_element_type=jnp.float32).astype(jnp.bfloat16)
```

```python
import functools

import jax
import jax.numpy as jnp
from jax import lax
from jax.experimental import pallas as pl
from jax.experimental.pallas import tpu as pltpu
from jax.sharding import PartitionSpec as P

LATENT = 512
ROPE = 64
HEAD_DIM = 128
QUERY = HEAD_DIM + ROPE
PARTS = 4
ROWS_AT_ONCE = 256
NT = (((1,), (1,)), ((), ()))
VMEM_BYTES = 48 * 1024 * 1024


def shifted(value, axis, steps):
    count = lax.axis_size(axis)
    return lax.ppermute(value, axis, [(i, (i + steps) % count) for i in range(count)])


def crossed(value, axis, bit):
    count = lax.axis_size(axis)
    return lax.ppermute(value, axis, [(i, i ^ bit) for i in range(count)])


def fold_keys_kernel(queries_ref, w_keys_ref, folded_ref):
    rows = queries_ref.shape[0]
    for head in range(w_keys_ref.shape[1] // HEAD_DIM):
        nope = queries_ref[:, head * QUERY : head * QUERY + HEAD_DIM]
        rope = queries_ref[:, head * QUERY + HEAD_DIM : (head + 1) * QUERY]
        weight = w_keys_ref[:, head * HEAD_DIM : (head + 1) * HEAD_DIM]
        here = slice(head * rows, (head + 1) * rows)
        product = lax.dot_general(nope, weight, NT, preferred_element_type=jnp.float32)
        folded_ref[here, :LATENT] = product.astype(jnp.bfloat16)
        folded_ref[here, LATENT:] = rope


def fold_keys(queries, w_keys):
    rows = queries.shape[0]
    heads = w_keys.shape[1] // HEAD_DIM
    return pl.pallas_call(
        fold_keys_kernel,
        out_shape=jax.ShapeDtypeStruct((heads * rows, LATENT + ROPE), jnp.bfloat16),
        in_specs=[pl.BlockSpec(memory_space=pltpu.VMEM)] * 2,
        out_specs=pl.BlockSpec(memory_space=pltpu.VMEM),
        compiler_params=pltpu.CompilerParams(vmem_limit_bytes=VMEM_BYTES),
        cost_estimate=pl.CostEstimate(
            flops=2 * rows * heads * HEAD_DIM * LATENT,
            bytes_accessed=2 * (queries.size + w_keys.size + heads * rows * (LATENT + ROPE)),
            transcendentals=0,
        ),
        name="fold_keys",
    )(queries, w_keys)


def attend_kernel(count, rows, order_ref, lens_ref, place_ref, folded_ref, w_values_ref, w_out_ref, *rest):
    blocks, rest = rest[:count], rest[count:]
    outs, rest = rest[:PARTS], rest[PARTS:]
    keys_ref, w_part_ref, attended_ref, block_sems, part_sems = rest
    half = rows // 2
    width = w_out_ref.shape[1] // PARTS
    heads = w_values_ref.shape[1] // HEAD_DIM
    exponent = (HEAD_DIM + ROPE) ** -0.5 * 1.4426950408889634
    ctx = place_ref[0]

    block_copies = []
    for step in range(count):
        copy = pltpu.make_async_copy(
            blocks[step], keys_ref.at[pl.ds(step * rows, rows)], block_sems.at[step]
        )
        copy.start()
        block_copies.append(copy)
    part_copies = []
    for part in range(PARTS):
        start = pl.multiple_of(place_ref[1 + part] * width, 128)
        copy = pltpu.make_async_copy(
            w_out_ref.at[:, pl.ds(start, width)], w_part_ref.at[part], part_sems.at[part]
        )
        copy.start()
        part_copies.append(copy)

    row = lax.broadcasted_iota(jnp.int32, (rows, rows), 0)
    lane = lax.broadcasted_iota(jnp.int32, (rows, rows), 1)
    query_pos = jnp.where(row < half, order_ref[2 * ctx], order_ref[2 * ctx + 1]) * half + row % half
    seen = []
    for step in range(count):
        source = lax.rem(ctx + (count - step), count)
        first, second = 2 * source, 2 * source + 1
        offset = lane % half
        key_pos = jnp.where(lane < half, order_ref[first], order_ref[second]) * half + offset
        length = jnp.where(lane < half, lens_ref[first], lens_ref[second])
        seen.append((key_pos <= query_pos) & (offset < length))
    visible = jnp.concatenate(seen, axis=1)
    stacked = ROWS_AT_ONCE // rows
    visible = jnp.concatenate([visible] * stacked, axis=0)

    for copy in block_copies:
        copy.wait()
    for group in range(heads // stacked):
        lines = slice(group * ROWS_AT_ONCE, (group + 1) * ROWS_AT_ONCE)
        scores = lax.dot_general(
            folded_ref[lines, :], keys_ref[...], NT, preferred_element_type=jnp.float32
        )
        scores = jnp.where(visible, scores, jnp.float32(-1e30))
        peak = jnp.max(scores, axis=1, keepdims=True)
        weights = jnp.exp2((scores - peak) * jnp.float32(exponent))
        total = jnp.sum(weights, axis=1, keepdims=True)
        mixed = jnp.dot(
            weights.astype(jnp.bfloat16), keys_ref[:, :LATENT], preferred_element_type=jnp.float32
        )
        mixed = (mixed / total).astype(jnp.bfloat16)
        for inner in range(stacked):
            head = group * stacked + inner
            columns = slice(head * HEAD_DIM, (head + 1) * HEAD_DIM)
            value = jnp.dot(
                mixed[inner * rows : (inner + 1) * rows, :],
                w_values_ref[:, columns],
                preferred_element_type=jnp.float32,
            )
            attended_ref[:, columns] = value.astype(jnp.bfloat16)

    for part in range(PARTS):
        part_copies[part].wait()
        outs[part][...] = jnp.dot(
            attended_ref[...], w_part_ref[part], preferred_element_type=jnp.float32
        ).astype(outs[part].dtype)


def attend(folded, blocks, w_values, w_out, block_order, valid_lengths, place, out_types):
    count = len(blocks)
    rows = blocks[0].shape[0]
    width = w_out.shape[1] // PARTS
    heads = w_values.shape[1] // HEAD_DIM
    keys = count * rows
    flops = 2 * heads * rows * (keys * (2 * LATENT + ROPE) + LATENT * HEAD_DIM)
    flops += 2 * rows * w_out.size
    smem = pl.BlockSpec(memory_space=pltpu.SMEM)
    vmem = pl.BlockSpec(memory_space=pltpu.VMEM)
    hbm = pl.BlockSpec(memory_space=pl.ANY)
    return pl.pallas_call(
        functools.partial(attend_kernel, count, rows),
        out_shape=[jax.ShapeDtypeStruct((rows, width), kind) for kind in out_types],
        in_specs=[smem, smem, smem, vmem, vmem, hbm] + [hbm] * count,
        out_specs=[vmem] * PARTS,
        scratch_shapes=[
            pltpu.VMEM((keys, LATENT + ROPE), jnp.bfloat16),
            pltpu.VMEM((PARTS, w_out.shape[0], width), jnp.bfloat16),
            pltpu.VMEM((rows, heads * HEAD_DIM), jnp.bfloat16),
            pltpu.SemaphoreType.DMA((count,)),
            pltpu.SemaphoreType.DMA((PARTS,)),
        ],
        compiler_params=pltpu.CompilerParams(vmem_limit_bytes=VMEM_BYTES),
        cost_estimate=pl.CostEstimate(
            flops=flops,
            bytes_accessed=2 * (folded.size + w_values.size + w_out.size + keys * (LATENT + ROPE)),
            transcendentals=heads * rows * keys,
        ),
        name="attend",
    )(block_order, valid_lengths, place, folded, w_values, w_out, *blocks)


def shards(queries, latent, w_keys, w_values, w_out, block_order, valid_lengths):
    ctx_count = lax.axis_size("ctx")
    head_count = lax.axis_size("head")
    ctx_place = lax.axis_index("ctx")
    head_place = lax.axis_index("head")
    blocks = [latent] + [shifted(latent, "ctx", step) for step in range(1, ctx_count)]
    folded = fold_keys(queries, w_keys)
    pairwise = head_count == 4
    if pairwise:
        parts = [head_place ^ 3, head_place ^ 1, head_place ^ 2, head_place]
        out_types = [jnp.bfloat16, jnp.bfloat16, jnp.float32, jnp.float32]
    else:
        parts = list(range(PARTS))
        out_types = [jnp.bfloat16] * PARTS
    place = jnp.stack([jnp.int32(item) for item in [ctx_place] + parts])
    across, beside, far, own = attend(
        folded, blocks, w_values, w_out, block_order, valid_lengths, place, out_types
    )
    if not pairwise:
        whole = jnp.concatenate([across, beside, far, own], axis=1)
        return lax.psum_scatter(whole, "head", scatter_dimension=1, tiled=True)
    far = far + crossed(across, "head", 1).astype(jnp.float32)
    near = crossed(beside, "head", 1).astype(jnp.float32)
    far = crossed(far.astype(jnp.bfloat16), "head", 2).astype(jnp.float32)
    return (own + near + far).astype(jnp.bfloat16)


def solution(mesh):
    in_specs = (
        P(("groups", "ctx"), "head"),
        P(("groups", "ctx"), None),
        P(None, "head"),
        P(None, "head"),
        P("head", None),
        P("groups"),
        P("groups"),
    )
    out_specs = P(("groups", "ctx"), "head")
    return jax.shard_map(shards, mesh=mesh, in_specs=in_specs, out_specs=out_specs, check_vma=False)
```

```python
import functools

import jax
import jax.numpy as jnp
from jax import lax
from jax.experimental import pallas as pl
from jax.experimental.pallas import tpu as pltpu
from jax.sharding import PartitionSpec as P

LATENT = 512
ROPE = 64
HEAD_DIM = 128
QUERY = HEAD_DIM + ROPE
PARTS = 4
ROWS_AT_ONCE = 256
NT = (((1,), (1,)), ((), ()))
VMEM_BYTES = 32 * 1024 * 1024
HIDDEN = -1e30


def routed(value, route):
    ctx_count = lax.axis_size("ctx")
    head_count = lax.axis_size("head")
    pairs = []
    for ctx in range(ctx_count):
        for head in range(head_count):
            target = route(ctx, head)
            if target is not None:
                pairs.append((ctx * head_count + head, target[0] * head_count + target[1]))
    return lax.ppermute(value, ("ctx", "head"), pairs)


def is_paired():
    return lax.axis_size("ctx") == 4 and lax.axis_size("head") == 4


def key_sources():
    count = lax.axis_size("ctx")
    ctx = lax.axis_index("ctx")
    if is_paired():
        step = 1 + 2 * (lax.axis_index("head") & 1)
        return [ctx, (ctx - step) & 3, (ctx + step) & 3, ctx ^ 2]
    return [ctx] + [lax.rem(ctx + (count - step), count) for step in range(1, count)]


def part_order():
    if is_paired():
        head = lax.axis_index("head")
        return [head ^ 3, head ^ 1, head ^ 2, head]
    return list(range(PARTS))


def prepare_kernel(
    rows,
    order_hbm,
    lens_hbm,
    queries_ref,
    w_keys_ref,
    w_values_ref,
    w_out_ref,
    folded_ref,
    bias_ref,
    values_ref,
    parts_ref,
    order_ref,
    lens_ref,
    query_buffer,
    key_buffer,
    sems,
    part_sems,
):
    half = rows // 2
    width = w_out_ref.shape[1] // PARTS
    scalars = [
        pltpu.make_async_copy(order_hbm, order_ref, sems.at[3]),
        pltpu.make_async_copy(lens_hbm, lens_ref, sems.at[4]),
    ]
    first = [
        pltpu.make_async_copy(queries_ref, query_buffer, sems.at[0]),
        pltpu.make_async_copy(w_keys_ref, key_buffer, sems.at[1]),
    ]
    later = [pltpu.make_async_copy(w_values_ref, values_ref, sems.at[2])]
    for slot, part in enumerate(part_order()):
        start = pl.multiple_of(part * width, 128)
        later.append(
            pltpu.make_async_copy(
                w_out_ref.at[:, pl.ds(start, width)], parts_ref.at[slot], part_sems.at[slot]
            )
        )
    for copy in scalars + first + later:
        copy.start()

    for copy in scalars:
        copy.wait()
    ctx = lax.axis_index("ctx")
    row = lax.broadcasted_iota(jnp.int32, (rows, rows), 0)
    lane = lax.broadcasted_iota(jnp.int32, (rows, rows), 1)
    query_pos = jnp.where(row < half, order_ref[2 * ctx], order_ref[2 * ctx + 1]) * half + row % half
    offset = lane % half
    for step, source in enumerate(key_sources()):
        key_place = jnp.where(lane < half, order_ref[2 * source], order_ref[2 * source + 1])
        length = jnp.where(lane < half, lens_ref[2 * source], lens_ref[2 * source + 1])
        visible = (key_place * half + offset <= query_pos) & (offset < length)
        bias_ref[:, step * rows : (step + 1) * rows] = jnp.where(visible, 0.0, HIDDEN)

    for copy in first:
        copy.wait()
    for head in range(w_keys_ref.shape[1] // HEAD_DIM):
        nope = query_buffer[:, head * QUERY : head * QUERY + HEAD_DIM]
        rope = query_buffer[:, head * QUERY + HEAD_DIM : (head + 1) * QUERY]
        weight = key_buffer[:, head * HEAD_DIM : (head + 1) * HEAD_DIM]
        here = slice(head * rows, (head + 1) * rows)
        product = lax.dot_general(nope, weight, NT, preferred_element_type=jnp.float32)
        folded_ref[here, :LATENT] = product.astype(jnp.bfloat16)
        folded_ref[here, LATENT:] = rope
    for copy in later:
        copy.wait()


def prepare(*operands):
    order, lens, queries, w_keys, w_values, w_out = operands
    rows = queries.shape[0]
    count = lax.axis_size("ctx")
    heads = w_keys.shape[1] // HEAD_DIM
    vmem = pl.BlockSpec(memory_space=pltpu.VMEM)
    hbm = pl.BlockSpec(memory_space=pltpu.HBM)
    return pl.pallas_call(
        functools.partial(prepare_kernel, rows),
        out_shape=[
            jax.ShapeDtypeStruct((heads * rows, LATENT + ROPE), jnp.bfloat16),
            jax.ShapeDtypeStruct((rows, count * rows), jnp.float32),
            jax.ShapeDtypeStruct(w_values.shape, jnp.bfloat16),
            jax.ShapeDtypeStruct((PARTS, w_out.shape[0], w_out.shape[1] // PARTS), jnp.bfloat16),
        ],
        in_specs=[hbm] * 6,
        out_specs=[vmem] * 4,
        scratch_shapes=[
            pltpu.SMEM(order.shape, jnp.int32),
            pltpu.SMEM(lens.shape, jnp.int32),
            pltpu.VMEM(queries.shape, jnp.bfloat16),
            pltpu.VMEM(w_keys.shape, jnp.bfloat16),
            pltpu.SemaphoreType.DMA((5,)),
            pltpu.SemaphoreType.DMA((PARTS,)),
        ],
        compiler_params=pltpu.CompilerParams(vmem_limit_bytes=VMEM_BYTES),
        cost_estimate=pl.CostEstimate(
            flops=2 * rows * heads * HEAD_DIM * LATENT,
            bytes_accessed=2 * (queries.size + w_keys.size + w_values.size + w_out.size),
            transcendentals=0,
        ),
        name="prepare",
    )(*[pltpu.with_memory_space_constraint(item, pltpu.HBM) for item in operands])


def attend_kernel(count, folded_ref, bias_ref, values_ref, parts_ref, *rest):
    blocks, rest = rest[: count + 1], rest[count + 1 :]
    outs, rest = rest[:PARTS], rest[PARTS:]
    keys_ref, attended_ref = rest
    rows = bias_ref.shape[0]
    heads = values_ref.shape[1] // HEAD_DIM
    exponent = QUERY**-0.5 * 1.4426950408889634

    for step in range(count - 1):
        keys_ref[:, step * rows : (step + 1) * rows] = blocks[step][...]
    last = slice((count - 1) * rows, count * rows)

    direct = (lax.axis_index("ctx") ^ lax.axis_index("head")) & 1 == 0

    @pl.when(direct)
    def _():
        keys_ref[:, last] = blocks[count - 1][...]

    @pl.when(jnp.logical_not(direct))
    def _():
        keys_ref[:, last] = blocks[count][...]

    stacked = ROWS_AT_ONCE // rows
    bias = jnp.concatenate([bias_ref[...]] * stacked, axis=0)
    for group in range(heads // stacked):
        lines = slice(group * ROWS_AT_ONCE, (group + 1) * ROWS_AT_ONCE)
        scores = jnp.dot(folded_ref[lines, :], keys_ref[...], preferred_element_type=jnp.float32)
        scores = scores + bias
        peak = jnp.max(scores, axis=1, keepdims=True)
        weights = jnp.exp2((scores - peak) * jnp.float32(exponent))
        total = jnp.sum(weights, axis=1, keepdims=True)
        mixed = lax.dot_general(
            weights.astype(jnp.bfloat16), keys_ref[:LATENT, :], NT, preferred_element_type=jnp.float32
        )
        mixed = (mixed / total).astype(jnp.bfloat16)
        for inner in range(stacked):
            head = group * stacked + inner
            columns = slice(head * HEAD_DIM, (head + 1) * HEAD_DIM)
            value = jnp.dot(
                mixed[inner * rows : (inner + 1) * rows, :],
                values_ref[:, columns],
                preferred_element_type=jnp.float32,
            )
            attended_ref[:, columns] = value.astype(jnp.bfloat16)

    for part in range(PARTS):
        outs[part][...] = jnp.dot(
            attended_ref[...], parts_ref[part], preferred_element_type=jnp.float32
        ).astype(outs[part].dtype)


def attend(prepared, blocks, out_types):
    folded, bias, values, parts = prepared
    rows, keys = bias.shape
    heads = values.shape[1] // HEAD_DIM
    width = parts.shape[2]
    flops = 2 * heads * rows * (keys * (2 * LATENT + ROPE) + LATENT * HEAD_DIM)
    flops += 2 * rows * parts.size
    vmem = pl.BlockSpec(memory_space=pltpu.VMEM)
    return pl.pallas_call(
        functools.partial(attend_kernel, keys // rows),
        out_shape=[jax.ShapeDtypeStruct((rows, width), kind) for kind in out_types],
        in_specs=[vmem] * (4 + len(blocks)),
        out_specs=[vmem] * PARTS,
        scratch_shapes=[
            pltpu.VMEM((LATENT + ROPE, keys), jnp.bfloat16),
            pltpu.VMEM((rows, heads * HEAD_DIM), jnp.bfloat16),
        ],
        compiler_params=pltpu.CompilerParams(vmem_limit_bytes=VMEM_BYTES),
        cost_estimate=pl.CostEstimate(
            flops=flops,
            bytes_accessed=2 * (folded.size + values.size + parts.size + keys * (LATENT + ROPE)),
            transcendentals=heads * rows * keys,
        ),
        name="attend",
    )(folded, bias, values, parts, *blocks)


def shards(queries, latent, w_keys, w_values, w_out, block_order, valid_lengths):
    ctx_count = lax.axis_size("ctx")
    block = latent.T
    prepared = prepare(block_order, valid_lengths, queries, w_keys, w_values, w_out)

    if not is_paired():
        blocks = [block]
        for step in range(1, ctx_count):
            blocks.append(routed(block, lambda ctx, head: ((ctx + step) % ctx_count, head)))
        blocks.append(blocks[-1])
        shares = attend(prepared, blocks, [jnp.bfloat16] * PARTS)
        whole = jnp.concatenate(shares, axis=1)
        return lax.psum_scatter(whole, "head", scatter_dimension=1, tiled=True)

    def next_to(ctx, head):
        return (ctx + 1 + 2 * (head & 1)) & 3, head

    def two_away(ctx, head):
        return (ctx ^ 2, head) if (ctx ^ head) & 1 == 0 else None

    def other_core(ctx, head):
        return ctx, head ^ 1

    def other_core_two_away(ctx, head):
        return (ctx, head ^ 1) if (ctx ^ head) & 1 == 0 else None

    near = routed(block, next_to)
    far = routed(block, two_away)
    near, far, prepared = lax.optimization_barrier((near, far, prepared))
    near_swapped = routed(near, other_core)
    far_swapped = routed(far, other_core_two_away)
    across, beside, far, own = attend(
        prepared,
        [block, near, near_swapped, far, far_swapped],
        [jnp.bfloat16, jnp.bfloat16, jnp.float32, jnp.float32],
    )
    far = far + routed(across, other_core).astype(jnp.float32)
    near = routed(beside, other_core).astype(jnp.float32)
    far = routed(far.astype(jnp.bfloat16), lambda ctx, head: (ctx, head ^ 2)).astype(jnp.float32)
    return (own + near + far).astype(jnp.bfloat16)


def solution(mesh):
    in_specs = (
        P(("groups", "ctx"), "head"),
        P(("groups", "ctx"), None),
        P(None, "head"),
        P(None, "head"),
        P("head", None),
        P("groups"),
        P("groups"),
    )
    out_specs = P(("groups", "ctx"), "head")
    return jax.shard_map(shards, mesh=mesh, in_specs=in_specs, out_specs=out_specs, check_vma=False)
```

```python
import functools

import jax
import jax.numpy as jnp
from jax import lax
from jax.experimental import pallas as pl
from jax.experimental.pallas import tpu as pltpu
from jax.sharding import PartitionSpec as P

LATENT = 512
ROPE = 64
HEAD_DIM = 128
QUERY = HEAD_DIM + ROPE
PARTS = 4
ROWS_AT_ONCE = 256
NT = (((1,), (1,)), ((), ()))
VMEM_BYTES = 32 * 1024 * 1024
HIDDEN = -1e30


def routed(value, route):
    ctx_count = lax.axis_size("ctx")
    head_count = lax.axis_size("head")
    pairs = []
    for ctx in range(ctx_count):
        for head in range(head_count):
            target = route(ctx, head)
            if target is not None:
                pairs.append((ctx * head_count + head, target[0] * head_count + target[1]))
    return lax.ppermute(value, ("ctx", "head"), pairs)


def is_paired():
    return lax.axis_size("ctx") == 4 and lax.axis_size("head") == 4


def key_sources():
    count = lax.axis_size("ctx")
    ctx = lax.axis_index("ctx")
    if is_paired():
        step = 1 + 2 * (lax.axis_index("head") & 1)
        return [ctx, (ctx - step) & 3, (ctx + step) & 3, ctx ^ 2]
    return [ctx] + [lax.rem(ctx + (count - step), count) for step in range(1, count)]


def part_order():
    if is_paired():
        head = lax.axis_index("head")
        return [head ^ 3, head ^ 1, head ^ 2, head]
    return list(range(PARTS))


def prepare_kernel(
    rows,
    order_hbm,
    lens_hbm,
    queries_ref,
    w_keys_ref,
    w_values_ref,
    w_out_ref,
    folded_ref,
    bias_ref,
    values_ref,
    parts_ref,
    order_ref,
    lens_ref,
    query_buffer,
    key_buffer,
    sems,
    part_sems,
):
    half = rows // 2
    width = w_out_ref.shape[1] // PARTS
    scalars = [
        pltpu.make_async_copy(order_hbm, order_ref, sems.at[3]),
        pltpu.make_async_copy(lens_hbm, lens_ref, sems.at[4]),
    ]
    first = [
        pltpu.make_async_copy(queries_ref, query_buffer, sems.at[0]),
        pltpu.make_async_copy(w_keys_ref, key_buffer, sems.at[1]),
    ]
    later = [pltpu.make_async_copy(w_values_ref, values_ref, sems.at[2])]
    for slot, part in enumerate(part_order()):
        start = pl.multiple_of(part * width, 128)
        later.append(
            pltpu.make_async_copy(
                w_out_ref.at[:, pl.ds(start, width)], parts_ref.at[slot], part_sems.at[slot]
            )
        )
    for copy in scalars + first + later:
        copy.start()

    for copy in scalars:
        copy.wait()
    ctx = lax.axis_index("ctx")
    row = lax.broadcasted_iota(jnp.int32, (rows, rows), 0)
    lane = lax.broadcasted_iota(jnp.int32, (rows, rows), 1)
    query_pos = jnp.where(row < half, order_ref[2 * ctx], order_ref[2 * ctx + 1]) * half + row % half
    offset = lane % half
    for step, source in enumerate(key_sources()):
        key_place = jnp.where(lane < half, order_ref[2 * source], order_ref[2 * source + 1])
        length = jnp.where(lane < half, lens_ref[2 * source], lens_ref[2 * source + 1])
        visible = (key_place * half + offset <= query_pos) & (offset < length)
        bias_ref[:, step * rows : (step + 1) * rows] = jnp.where(visible, 0.0, HIDDEN)

    for copy in first:
        copy.wait()
    for head in range(w_keys_ref.shape[1] // HEAD_DIM):
        nope = query_buffer[:, head * QUERY : head * QUERY + HEAD_DIM]
        rope = query_buffer[:, head * QUERY + HEAD_DIM : (head + 1) * QUERY]
        weight = key_buffer[:, head * HEAD_DIM : (head + 1) * HEAD_DIM]
        here = slice(head * rows, (head + 1) * rows)
        product = lax.dot_general(nope, weight, NT, preferred_element_type=jnp.float32)
        folded_ref[here, :LATENT] = product.astype(jnp.bfloat16)
        folded_ref[here, LATENT:] = rope
    for copy in later:
        copy.wait()


def prepare(*operands):
    order, lens, queries, w_keys, w_values, w_out = operands
    rows = queries.shape[0]
    count = lax.axis_size("ctx")
    heads = w_keys.shape[1] // HEAD_DIM
    vmem = pl.BlockSpec(memory_space=pltpu.VMEM)
    hbm = pl.BlockSpec(memory_space=pltpu.HBM)
    return pl.pallas_call(
        functools.partial(prepare_kernel, rows),
        out_shape=[
            jax.ShapeDtypeStruct((heads * rows, LATENT + ROPE), jnp.bfloat16),
            jax.ShapeDtypeStruct((rows, count * rows), jnp.float32),
            jax.ShapeDtypeStruct(w_values.shape, jnp.bfloat16),
            jax.ShapeDtypeStruct((PARTS, w_out.shape[0], w_out.shape[1] // PARTS), jnp.bfloat16),
        ],
        in_specs=[hbm] * 6,
        out_specs=[vmem] * 4,
        scratch_shapes=[
            pltpu.SMEM(order.shape, jnp.int32),
            pltpu.SMEM(lens.shape, jnp.int32),
            pltpu.VMEM(queries.shape, jnp.bfloat16),
            pltpu.VMEM(w_keys.shape, jnp.bfloat16),
            pltpu.SemaphoreType.DMA((5,)),
            pltpu.SemaphoreType.DMA((PARTS,)),
        ],
        compiler_params=pltpu.CompilerParams(vmem_limit_bytes=VMEM_BYTES),
        cost_estimate=pl.CostEstimate(
            flops=2 * rows * heads * HEAD_DIM * LATENT,
            bytes_accessed=2 * (queries.size + w_keys.size + w_values.size + w_out.size),
            transcendentals=0,
        ),
        name="prepare",
    )(*[pltpu.with_memory_space_constraint(item, pltpu.HBM) for item in operands])


def attend_kernel(count, folded_ref, bias_ref, values_ref, parts_ref, *rest):
    blocks, rest = rest[: count + 1], rest[count + 1 :]
    outs, rest = rest[:PARTS], rest[PARTS:]
    keys_ref, attended_ref = rest
    rows = bias_ref.shape[0]
    heads = values_ref.shape[1] // HEAD_DIM
    exponent = QUERY**-0.5 * 1.4426950408889634

    for step in range(count - 1):
        keys_ref[:, step * rows : (step + 1) * rows] = blocks[step][...]
    last = slice((count - 1) * rows, count * rows)

    direct = (lax.axis_index("ctx") ^ lax.axis_index("head")) & 1 == 0

    @pl.when(direct)
    def _():
        keys_ref[:, last] = blocks[count - 1][...]

    @pl.when(jnp.logical_not(direct))
    def _():
        keys_ref[:, last] = blocks[count][...]

    stacked = ROWS_AT_ONCE // rows
    bias = jnp.concatenate([bias_ref[...]] * stacked, axis=0)
    for group in range(heads // stacked):
        lines = slice(group * ROWS_AT_ONCE, (group + 1) * ROWS_AT_ONCE)
        scores = jnp.dot(folded_ref[lines, :], keys_ref[...], preferred_element_type=jnp.float32)
        scores = scores + bias
        peak = jnp.max(scores, axis=1, keepdims=True)
        weights = jnp.exp2((scores - peak) * jnp.float32(exponent))
        total = jnp.sum(weights, axis=1, keepdims=True)
        mixed = lax.dot_general(
            weights.astype(jnp.bfloat16), keys_ref[:LATENT, :], NT, preferred_element_type=jnp.float32
        )
        mixed = (mixed / total).astype(jnp.bfloat16)
        for inner in range(stacked):
            head = group * stacked + inner
            columns = slice(head * HEAD_DIM, (head + 1) * HEAD_DIM)
            value = jnp.dot(
                mixed[inner * rows : (inner + 1) * rows, :],
                values_ref[:, columns],
                preferred_element_type=jnp.float32,
            )
            attended_ref[:, columns] = value.astype(jnp.bfloat16)

    for part in range(PARTS):
        outs[part][...] = jnp.dot(
            attended_ref[...], parts_ref[part], preferred_element_type=jnp.float32
        ).astype(outs[part].dtype)


def attend(prepared, blocks, out_types):
    folded, bias, values, parts = prepared
    rows, keys = bias.shape
    heads = values.shape[1] // HEAD_DIM
    width = parts.shape[2]
    flops = 2 * heads * rows * (keys * (2 * LATENT + ROPE) + LATENT * HEAD_DIM)
    flops += 2 * rows * parts.size
    vmem = pl.BlockSpec(memory_space=pltpu.VMEM)
    return pl.pallas_call(
        functools.partial(attend_kernel, keys // rows),
        out_shape=[jax.ShapeDtypeStruct((rows, width), kind) for kind in out_types],
        in_specs=[vmem] * (4 + len(blocks)),
        out_specs=[vmem] * PARTS,
        scratch_shapes=[
            pltpu.VMEM((LATENT + ROPE, keys), jnp.bfloat16),
            pltpu.VMEM((rows, heads * HEAD_DIM), jnp.bfloat16),
        ],
        compiler_params=pltpu.CompilerParams(vmem_limit_bytes=VMEM_BYTES),
        cost_estimate=pl.CostEstimate(
            flops=flops,
            bytes_accessed=2 * (folded.size + values.size + parts.size + keys * (LATENT + ROPE)),
            transcendentals=heads * rows * keys,
        ),
        name="attend",
    )(folded, bias, values, parts, *blocks)


def shards(queries, latent, w_keys, w_values, w_out, block_order, valid_lengths):
    ctx_count = lax.axis_size("ctx")
    block = latent.T
    prepared = prepare(block_order, valid_lengths, queries, w_keys, w_values, w_out)

    if not is_paired():
        blocks = [block]
        for step in range(1, ctx_count):
            blocks.append(routed(block, lambda ctx, head: ((ctx + step) % ctx_count, head)))
        blocks.append(blocks[-1])
        shares = attend(prepared, blocks, [jnp.bfloat16] * PARTS)
        whole = jnp.concatenate(shares, axis=1)
        return lax.psum_scatter(whole, "head", scatter_dimension=1, tiled=True)

    def next_to(ctx, head):
        return (ctx + 1 + 2 * (head & 1)) & 3, head

    def two_away(ctx, head):
        return (ctx ^ 2 if (ctx ^ head) & 1 == 0 else ctx), head

    def other_core(ctx, head):
        return ctx, head ^ 1

    def other_chip(ctx, head):
        return ctx, head ^ 2

    near = routed(block, next_to)
    far = routed(block, two_away)
    near, prepared = lax.optimization_barrier((near, prepared))
    near_swapped = routed(near, other_core)
    far, _ = lax.optimization_barrier((far, near))
    far_swapped = routed(far, other_core)
    across, beside, far_part, own = attend(
        prepared,
        [block, near, near_swapped, far, far_swapped],
        [jnp.bfloat16, jnp.bfloat16, jnp.float32, jnp.float32],
    )
    far_part = (far_part + routed(across, other_core).astype(jnp.float32)).astype(jnp.bfloat16)
    far_part, beside = lax.optimization_barrier((far_part, beside))
    far_part = routed(far_part, other_chip).astype(jnp.float32)
    beside = routed(beside, other_core).astype(jnp.float32)
    return (own + beside + far_part).astype(jnp.bfloat16)


def solution(mesh):
    in_specs = (
        P(("groups", "ctx"), "head"),
        P(("groups", "ctx"), None),
        P(None, "head"),
        P(None, "head"),
        P("head", None),
        P("groups"),
        P("groups"),
    )
    out_specs = P(("groups", "ctx"), "head")
    return jax.shard_map(shards, mesh=mesh, in_specs=in_specs, out_specs=out_specs, check_vma=False)
```

```python
import functools

import jax
import jax.numpy as jnp
from jax import lax
from jax.experimental import pallas as pl
from jax.experimental.pallas import tpu as pltpu
from jax.sharding import PartitionSpec as P

LATENT = 512
ROPE = 64
HEAD_DIM = 128
QUERY = HEAD_DIM + ROPE
PARTS = 4
ROWS_AT_ONCE = 256
NT = (((1,), (1,)), ((), ()))
VMEM_BYTES = 32 * 1024 * 1024
HIDDEN = -1e30


def routed(value, route):
    ctx_count = lax.axis_size("ctx")
    head_count = lax.axis_size("head")
    pairs = []
    for ctx in range(ctx_count):
        for head in range(head_count):
            target = route(ctx, head)
            if target is not None:
                pairs.append((ctx * head_count + head, target[0] * head_count + target[1]))
    return lax.ppermute(value, ("ctx", "head"), pairs)


def is_paired():
    return lax.axis_size("ctx") == 4 and lax.axis_size("head") == 4


def key_sources():
    count = lax.axis_size("ctx")
    ctx = lax.axis_index("ctx")
    if is_paired():
        step = jnp.where(ctx < 2, 1, 3)
        return [ctx, (ctx + step) & 3, ctx ^ 2, (ctx - step) & 3]
    return [ctx] + [lax.rem(ctx + (count - step), count) for step in range(1, count)]


def part_order():
    if is_paired():
        head = lax.axis_index("head")
        return [head ^ 3, head ^ 1, head ^ 2, head]
    return list(range(PARTS))


def part_copy(w_out_ref, slot, target, sem):
    width = target.shape[1]
    start = pl.multiple_of(part_order()[slot] * width, 128)
    return pltpu.make_async_copy(w_out_ref.at[:, pl.ds(start, width)], target, sem)


def prepare_kernel(
    rows,
    order_hbm,
    lens_hbm,
    queries_ref,
    w_keys_ref,
    w_values_ref,
    w_out_ref,
    folded_ref,
    bias_ref,
    values_ref,
    part_ref,
    order_ref,
    lens_ref,
    query_buffer,
    key_buffer,
    sems,
):
    half = rows // 2
    scalars = [
        pltpu.make_async_copy(order_hbm, order_ref, sems.at[3]),
        pltpu.make_async_copy(lens_hbm, lens_ref, sems.at[4]),
    ]
    first = [
        pltpu.make_async_copy(queries_ref, query_buffer, sems.at[0]),
        pltpu.make_async_copy(w_keys_ref, key_buffer, sems.at[1]),
    ]
    later = [
        pltpu.make_async_copy(w_values_ref, values_ref, sems.at[2]),
        part_copy(w_out_ref, 0, part_ref, sems.at[5]),
    ]
    for copy in scalars + first + later:
        copy.start()

    for copy in scalars:
        copy.wait()
    ctx = lax.axis_index("ctx")
    row = lax.broadcasted_iota(jnp.int32, (rows, rows), 0)
    lane = lax.broadcasted_iota(jnp.int32, (rows, rows), 1)
    query_pos = jnp.where(row < half, order_ref[2 * ctx], order_ref[2 * ctx + 1]) * half + row % half
    offset = lane % half
    for step, source in enumerate(key_sources()):
        key_place = jnp.where(lane < half, order_ref[2 * source], order_ref[2 * source + 1])
        length = jnp.where(lane < half, lens_ref[2 * source], lens_ref[2 * source + 1])
        visible = (key_place * half + offset <= query_pos) & (offset < length)
        bias_ref[:, step * rows : (step + 1) * rows] = jnp.where(visible, 0.0, HIDDEN)

    for copy in first:
        copy.wait()
    for head in range(w_keys_ref.shape[1] // HEAD_DIM):
        nope = query_buffer[:, head * QUERY : head * QUERY + HEAD_DIM]
        rope = query_buffer[:, head * QUERY + HEAD_DIM : (head + 1) * QUERY]
        weight = key_buffer[:, head * HEAD_DIM : (head + 1) * HEAD_DIM]
        here = slice(head * rows, (head + 1) * rows)
        product = lax.dot_general(nope, weight, NT, preferred_element_type=jnp.float32)
        folded_ref[here, :LATENT] = product.astype(jnp.bfloat16)
        folded_ref[here, LATENT:] = rope
    for copy in later:
        copy.wait()


VMEM = pl.BlockSpec(memory_space=pltpu.VMEM)
HBM = pl.BlockSpec(memory_space=pltpu.HBM)


def in_hbm(value):
    return pltpu.with_memory_space_constraint(value, pltpu.HBM)


def prepare(*operands):
    order, lens, queries, w_keys, w_values, w_out = operands
    rows = queries.shape[0]
    count = lax.axis_size("ctx")
    heads = w_keys.shape[1] // HEAD_DIM
    return pl.pallas_call(
        functools.partial(prepare_kernel, rows),
        out_shape=[
            jax.ShapeDtypeStruct((heads * rows, LATENT + ROPE), jnp.bfloat16),
            jax.ShapeDtypeStruct((rows, count * rows), jnp.float32),
            jax.ShapeDtypeStruct(w_values.shape, jnp.bfloat16),
            jax.ShapeDtypeStruct((w_out.shape[0], w_out.shape[1] // PARTS), jnp.bfloat16),
        ],
        in_specs=[HBM] * 6,
        out_specs=[VMEM] * 4,
        scratch_shapes=[
            pltpu.SMEM(order.shape, jnp.int32),
            pltpu.SMEM(lens.shape, jnp.int32),
            pltpu.VMEM(queries.shape, jnp.bfloat16),
            pltpu.VMEM(w_keys.shape, jnp.bfloat16),
            pltpu.SemaphoreType.DMA((6,)),
        ],
        compiler_params=pltpu.CompilerParams(vmem_limit_bytes=VMEM_BYTES),
        cost_estimate=pl.CostEstimate(
            flops=2 * rows * heads * HEAD_DIM * LATENT,
            bytes_accessed=2 * (queries.size + w_keys.size + w_values.size + w_out.size // PARTS),
            transcendentals=0,
        ),
        name="prepare",
    )(*[in_hbm(item) for item in operands])


def on_long_side():
    return (lax.axis_index("ctx") < 2) == (lax.axis_index("head") & 1 == 1)


def at_an_end():
    ctx = lax.axis_index("ctx")
    return (ctx == 0) | (ctx == 3)


def place_if(keys_ref, slot, block_ref, condition):
    rows = block_ref.shape[1]

    @pl.when(condition)
    def _():
        keys_ref[:, slot * rows : (slot + 1) * rows] = block_ref[...]


EXPONENT = QUERY**-0.5 * 1.4426950408889634


def begin_kernel(paired, folded_ref, bias_ref, w_out_ref, *rest):
    blocks = rest[: 3 if paired else 1]
    peak_ref, total_ref, sums_ref, part_a, part_b, keys_ref, sems = rest[len(blocks) :]
    copies = [
        part_copy(w_out_ref, 1, part_a, sems.at[0]),
        part_copy(w_out_ref, 2, part_b, sems.at[1]),
    ]
    for copy in copies:
        copy.start()
    rows, keys = bias_ref.shape[0], keys_ref.shape[1]
    keys_ref[:, :rows] = blocks[0][...]
    if paired:
        long_side = on_long_side()
        place_if(keys_ref, 1, blocks[1], long_side)
        place_if(keys_ref, 1, blocks[2], jnp.logical_not(long_side))
    stacked = ROWS_AT_ONCE // rows
    bias = jnp.concatenate([bias_ref[:, :keys]] * stacked, axis=0)
    for group in range(folded_ref.shape[0] // ROWS_AT_ONCE):
        lines = slice(group * ROWS_AT_ONCE, (group + 1) * ROWS_AT_ONCE)
        scores = jnp.dot(folded_ref[lines, :], keys_ref[...], preferred_element_type=jnp.float32)
        scores = scores + bias
        peak = jnp.max(scores, axis=1, keepdims=True)
        weights = jnp.exp2((scores - peak) * jnp.float32(EXPONENT))
        total = jnp.sum(weights, axis=1, keepdims=True)
        peak_ref[lines, :] = jnp.broadcast_to(peak, (ROWS_AT_ONCE, 128))
        total_ref[lines, :] = jnp.broadcast_to(total, (ROWS_AT_ONCE, 128))
        sums_ref[lines, :] = lax.dot_general(
            weights.astype(jnp.bfloat16), keys_ref[:LATENT, :], NT, preferred_element_type=jnp.float32
        )
    for copy in copies:
        copy.wait()


def begin(folded, bias, w_out, blocks):
    lines = folded.shape[0]
    rows = bias.shape[0]
    keys = rows * (2 if is_paired() else 1)
    part = jax.ShapeDtypeStruct((w_out.shape[0], w_out.shape[1] // PARTS), jnp.bfloat16)
    return pl.pallas_call(
        functools.partial(begin_kernel, is_paired()),
        out_shape=[
            jax.ShapeDtypeStruct((lines, 128), jnp.float32),
            jax.ShapeDtypeStruct((lines, 128), jnp.float32),
            jax.ShapeDtypeStruct((lines, LATENT), jnp.float32),
            part,
            part,
        ],
        in_specs=[VMEM, VMEM, HBM] + [VMEM] * len(blocks),
        out_specs=[VMEM] * 5,
        scratch_shapes=[
            pltpu.VMEM((LATENT + ROPE, keys), jnp.bfloat16),
            pltpu.SemaphoreType.DMA((2,)),
        ],
        compiler_params=pltpu.CompilerParams(vmem_limit_bytes=VMEM_BYTES),
        cost_estimate=pl.CostEstimate(
            flops=2 * lines * keys * (2 * LATENT + ROPE),
            bytes_accessed=w_out.size,
            transcendentals=lines * keys,
        ),
        name="begin",
    )(folded, bias, in_hbm(w_out), *blocks)


def finish_kernel(paired, count, *refs):
    folded_ref, bias_ref, values_ref, peak_ref, total_ref, sums_ref = refs[:6]
    part_refs, w_out_ref, refs = refs[6:9], refs[9], refs[10:]
    blocks, refs = refs[:count], refs[count:]
    outs, (keys_ref, attended_ref, last_part, sem) = refs[:PARTS], refs[PARTS:]
    last_copy = part_copy(w_out_ref, 3, last_part, sem.at[0])
    last_copy.start()
    rows, keys = bias_ref.shape[0], keys_ref.shape[1]
    if paired:
        near, near_swapped, far, far_swapped, last, last_swapped = blocks
        long_side, end = on_long_side(), at_an_end()
        short_side, middle = jnp.logical_not(long_side), jnp.logical_not(end)
        place_if(keys_ref, 0, far, long_side)
        place_if(keys_ref, 0, far_swapped, short_side)
        place_if(keys_ref, 1, last, long_side & end)
        place_if(keys_ref, 1, last_swapped, short_side & end)
        place_if(keys_ref, 1, near_swapped, long_side & middle)
        place_if(keys_ref, 1, near, short_side & middle)
    else:
        for step in range(count):
            keys_ref[:, step * rows : (step + 1) * rows] = blocks[step][...]
    stacked = ROWS_AT_ONCE // rows
    bias = jnp.concatenate([bias_ref[:, bias_ref.shape[1] - keys :]] * stacked, axis=0)
    for group in range(folded_ref.shape[0] // ROWS_AT_ONCE):
        lines = slice(group * ROWS_AT_ONCE, (group + 1) * ROWS_AT_ONCE)
        scores = jnp.dot(folded_ref[lines, :], keys_ref[...], preferred_element_type=jnp.float32)
        scores = scores + bias
        old_peak = peak_ref[lines, :1]
        peak = jnp.maximum(old_peak, jnp.max(scores, axis=1, keepdims=True))
        factor = jnp.exp2((old_peak - peak) * jnp.float32(EXPONENT))
        weights = jnp.exp2((scores - peak) * jnp.float32(EXPONENT))
        total = total_ref[lines, :1] * factor + jnp.sum(weights, axis=1, keepdims=True)
        mixed = lax.dot_general(
            weights.astype(jnp.bfloat16), keys_ref[:LATENT, :], NT, preferred_element_type=jnp.float32
        )
        mixed = ((sums_ref[lines, :] * factor + mixed) / total).astype(jnp.bfloat16)
        for inner in range(stacked):
            head = group * stacked + inner
            columns = slice(head * HEAD_DIM, (head + 1) * HEAD_DIM)
            value = jnp.dot(
                mixed[inner * rows : (inner + 1) * rows, :],
                values_ref[:, columns],
                preferred_element_type=jnp.float32,
            )
            attended_ref[:, columns] = value.astype(jnp.bfloat16)

    for slot in range(PARTS):
        if slot == PARTS - 1:
            last_copy.wait()
            weight = last_part[...]
        else:
            weight = part_refs[slot][...]
        outs[slot][...] = jnp.dot(
            attended_ref[...], weight, preferred_element_type=jnp.float32
        ).astype(outs[slot].dtype)


def finish(folded, bias, values, state, parts, w_out, blocks, out_types):
    lines = folded.shape[0]
    rows = bias.shape[0]
    width = w_out.shape[1] // PARTS
    keys = bias.shape[1] - rows * (2 if is_paired() else 1)
    flops = 2 * lines * (keys * (2 * LATENT + ROPE) + LATENT * HEAD_DIM)
    flops += 2 * rows * w_out.size
    return pl.pallas_call(
        functools.partial(finish_kernel, is_paired(), len(blocks)),
        out_shape=[jax.ShapeDtypeStruct((rows, width), kind) for kind in out_types],
        in_specs=[VMEM] * 9 + [HBM] + [VMEM] * len(blocks),
        out_specs=[VMEM] * PARTS,
        scratch_shapes=[
            pltpu.VMEM((LATENT + ROPE, keys), jnp.bfloat16),
            pltpu.VMEM((rows, w_out.shape[0]), jnp.bfloat16),
            pltpu.VMEM((w_out.shape[0], width), jnp.bfloat16),
            pltpu.SemaphoreType.DMA((1,)),
        ],
        compiler_params=pltpu.CompilerParams(vmem_limit_bytes=VMEM_BYTES),
        cost_estimate=pl.CostEstimate(
            flops=flops, bytes_accessed=w_out.size // 2, transcendentals=lines * keys
        ),
        name="finish",
    )(folded, bias, values, *state, *parts, in_hbm(w_out), *blocks)


def along_ring(ctx, head):
    if head & 1 == 0:
        return (ctx + 1, head) if ctx < 3 else (ctx, head ^ 1)
    return (ctx - 1, head) if ctx > 0 else (ctx, head ^ 1)


def other_core(ctx, head):
    return ctx, head ^ 1


def other_chip(ctx, head):
    return ctx, head ^ 2


def shards(queries, latent, w_keys, w_values, w_out, block_order, valid_lengths):
    ctx_count = lax.axis_size("ctx")
    block = latent.T
    prepared = prepare(block_order, valid_lengths, queries, w_keys, w_values, w_out)

    if not is_paired():
        blocks = []
        for step in range(1, ctx_count):
            blocks.append(routed(block, lambda ctx, head: ((ctx + step) % ctx_count, head)))
        folded, bias, values, part_0 = prepared
        *state, part_1, part_2 = begin(folded, bias, w_out, [block])
        parts = [part_0, part_1, part_2]
        kinds = [jnp.bfloat16] * PARTS
        shares = finish(folded, bias, values, state, parts, w_out, blocks, kinds)
        whole = jnp.concatenate(shares, axis=1)
        return lax.psum_scatter(whole, "head", scatter_dimension=1, tiled=True)

    near = routed(block, along_ring)
    near, prepared = lax.optimization_barrier((near, prepared))
    folded, bias, values, part_0 = prepared
    far = routed(near, along_ring)
    near_swapped = routed(near, other_core)
    begun = begin(folded, bias, w_out, [block, near, near_swapped])
    far, begun = lax.optimization_barrier((far, begun))
    *state, part_1, part_2 = begun
    last = routed(far, along_ring)
    far_swapped = routed(far, other_core)
    last_swapped = routed(last, other_core)
    across, beside, far_part, own = finish(
        folded,
        bias,
        values,
        state,
        [part_0, part_1, part_2],
        w_out,
        [near, near_swapped, far, far_swapped, last, last_swapped],
        [jnp.bfloat16, jnp.bfloat16, jnp.float32, jnp.float32],
    )
    far_part = (far_part + routed(across, other_core).astype(jnp.float32)).astype(jnp.bfloat16)
    far_part, beside = lax.optimization_barrier((far_part, beside))
    far_part = routed(far_part, other_chip).astype(jnp.float32)
    beside = routed(beside, other_core).astype(jnp.float32)
    return (own + beside + far_part).astype(jnp.bfloat16)


def solution(mesh):
    in_specs = (
        P(("groups", "ctx"), "head"),
        P(("groups", "ctx"), None),
        P(None, "head"),
        P(None, "head"),
        P("head", None),
        P("groups"),
        P("groups"),
    )
    out_specs = P(("groups", "ctx"), "head")
    return jax.shard_map(shards, mesh=mesh, in_specs=in_specs, out_specs=out_specs, check_vma=False)
```

```python
import functools

import jax
import jax.numpy as jnp
from jax import lax
from jax.experimental import pallas as pl
from jax.experimental.pallas import tpu as pltpu
from jax.sharding import PartitionSpec as P

LATENT = 512
ROPE = 64
HEAD_DIM = 128
QUERY = HEAD_DIM + ROPE
PARTS = 4
ROWS_AT_ONCE = 256
NT = (((1,), (1,)), ((), ()))
VMEM_BYTES = 32 * 1024 * 1024
HIDDEN = -1e30


def routed(value, route):
    ctx_count = lax.axis_size("ctx")
    head_count = lax.axis_size("head")
    pairs = []
    for ctx in range(ctx_count):
        for head in range(head_count):
            target = route(ctx, head)
            if target is not None:
                pairs.append((ctx * head_count + head, target[0] * head_count + target[1]))
    return lax.ppermute(value, ("ctx", "head"), pairs)


def is_paired():
    return lax.axis_size("ctx") == 4 and lax.axis_size("head") == 4


def key_sources():
    count = lax.axis_size("ctx")
    ctx = lax.axis_index("ctx")
    if is_paired():
        step = 1 + 2 * (lax.axis_index("head") & 1)
        return [ctx, (ctx - step) & 3, (ctx + step) & 3, ctx ^ 2]
    return [ctx] + [lax.rem(ctx + (count - step), count) for step in range(1, count)]


def part_order():
    if is_paired():
        head = lax.axis_index("head")
        return [head ^ 3, head ^ 2, head ^ 1, head]
    return list(range(PARTS))


VMEM = pl.BlockSpec(memory_space=pltpu.VMEM)
HBM = pl.BlockSpec(memory_space=pltpu.HBM)
PARAMS = pltpu.CompilerParams(vmem_limit_bytes=VMEM_BYTES)
EXPONENT = QUERY**-0.5 * 1.4426950408889634


def prepare_kernel(half, *refs):
    order_hbm, lens_hbm, queries_ref, w_keys_ref, w_values_ref, w_out_ref = refs[:6]
    folded_ref, bias_ref, values_ref = refs[6:9]
    part_refs = refs[9 : 9 + PARTS]
    order_ref, lens_ref, query_buffer, key_buffer, sems = refs[9 + PARTS :]
    width = w_out_ref.shape[1] // PARTS
    heads = w_keys_ref.shape[1] // HEAD_DIM
    rows = 2 * half
    scalars = [
        pltpu.make_async_copy(order_hbm, order_ref, sems.at[0]),
        pltpu.make_async_copy(lens_hbm, lens_ref, sems.at[1]),
    ]
    first = [
        pltpu.make_async_copy(queries_ref, query_buffer, sems.at[2]),
        pltpu.make_async_copy(w_keys_ref, key_buffer, sems.at[3]),
    ]
    later = [pltpu.make_async_copy(w_values_ref, values_ref, sems.at[4])]
    for slot, part in enumerate(part_order()):
        start = pl.multiple_of(part * width, 128)
        source = w_out_ref.at[:, pl.ds(start, width)]
        later.append(pltpu.make_async_copy(source, part_refs[slot], sems.at[5 + slot]))
    for copy in scalars + first + later:
        copy.start()

    for copy in scalars:
        copy.wait()
    ctx = lax.axis_index("ctx")
    row = lax.broadcasted_iota(jnp.int32, (rows, rows), 0)
    lane = lax.broadcasted_iota(jnp.int32, (rows, rows), 1)
    query_pos = jnp.where(row < half, order_ref[2 * ctx], order_ref[2 * ctx + 1]) * half + row % half
    offset = lane % half
    for step, source in enumerate(key_sources()):
        key_place = jnp.where(lane < half, order_ref[2 * source], order_ref[2 * source + 1])
        length = jnp.where(lane < half, lens_ref[2 * source], lens_ref[2 * source + 1])
        visible = (key_place * half + offset <= query_pos) & (offset < length)
        bias_ref[:, step * rows : (step + 1) * rows] = jnp.where(visible, 0.0, HIDDEN)

    for copy in first:
        copy.wait()
    for head in range(heads):
        nope = query_buffer[:, head * QUERY : head * QUERY + HEAD_DIM]
        rope = query_buffer[:, head * QUERY + HEAD_DIM : (head + 1) * QUERY]
        weight = key_buffer[:, head * HEAD_DIM : (head + 1) * HEAD_DIM]
        product = lax.dot_general(nope, weight, NT, preferred_element_type=jnp.float32)
        product = product.astype(jnp.bfloat16)
        for side in range(2):
            target = slice((side * heads + head) * half, (side * heads + head + 1) * half)
            origin = slice(side * half, (side + 1) * half)
            folded_ref[target, :LATENT] = product[origin, :]
            folded_ref[target, LATENT:] = rope[origin, :]
    for copy in later:
        copy.wait()


def prepare(*operands):
    order, lens, queries, w_keys, w_values, w_out = operands
    rows = queries.shape[0]
    count = lax.axis_size("ctx")
    heads = w_keys.shape[1] // HEAD_DIM
    part = jax.ShapeDtypeStruct((w_out.shape[0], w_out.shape[1] // PARTS), jnp.bfloat16)
    return pl.pallas_call(
        functools.partial(prepare_kernel, rows // 2),
        out_shape=[
            jax.ShapeDtypeStruct((heads * rows, LATENT + ROPE), jnp.bfloat16),
            jax.ShapeDtypeStruct((rows, count * rows), jnp.float32),
            jax.ShapeDtypeStruct(w_values.shape, jnp.bfloat16),
        ]
        + [part] * PARTS,
        in_specs=[HBM] * 6,
        out_specs=[VMEM] * (3 + PARTS),
        scratch_shapes=[
            pltpu.SMEM(order.shape, jnp.int32),
            pltpu.SMEM(lens.shape, jnp.int32),
            pltpu.VMEM(queries.shape, jnp.bfloat16),
            pltpu.VMEM(w_keys.shape, jnp.bfloat16),
            pltpu.SemaphoreType.DMA((5 + PARTS,)),
        ],
        compiler_params=PARAMS,
        cost_estimate=pl.CostEstimate(
            flops=2 * rows * heads * HEAD_DIM * LATENT,
            bytes_accessed=2 * (queries.size + w_keys.size + w_values.size + w_out.size),
            transcendentals=0,
        ),
        name="prepare",
    )(*[pltpu.with_memory_space_constraint(item, pltpu.HBM) for item in operands])


def attend_rows(side, folded_ref, bias_ref, values_ref, keys_ref, attended_ref):
    half = bias_ref.shape[0] // 2
    heads = values_ref.shape[1] // HEAD_DIM
    stacked = ROWS_AT_ONCE // half
    bias = jnp.concatenate([bias_ref[side * half : (side + 1) * half, :]] * stacked, axis=0)
    for group in range(heads // stacked):
        start = side * heads * half + group * ROWS_AT_ONCE
        scores = jnp.dot(
            folded_ref[start : start + ROWS_AT_ONCE, :],
            keys_ref[...],
            preferred_element_type=jnp.float32,
        )
        scores = scores + bias
        peak = jnp.max(scores, axis=1, keepdims=True)
        weights = jnp.exp2((scores - peak) * jnp.float32(EXPONENT))
        total = jnp.sum(weights, axis=1, keepdims=True)
        mixed = lax.dot_general(
            weights.astype(jnp.bfloat16), keys_ref[:LATENT, :], NT, preferred_element_type=jnp.float32
        )
        mixed = (mixed / total).astype(jnp.bfloat16)
        for inner in range(stacked):
            head = group * stacked + inner
            columns = slice(head * HEAD_DIM, (head + 1) * HEAD_DIM)
            value = jnp.dot(
                mixed[inner * half : (inner + 1) * half, :],
                values_ref[:, columns],
                preferred_element_type=jnp.float32,
            )
            attended_ref[:, columns] = value.astype(jnp.bfloat16)


def project(attended_ref, part_ref, share_ref):
    share = jnp.dot(attended_ref[...], part_ref[...], preferred_element_type=jnp.float32)
    share_ref[...] = share.astype(share_ref.dtype)


def place_if(keys_ref, slot, block_ref, condition):
    rows = block_ref.shape[1]

    @pl.when(condition)
    def _():
        keys_ref[:, slot * rows : (slot + 1) * rows] = block_ref[...]


def first_half_kernel(count, paired, folded_ref, bias_ref, values_ref, part_ref, *rest):
    blocks, (keys_ref, attended_ref, share_ref) = rest[:count], rest[count:]
    rows = blocks[0].shape[1]
    certain = count - 2 if paired else count
    for slot in range(certain):
        keys_ref[:, slot * rows : (slot + 1) * rows] = blocks[slot][...]
    if paired:
        direct = (lax.axis_index("ctx") ^ lax.axis_index("head")) & 1 == 0
        place_if(keys_ref, certain, blocks[certain], direct)
        place_if(keys_ref, certain, blocks[certain + 1], jnp.logical_not(direct))
    attend_rows(0, folded_ref, bias_ref, values_ref, keys_ref, attended_ref)
    project(attended_ref, part_ref, share_ref)


def second_half_kernel(folded_ref, bias_ref, values_ref, part_ref, keys_ref, attended_ref, share_ref):
    attend_rows(1, folded_ref, bias_ref, values_ref, keys_ref, attended_ref)
    project(attended_ref, part_ref, share_ref)


def attend_half(folded, bias, values, part, blocks, kind, keys=None):
    rows, key_count = bias.shape
    half = rows // 2
    heads = values.shape[1] // HEAD_DIM
    flops = 2 * heads * half * (key_count * (2 * LATENT + ROPE) + LATENT * HEAD_DIM)
    outs = [
        jax.ShapeDtypeStruct((half, values.shape[1]), jnp.bfloat16),
        jax.ShapeDtypeStruct((half, part.shape[1]), kind),
    ]
    if keys is None:
        kernel = functools.partial(first_half_kernel, len(blocks), is_paired())
        outs = [jax.ShapeDtypeStruct((LATENT + ROPE, key_count), jnp.bfloat16)] + outs
        extra = blocks
    else:
        kernel = second_half_kernel
        extra = [keys]
    return pl.pallas_call(
        kernel,
        out_shape=outs,
        in_specs=[VMEM] * (4 + len(extra)),
        out_specs=[VMEM] * len(outs),
        compiler_params=PARAMS,
        cost_estimate=pl.CostEstimate(
            flops=flops + 2 * half * part.size,
            bytes_accessed=folded.size + 2 * (values.size + part.size),
            transcendentals=heads * half * key_count,
        ),
        name="first_half" if keys is None else "second_half",
    )(folded, bias, values, part, *extra)


def project_kernel(attended_ref, *refs):
    count = len(refs) // 2
    for part_ref, share_ref in zip(refs[:count], refs[count:]):
        project(attended_ref, part_ref, share_ref)


def project_parts(attended, parts, kinds):
    half = attended.shape[0]
    shares = [
        jax.ShapeDtypeStruct((half, part.shape[1]), kind) for part, kind in zip(parts, kinds)
    ]
    size = sum(part.size for part in parts)
    return pl.pallas_call(
        project_kernel,
        out_shape=shares,
        in_specs=[VMEM] * (1 + len(parts)),
        out_specs=[VMEM] * len(parts),
        compiler_params=PARAMS,
        cost_estimate=pl.CostEstimate(
            flops=2 * half * size, bytes_accessed=2 * size, transcendentals=0
        ),
        name="project_parts",
    )(attended, *parts)


def next_to(ctx, head):
    return (ctx + 1 + 2 * (head & 1)) & 3, head


def two_away(ctx, head):
    return (ctx ^ 2 if (ctx ^ head) & 1 == 0 else ctx), head


def other_core(ctx, head):
    return ctx, head ^ 1


def other_chip(ctx, head):
    return ctx, head ^ 2


def shards(queries, latent, w_keys, w_values, w_out, block_order, valid_lengths):
    ctx_count = lax.axis_size("ctx")
    block = latent.T
    prepared = prepare(block_order, valid_lengths, queries, w_keys, w_values, w_out)
    narrow, wide = jnp.bfloat16, jnp.float32

    if not is_paired():
        blocks = [block]
        for step in range(1, ctx_count):
            blocks.append(routed(block, lambda ctx, head: ((ctx + step) % ctx_count, head)))
        folded, bias, values, *parts = prepared
        keys, first, share = attend_half(folded, bias, values, parts[0], blocks, narrow)
        shares = [share] + list(project_parts(first, parts[1:], [narrow] * 3))
        upper = jnp.concatenate(shares, axis=1)
        second, share = attend_half(folded, bias, values, parts[0], None, narrow, keys)
        shares = [share] + list(project_parts(second, parts[1:], [narrow] * 3))
        lower = jnp.concatenate(shares, axis=1)
        whole = jnp.concatenate([upper, lower], axis=0)
        return lax.psum_scatter(whole, "head", scatter_dimension=1, tiled=True)

    near = routed(block, next_to)
    far = routed(block, two_away)
    near, prepared = lax.optimization_barrier((near, prepared))
    near_swapped = routed(near, other_core)
    far, _ = lax.optimization_barrier((far, near))
    far_swapped = routed(far, other_core)
    folded, bias, values, *parts = prepared

    def send_on(attended, across):
        received = routed(across, other_core)
        far_part, beside, own = project_parts(attended, parts[1:], [wide, narrow, wide])
        far_part = (far_part + received.astype(wide)).astype(narrow)
        far_part, beside = lax.optimization_barrier((far_part, beside))
        return far_part, beside, own

    blocks = [block, near, near_swapped, far, far_swapped]
    keys, attended, across = attend_half(folded, bias, values, parts[0], blocks, narrow)
    far_part, beside, own = send_on(attended, across)
    keys, far_part = lax.optimization_barrier((keys, far_part))
    upper = (routed(far_part, other_chip), routed(beside, other_core), own)
    attended, across = attend_half(folded, bias, values, parts[0], None, narrow, keys)
    far_part, beside, own = send_on(attended, across)
    lower = (routed(far_part, other_chip), routed(beside, other_core), own)
    halves = [
        (own + beside.astype(wide) + far_part.astype(wide)).astype(narrow)
        for far_part, beside, own in (upper, lower)
    ]
    return jnp.concatenate(halves, axis=0)


def solution(mesh):
    in_specs = (
        P(("groups", "ctx"), "head"),
        P(("groups", "ctx"), None),
        P(None, "head"),
        P(None, "head"),
        P("head", None),
        P("groups"),
        P("groups"),
    )
    out_specs = P(("groups", "ctx"), "head")
    return jax.shard_map(shards, mesh=mesh, in_specs=in_specs, out_specs=out_specs, check_vma=False)
```

```python
import functools

import jax
import jax.numpy as jnp
from jax import lax
from jax.experimental import pallas as pl
from jax.experimental.pallas import tpu as pltpu
from jax.sharding import PartitionSpec as P

LATENT = 512
ROPE = 64
HEAD_DIM = 128
QUERY = HEAD_DIM + ROPE
PARTS = 4
ROWS_AT_ONCE = 256
NT = (((1,), (1,)), ((), ()))
VMEM_BYTES = 32 * 1024 * 1024
HIDDEN = -1e30


def routed(value, route):
    ctx_count = lax.axis_size("ctx")
    head_count = lax.axis_size("head")
    pairs = []
    for ctx in range(ctx_count):
        for head in range(head_count):
            target = route(ctx, head)
            if target is not None:
                pairs.append((ctx * head_count + head, target[0] * head_count + target[1]))
    return lax.ppermute(value, ("ctx", "head"), pairs)


def is_paired():
    return lax.axis_size("ctx") == 4 and lax.axis_size("head") == 4


def key_sources():
    count = lax.axis_size("ctx")
    ctx = lax.axis_index("ctx")
    if is_paired():
        step = 1 + 2 * (lax.axis_index("head") & 1)
        return [ctx, (ctx - step) & 3, (ctx + step) & 3, ctx ^ 2]
    return [ctx] + [lax.rem(ctx + (count - step), count) for step in range(1, count)]


def part_order():
    if is_paired():
        head = lax.axis_index("head")
        return [head ^ 3, head ^ 2, head ^ 1, head]
    return list(range(PARTS))


VMEM = pl.BlockSpec(memory_space=pltpu.VMEM)
HBM = pl.BlockSpec(memory_space=pltpu.HBM)
FIRST_PIECE = 512
PARAMS = pltpu.CompilerParams(vmem_limit_bytes=VMEM_BYTES)
SHORT = pl.CostEstimate(flops=1024, bytes_accessed=1024, transcendentals=0)
EXPONENT = QUERY**-0.5 * 1.4426950408889634


def prepare_kernel(half, *refs):
    order_hbm, lens_hbm, queries_ref, w_keys_ref, w_values_ref, w_out_ref = refs[:6]
    folded_ref, bias_ref, values_ref = refs[6:9]
    part_refs = refs[9 : 9 + PARTS]
    order_ref, lens_ref, query_buffer, key_buffer, sems = refs[9 + PARTS :]
    width = w_out_ref.shape[1] // PARTS
    heads = w_keys_ref.shape[1] // HEAD_DIM
    rows = 2 * half
    scalars = [
        pltpu.make_async_copy(order_hbm, order_ref, sems.at[0]),
        pltpu.make_async_copy(lens_hbm, lens_ref, sems.at[1]),
    ]
    first = [
        pltpu.make_async_copy(queries_ref, query_buffer, sems.at[2]),
        pltpu.make_async_copy(w_keys_ref, key_buffer, sems.at[3]),
    ]
    later = [pltpu.make_async_copy(w_values_ref, values_ref, sems.at[4])]
    for slot, part in enumerate(part_order()):
        start = pl.multiple_of(part * width, 128)
        source = w_out_ref.at[:, pl.ds(start, width)]
        later.append(pltpu.make_async_copy(source, part_refs[slot], sems.at[5 + slot]))
    for copy in scalars + first + later:
        copy.start()

    for copy in scalars:
        copy.wait()
    ctx = lax.axis_index("ctx")
    row = lax.broadcasted_iota(jnp.int32, (rows, rows), 0)
    lane = lax.broadcasted_iota(jnp.int32, (rows, rows), 1)
    query_pos = jnp.where(row < half, order_ref[2 * ctx], order_ref[2 * ctx + 1]) * half + row % half
    offset = lane % half
    for step, source in enumerate(key_sources()):
        key_place = jnp.where(lane < half, order_ref[2 * source], order_ref[2 * source + 1])
        length = jnp.where(lane < half, lens_ref[2 * source], lens_ref[2 * source + 1])
        visible = (key_place * half + offset <= query_pos) & (offset < length)
        bias_ref[:, step * rows : (step + 1) * rows] = jnp.where(visible, 0.0, HIDDEN)

    for copy in first:
        copy.wait()
    for head in range(heads):
        nope = query_buffer[:, head * QUERY : head * QUERY + HEAD_DIM]
        rope = query_buffer[:, head * QUERY + HEAD_DIM : (head + 1) * QUERY]
        weight = key_buffer[:, head * HEAD_DIM : (head + 1) * HEAD_DIM]
        product = lax.dot_general(nope, weight, NT, preferred_element_type=jnp.float32)
        here = slice(head * rows, (head + 1) * rows)
        folded_ref[here, :LATENT] = product.astype(jnp.bfloat16)
        folded_ref[here, LATENT:] = rope
    for copy in later:
        copy.wait()


def prepare(*operands):
    order, lens, queries, w_keys, w_values, w_out = operands
    rows = queries.shape[0]
    count = lax.axis_size("ctx")
    heads = w_keys.shape[1] // HEAD_DIM
    part = jax.ShapeDtypeStruct((w_out.shape[0], w_out.shape[1] // PARTS), jnp.bfloat16)
    return pl.pallas_call(
        functools.partial(prepare_kernel, rows // 2),
        out_shape=[
            jax.ShapeDtypeStruct((heads * rows, LATENT + ROPE), jnp.bfloat16),
            jax.ShapeDtypeStruct((rows, count * rows), jnp.float32),
            jax.ShapeDtypeStruct(w_values.shape, jnp.bfloat16),
        ]
        + [part] * PARTS,
        in_specs=[HBM] * 6,
        out_specs=[VMEM] * (3 + PARTS),
        scratch_shapes=[
            pltpu.SMEM(order.shape, jnp.int32),
            pltpu.SMEM(lens.shape, jnp.int32),
            pltpu.VMEM(queries.shape, jnp.bfloat16),
            pltpu.VMEM(w_keys.shape, jnp.bfloat16),
            pltpu.SemaphoreType.DMA((5 + PARTS,)),
        ],
        compiler_params=PARAMS,
        cost_estimate=pl.CostEstimate(
            flops=2 * rows * heads * HEAD_DIM * LATENT,
            bytes_accessed=2 * (queries.size + w_keys.size + w_values.size + w_out.size),
            transcendentals=0,
        ),
        name="prepare",
    )(*[pltpu.with_memory_space_constraint(item, pltpu.HBM) for item in operands])


def place_if(keys_ref, slot, block_ref, condition):
    rows = block_ref.shape[1]

    @pl.when(condition)
    def _():
        keys_ref[:, slot * rows : (slot + 1) * rows] = block_ref[...]


def project(attended_ref, part_ref, share_refs):
    start = 0
    for share_ref in share_refs:
        stop = start + share_ref.shape[1]
        share = jnp.dot(
            attended_ref[...], part_ref[:, start:stop], preferred_element_type=jnp.float32
        )
        share_ref[...] = share.astype(share_ref.dtype)
        start = stop


def attend_kernel(count, paired, folded_ref, bias_ref, values_ref, part_ref, *rest):
    blocks, (attended_ref, *shares, keys_ref) = rest[:count], rest[count:]
    rows = bias_ref.shape[0]
    heads = values_ref.shape[1] // HEAD_DIM
    certain = count - 2 if paired else count
    for slot in range(certain):
        keys_ref[:, slot * rows : (slot + 1) * rows] = blocks[slot][...]
    if paired:
        direct = (lax.axis_index("ctx") ^ lax.axis_index("head")) & 1 == 0
        place_if(keys_ref, certain, blocks[certain], direct)
        place_if(keys_ref, certain, blocks[certain + 1], jnp.logical_not(direct))
    stacked = ROWS_AT_ONCE // rows
    bias = jnp.concatenate([bias_ref[...]] * stacked, axis=0)
    for group in range(heads // stacked):
        lines = slice(group * ROWS_AT_ONCE, (group + 1) * ROWS_AT_ONCE)
        scores = jnp.dot(folded_ref[lines, :], keys_ref[...], preferred_element_type=jnp.float32)
        scores = scores + bias
        peak = jnp.max(scores, axis=1, keepdims=True)
        weights = jnp.exp2((scores - peak) * jnp.float32(EXPONENT))
        inverse = 1.0 / jnp.sum(weights, axis=1, keepdims=True)
        mixed = lax.dot_general(
            weights.astype(jnp.bfloat16), keys_ref[:LATENT, :], NT, preferred_element_type=jnp.float32
        ).astype(jnp.bfloat16)
        for inner in range(stacked):
            head = group * stacked + inner
            columns = slice(head * HEAD_DIM, (head + 1) * HEAD_DIM)
            lines = slice(inner * rows, (inner + 1) * rows)
            value = jnp.dot(
                mixed[lines, :], values_ref[:, columns], preferred_element_type=jnp.float32
            )
            attended_ref[:, columns] = (value * inverse[lines, :]).astype(jnp.bfloat16)
    project(attended_ref, part_ref, shares)


def share_shapes(rows, widths, kind):
    return [jax.ShapeDtypeStruct((rows, width), kind) for width in widths]


def attend(folded, bias, values, part, blocks, widths):
    rows, keys = bias.shape
    heads = values.shape[1] // HEAD_DIM
    flops = 2 * heads * rows * (keys * (2 * LATENT + ROPE) + LATENT * HEAD_DIM)
    return pl.pallas_call(
        functools.partial(attend_kernel, len(blocks), is_paired()),
        out_shape=share_shapes(rows, [values.shape[1]] + widths, jnp.bfloat16),
        in_specs=[VMEM] * (4 + len(blocks)),
        out_specs=[VMEM] * (1 + len(widths)),
        scratch_shapes=[pltpu.VMEM((LATENT + ROPE, keys), jnp.bfloat16)],
        compiler_params=PARAMS,
        cost_estimate=pl.CostEstimate(
            flops=flops + 2 * rows * part.size,
            bytes_accessed=2 * (folded.size + values.size + part.size),
            transcendentals=heads * rows * keys,
        ),
        name="attend",
    )(folded, bias, values, part, *blocks)


def project_kernel(pieces, attended_ref, *refs):
    parts, shares = refs[: len(pieces)], list(refs[len(pieces) :])
    for part_ref, count in zip(parts, pieces):
        project(attended_ref, part_ref, shares[:count])
        shares = shares[count:]


def project_parts(attended, parts, outs):
    flat = [out for group in outs for out in group]
    return pl.pallas_call(
        functools.partial(project_kernel, [len(group) for group in outs]),
        out_shape=flat,
        in_specs=[VMEM] * (1 + len(parts)),
        out_specs=[VMEM] * len(flat),
        compiler_params=PARAMS,
        cost_estimate=SHORT,
        name="project_parts",
    )(attended, *parts)


def next_to(ctx, head):
    return (ctx + 1 + 2 * (head & 1)) & 3, head


def two_away(ctx, head):
    return (ctx ^ 2 if (ctx ^ head) & 1 == 0 else ctx), head


def other_core(ctx, head):
    return ctx, head ^ 1


def other_chip(ctx, head):
    return ctx, head ^ 2


def shards(queries, latent, w_keys, w_values, w_out, block_order, valid_lengths):
    ctx_count = lax.axis_size("ctx")
    rows = queries.shape[0]
    width = w_out.shape[1] // PARTS
    block = latent.T
    prepared = prepare(block_order, valid_lengths, queries, w_keys, w_values, w_out)
    narrow, wide = jnp.bfloat16, jnp.float32

    if not is_paired():
        blocks = [block]
        for step in range(1, ctx_count):
            blocks.append(routed(block, lambda ctx, head: ((ctx + step) % ctx_count, head)))
        folded, bias, values, *parts = prepared
        attended, share = attend(folded, bias, values, parts[0], blocks, [width])
        outs = [share_shapes(rows, [width], narrow)] * (PARTS - 1)
        shares = [share] + list(project_parts(attended, parts[1:], outs))
        whole = jnp.concatenate(shares, axis=1)
        return lax.psum_scatter(whole, "head", scatter_dimension=1, tiled=True)

    widths = [FIRST_PIECE, width - FIRST_PIECE]
    near = routed(block, next_to)
    far = routed(block, two_away)
    near, prepared = lax.optimization_barrier((near, prepared))
    near_swapped = routed(near, other_core)
    far, near_swapped = lax.optimization_barrier((far, near_swapped))
    far_swapped = routed(far, other_core)
    folded, bias, values, *parts = prepared
    blocks = [block, near, near_swapped, far, far_swapped]

    attended, *across = attend(folded, bias, values, parts[0], blocks, widths)
    received = [routed(piece, other_core) for piece in across]
    sums = project_parts(attended, parts[1:2], [share_shapes(rows, widths, wide)])
    sums = [(mine + other.astype(wide)).astype(narrow) for mine, other in zip(sums, received)]
    first = routed(sums[0], other_chip)
    attended, sums[1] = lax.optimization_barrier((attended, sums[1]))
    second = routed(sums[1], other_chip)
    outs = [share_shapes(rows, [width], narrow), share_shapes(rows, [width], wide)]
    beside, own = project_parts(attended, parts[2:], outs)
    beside, first = lax.optimization_barrier((beside, first))
    beside = routed(beside, other_core)
    other = jnp.concatenate([first, second], axis=1)
    return (own + beside.astype(wide) + other.astype(wide)).astype(narrow)


def solution(mesh):
    in_specs = (
        P(("groups", "ctx"), "head"),
        P(("groups", "ctx"), None),
        P(None, "head"),
        P(None, "head"),
        P("head", None),
        P("groups"),
        P("groups"),
    )
    out_specs = P(("groups", "ctx"), "head")
    return jax.shard_map(shards, mesh=mesh, in_specs=in_specs, out_specs=out_specs, check_vma=False)
```

```python
import functools

import jax
import jax.numpy as jnp
from jax import lax
from jax.experimental import pallas as pl
from jax.experimental.pallas import tpu as pltpu
from jax.sharding import PartitionSpec as P

LATENT = 512
ROPE = 64
HEAD_DIM = 128
QUERY = HEAD_DIM + ROPE
PARTS = 4
ROWS_AT_ONCE = 256
NT = (((1,), (1,)), ((), ()))
VMEM_BYTES = 32 * 1024 * 1024
HIDDEN = -1e30


def routed(value, route):
    ctx_count = lax.axis_size("ctx")
    head_count = lax.axis_size("head")
    pairs = []
    for ctx in range(ctx_count):
        for head in range(head_count):
            target = route(ctx, head)
            if target is not None:
                pairs.append((ctx * head_count + head, target[0] * head_count + target[1]))
    return lax.ppermute(value, ("ctx", "head"), pairs)


def is_paired():
    return lax.axis_size("ctx") == 4 and lax.axis_size("head") == 4


def key_sources():
    count = lax.axis_size("ctx")
    ctx = lax.axis_index("ctx")
    if is_paired():
        step = 1 + 2 * (lax.axis_index("head") & 1)
        return [ctx, (ctx - step) & 3, (ctx + step) & 3, ctx ^ 2]
    return [ctx] + [lax.rem(ctx + (count - step), count) for step in range(1, count)]


def part_order():
    if is_paired():
        head = lax.axis_index("head")
        return [head ^ 3, head ^ 2, head ^ 1, head]
    return list(range(PARTS))


VMEM = pl.BlockSpec(memory_space=pltpu.VMEM)
HBM = pl.BlockSpec(memory_space=pltpu.HBM)
PARAMS = pltpu.CompilerParams(vmem_limit_bytes=VMEM_BYTES)
SHORT = pl.CostEstimate(flops=1024, bytes_accessed=1024, transcendentals=0)
EXPONENT = QUERY**-0.5 * 1.4426950408889634


def prepare_kernel(half, *refs):
    order_hbm, lens_hbm, queries_ref, w_keys_ref, w_values_ref, w_out_ref = refs[:6]
    folded_ref, bias_ref, values_ref = refs[6:9]
    part_refs = refs[9 : 9 + PARTS]
    order_ref, lens_ref, query_buffer, key_buffer, sems = refs[9 + PARTS :]
    width = w_out_ref.shape[1] // PARTS
    heads = w_keys_ref.shape[1] // HEAD_DIM
    rows = 2 * half
    scalars = [
        pltpu.make_async_copy(order_hbm, order_ref, sems.at[0]),
        pltpu.make_async_copy(lens_hbm, lens_ref, sems.at[1]),
    ]
    first = [
        pltpu.make_async_copy(queries_ref, query_buffer, sems.at[2]),
        pltpu.make_async_copy(w_keys_ref, key_buffer, sems.at[3]),
    ]
    later = [pltpu.make_async_copy(w_values_ref, values_ref, sems.at[4])]
    for slot, part in enumerate(part_order()):
        start = pl.multiple_of(part * width, 128)
        source = w_out_ref.at[:, pl.ds(start, width)]
        later.append(pltpu.make_async_copy(source, part_refs[slot], sems.at[5 + slot]))
    for copy in scalars + first + later:
        copy.start()

    for copy in scalars:
        copy.wait()
    ctx = lax.axis_index("ctx")
    row = lax.broadcasted_iota(jnp.int32, (rows, rows), 0)
    lane = lax.broadcasted_iota(jnp.int32, (rows, rows), 1)
    query_pos = jnp.where(row < half, order_ref[2 * ctx], order_ref[2 * ctx + 1]) * half + row % half
    offset = lane % half
    for step, source in enumerate(key_sources()):
        key_place = jnp.where(lane < half, order_ref[2 * source], order_ref[2 * source + 1])
        length = jnp.where(lane < half, lens_ref[2 * source], lens_ref[2 * source + 1])
        visible = (key_place * half + offset <= query_pos) & (offset < length)
        bias_ref[:, step * rows : (step + 1) * rows] = jnp.where(visible, 0.0, HIDDEN)

    for copy in first:
        copy.wait()
    for head in range(heads):
        nope = query_buffer[:, head * QUERY : head * QUERY + HEAD_DIM]
        rope = query_buffer[:, head * QUERY + HEAD_DIM : (head + 1) * QUERY]
        weight = key_buffer[:, head * HEAD_DIM : (head + 1) * HEAD_DIM]
        product = lax.dot_general(nope, weight, NT, preferred_element_type=jnp.float32)
        here = slice(head * rows, (head + 1) * rows)
        folded_ref[here, :LATENT] = product.astype(jnp.bfloat16)
        folded_ref[here, LATENT:] = rope
    for copy in later:
        copy.wait()


def prepare(*operands):
    order, lens, queries, w_keys, w_values, w_out = operands
    rows = queries.shape[0]
    count = lax.axis_size("ctx")
    heads = w_keys.shape[1] // HEAD_DIM
    part = jax.ShapeDtypeStruct((w_out.shape[0], w_out.shape[1] // PARTS), jnp.bfloat16)
    return pl.pallas_call(
        functools.partial(prepare_kernel, rows // 2),
        out_shape=[
            jax.ShapeDtypeStruct((heads * rows, LATENT + ROPE), jnp.bfloat16),
            jax.ShapeDtypeStruct((rows, count * rows), jnp.float32),
            jax.ShapeDtypeStruct(w_values.shape, jnp.bfloat16),
        ]
        + [part] * PARTS,
        in_specs=[HBM] * 6,
        out_specs=[VMEM] * (3 + PARTS),
        scratch_shapes=[
            pltpu.SMEM(order.shape, jnp.int32),
            pltpu.SMEM(lens.shape, jnp.int32),
            pltpu.VMEM(queries.shape, jnp.bfloat16),
            pltpu.VMEM(w_keys.shape, jnp.bfloat16),
            pltpu.SemaphoreType.DMA((5 + PARTS,)),
        ],
        compiler_params=PARAMS,
        cost_estimate=pl.CostEstimate(
            flops=2 * rows * heads * HEAD_DIM * LATENT,
            bytes_accessed=2 * (queries.size + w_keys.size + w_values.size + w_out.size),
            transcendentals=0,
        ),
        name="prepare",
    )(*[pltpu.with_memory_space_constraint(item, pltpu.HBM) for item in operands])


def place_if(keys_ref, slot, block_ref, condition):
    rows = block_ref.shape[1]

    @pl.when(condition)
    def _():
        keys_ref[:, slot * rows : (slot + 1) * rows] = block_ref[...]


def project(attended_ref, part_ref, share_refs):
    start = 0
    for share_ref in share_refs:
        stop = start + share_ref.shape[1]
        share = jnp.dot(
            attended_ref[...], part_ref[:, start:stop], preferred_element_type=jnp.float32
        )
        share_ref[...] = share.astype(share_ref.dtype)
        start = stop


def attend_kernel(count, paired, folded_ref, bias_ref, values_ref, part_ref, *rest):
    blocks, (attended_ref, *shares, keys_ref, latents_ref) = rest[:count], rest[count:]
    rows = bias_ref.shape[0]
    heads = values_ref.shape[1] // HEAD_DIM
    certain = count - 2 if paired else count
    for slot in range(certain):
        keys_ref[:, slot * rows : (slot + 1) * rows] = blocks[slot][...]
    if paired:
        direct = (lax.axis_index("ctx") ^ lax.axis_index("head")) & 1 == 0
        place_if(keys_ref, certain, blocks[certain], direct)
        place_if(keys_ref, certain, blocks[certain + 1], jnp.logical_not(direct))
    for slot in range(keys_ref.shape[1] // rows):
        here = slice(slot * rows, (slot + 1) * rows)
        latents_ref[here, :] = keys_ref[:LATENT, here].T
    stacked = ROWS_AT_ONCE // rows
    bias = jnp.concatenate([bias_ref[...]] * stacked, axis=0)
    for group in range(heads // stacked):
        lines = slice(group * ROWS_AT_ONCE, (group + 1) * ROWS_AT_ONCE)
        scores = jnp.dot(folded_ref[lines, :], keys_ref[...], preferred_element_type=jnp.float32)
        scores = scores + bias
        peak = jnp.max(scores, axis=1, keepdims=True)
        weights = jnp.exp2((scores - peak) * jnp.float32(EXPONENT))
        inverse = 1.0 / jnp.sum(weights, axis=1, keepdims=True)
        mixed = jnp.dot(
            weights.astype(jnp.bfloat16), latents_ref[...], preferred_element_type=jnp.float32
        ).astype(jnp.bfloat16)
        for inner in range(stacked):
            head = group * stacked + inner
            columns = slice(head * HEAD_DIM, (head + 1) * HEAD_DIM)
            lines = slice(inner * rows, (inner + 1) * rows)
            value = jnp.dot(
                mixed[lines, :], values_ref[:, columns], preferred_element_type=jnp.float32
            )
            attended_ref[:, columns] = (value * inverse[lines, :]).astype(jnp.bfloat16)
    project(attended_ref, part_ref, shares)


def share_shapes(rows, widths, kind):
    return [jax.ShapeDtypeStruct((rows, width), kind) for width in widths]


def attend(folded, bias, values, part, blocks, widths):
    rows, keys = bias.shape
    heads = values.shape[1] // HEAD_DIM
    flops = 2 * heads * rows * (keys * (2 * LATENT + ROPE) + LATENT * HEAD_DIM)
    return pl.pallas_call(
        functools.partial(attend_kernel, len(blocks), is_paired()),
        out_shape=share_shapes(rows, [values.shape[1]] + widths, jnp.bfloat16),
        in_specs=[VMEM] * (4 + len(blocks)),
        out_specs=[VMEM] * (1 + len(widths)),
        scratch_shapes=[
            pltpu.VMEM((LATENT + ROPE, keys), jnp.bfloat16),
            pltpu.VMEM((keys, LATENT), jnp.bfloat16),
        ],
        compiler_params=PARAMS,
        cost_estimate=pl.CostEstimate(
            flops=flops + 2 * rows * part.size,
            bytes_accessed=2 * (folded.size + values.size + part.size),
            transcendentals=heads * rows * keys,
        ),
        name="attend",
    )(folded, bias, values, part, *blocks)


def project_kernel(pieces, attended_ref, *refs):
    parts, shares = refs[: len(pieces)], list(refs[len(pieces) :])
    for part_ref, count in zip(parts, pieces):
        project(attended_ref, part_ref, shares[:count])
        shares = shares[count:]


def project_parts(attended, parts, outs):
    flat = [out for group in outs for out in group]
    return pl.pallas_call(
        functools.partial(project_kernel, [len(group) for group in outs]),
        out_shape=flat,
        in_specs=[VMEM] * (1 + len(parts)),
        out_specs=[VMEM] * len(flat),
        compiler_params=PARAMS,
        cost_estimate=SHORT,
        name="project_parts",
    )(attended, *parts)


def next_to(ctx, head):
    return (ctx + 1 + 2 * (head & 1)) & 3, head


def two_away(ctx, head):
    return (ctx ^ 2 if (ctx ^ head) & 1 == 0 else ctx), head


def other_core(ctx, head):
    return ctx, head ^ 1


def other_chip(ctx, head):
    return ctx, head ^ 2


def shards(queries, latent, w_keys, w_values, w_out, block_order, valid_lengths):
    ctx_count = lax.axis_size("ctx")
    rows = queries.shape[0]
    width = w_out.shape[1] // PARTS
    block = latent.T
    prepared = prepare(block_order, valid_lengths, queries, w_keys, w_values, w_out)
    narrow, wide = jnp.bfloat16, jnp.float32

    if not is_paired():
        blocks = [block]
        for step in range(1, ctx_count):
            blocks.append(routed(block, lambda ctx, head: ((ctx + step) % ctx_count, head)))
        folded, bias, values, *parts = prepared
        attended, share = attend(folded, bias, values, parts[0], blocks, [width])
        outs = [share_shapes(rows, [width], narrow)] * (PARTS - 1)
        shares = [share] + list(project_parts(attended, parts[1:], outs))
        whole = jnp.concatenate(shares, axis=1)
        return lax.psum_scatter(whole, "head", scatter_dimension=1, tiled=True)

    near = routed(block, next_to)
    far = routed(block, two_away)
    near, prepared = lax.optimization_barrier((near, prepared))
    near_swapped = routed(near, other_core)
    far, near_swapped = lax.optimization_barrier((far, near_swapped))
    far_swapped = routed(far, other_core)
    folded, bias, values, *parts = prepared
    blocks = [block, near, near_swapped, far, far_swapped]

    attended, across = attend(folded, bias, values, parts[0], blocks, [width])
    received = routed(across, other_core)
    outs = [share_shapes(rows, [width], kind) for kind in (wide, narrow, wide)]
    far_part, beside, own = project_parts(attended, parts[1:], outs)
    far_part = (far_part + received.astype(wide)).astype(narrow)
    far_part, beside = lax.optimization_barrier((far_part, beside))
    far_part = routed(far_part, other_chip).astype(wide)
    beside = routed(beside, other_core).astype(wide)
    return (own + beside + far_part).astype(narrow)


def solution(mesh):
    in_specs = (
        P(("groups", "ctx"), "head"),
        P(("groups", "ctx"), None),
        P(None, "head"),
        P(None, "head"),
        P("head", None),
        P("groups"),
        P("groups"),
    )
    out_specs = P(("groups", "ctx"), "head")
    return jax.shard_map(shards, mesh=mesh, in_specs=in_specs, out_specs=out_specs, check_vma=False)
```

```python
import functools

import jax
import jax.numpy as jnp
from jax import lax
from jax.experimental import pallas as pl
from jax.experimental.pallas import tpu as pltpu
from jax.sharding import PartitionSpec as P

LATENT = 512
ROPE = 64
HEAD_DIM = 128
QUERY = HEAD_DIM + ROPE
PARTS = 4
COLUMNS_AT_ONCE = 256
VMEM_BYTES = 32 * 1024 * 1024
HIDDEN = -1e30


def routed(value, route):
    ctx_count = lax.axis_size("ctx")
    head_count = lax.axis_size("head")
    pairs = []
    for ctx in range(ctx_count):
        for head in range(head_count):
            target = route(ctx, head)
            if target is not None:
                pairs.append((ctx * head_count + head, target[0] * head_count + target[1]))
    return lax.ppermute(value, ("ctx", "head"), pairs)


def is_paired():
    return lax.axis_size("ctx") == 4 and lax.axis_size("head") == 4


def key_sources():
    count = lax.axis_size("ctx")
    ctx = lax.axis_index("ctx")
    if is_paired():
        step = 1 + 2 * (lax.axis_index("head") & 1)
        return [ctx, (ctx - step) & 3, (ctx + step) & 3, ctx ^ 2]
    return [ctx] + [lax.rem(ctx + (count - step), count) for step in range(1, count)]


def part_order():
    if is_paired():
        head = lax.axis_index("head")
        return [head ^ 3, head ^ 2, head ^ 1, head]
    return list(range(PARTS))


VMEM = pl.BlockSpec(memory_space=pltpu.VMEM)
HBM = pl.BlockSpec(memory_space=pltpu.HBM)
PARAMS = pltpu.CompilerParams(vmem_limit_bytes=VMEM_BYTES)
SHORT = pl.CostEstimate(flops=1024, bytes_accessed=1024, transcendentals=0)
EXPONENT = QUERY**-0.5 * 1.4426950408889634


def prepare_kernel(half, *refs):
    order_hbm, lens_hbm, queries_ref, w_keys_ref, w_values_ref, w_out_ref = refs[:6]
    folded_ref, bias_ref, values_ref = refs[6:9]
    part_refs = refs[9 : 9 + PARTS]
    order_ref, lens_ref, query_buffer, key_buffer, value_buffer, turned_ref, sems = refs[9 + PARTS :]
    width = w_out_ref.shape[1] // PARTS
    heads = w_keys_ref.shape[1] // HEAD_DIM
    rows = 2 * half
    scalars = [
        pltpu.make_async_copy(order_hbm, order_ref, sems.at[0]),
        pltpu.make_async_copy(lens_hbm, lens_ref, sems.at[1]),
    ]
    first = [
        pltpu.make_async_copy(queries_ref, query_buffer, sems.at[2]),
        pltpu.make_async_copy(w_keys_ref, key_buffer, sems.at[3]),
    ]
    values_copy = pltpu.make_async_copy(w_values_ref, value_buffer, sems.at[4])
    later = []
    for slot, part in enumerate(part_order()):
        start = pl.multiple_of(part * width, 128)
        source = w_out_ref.at[:, pl.ds(start, width)]
        later.append(pltpu.make_async_copy(source, part_refs[slot], sems.at[5 + slot]))
    for copy in scalars + first + [values_copy] + later:
        copy.start()

    for copy in scalars:
        copy.wait()
    ctx = lax.axis_index("ctx")
    lane = lax.broadcasted_iota(jnp.int32, (rows, rows), 1)
    key = lax.broadcasted_iota(jnp.int32, (rows, rows), 0)
    query_pos = jnp.where(lane < half, order_ref[2 * ctx], order_ref[2 * ctx + 1]) * half
    query_pos = query_pos + lane % half
    offset = key % half
    for step, source in enumerate(key_sources()):
        key_place = jnp.where(key < half, order_ref[2 * source], order_ref[2 * source + 1])
        length = jnp.where(key < half, lens_ref[2 * source], lens_ref[2 * source + 1])
        visible = (key_place * half + offset <= query_pos) & (offset < length)
        bias_ref[step * rows : (step + 1) * rows, :] = jnp.where(visible, 0.0, HIDDEN)

    for copy in first:
        copy.wait()
    turned_ref[...] = query_buffer[...].T
    for head in range(heads):
        nope = turned_ref[head * QUERY : head * QUERY + HEAD_DIM, :]
        weight = key_buffer[:, head * HEAD_DIM : (head + 1) * HEAD_DIM]
        product = jnp.dot(weight, nope, preferred_element_type=jnp.float32)
        here = slice(head * rows, (head + 1) * rows)
        folded_ref[:LATENT, here] = product.astype(jnp.bfloat16)
        folded_ref[LATENT:, here] = turned_ref[head * QUERY + HEAD_DIM : (head + 1) * QUERY, :]
    values_copy.wait()
    values_ref[...] = value_buffer[...].T
    for copy in later:
        copy.wait()


def prepare(*operands):
    order, lens, queries, w_keys, w_values, w_out = operands
    rows = queries.shape[0]
    count = lax.axis_size("ctx")
    heads = w_keys.shape[1] // HEAD_DIM
    part = jax.ShapeDtypeStruct((w_out.shape[0], w_out.shape[1] // PARTS), jnp.bfloat16)
    return pl.pallas_call(
        functools.partial(prepare_kernel, rows // 2),
        out_shape=[
            jax.ShapeDtypeStruct((LATENT + ROPE, heads * rows), jnp.bfloat16),
            jax.ShapeDtypeStruct((count * rows, rows), jnp.float32),
            jax.ShapeDtypeStruct(w_values.shape[::-1], jnp.bfloat16),
        ]
        + [part] * PARTS,
        in_specs=[HBM] * 6,
        out_specs=[VMEM] * (3 + PARTS),
        scratch_shapes=[
            pltpu.SMEM(order.shape, jnp.int32),
            pltpu.SMEM(lens.shape, jnp.int32),
            pltpu.VMEM(queries.shape, jnp.bfloat16),
            pltpu.VMEM(w_keys.shape, jnp.bfloat16),
            pltpu.VMEM(w_values.shape, jnp.bfloat16),
            pltpu.VMEM(queries.shape[::-1], jnp.bfloat16),
            pltpu.SemaphoreType.DMA((5 + PARTS,)),
        ],
        compiler_params=PARAMS,
        cost_estimate=pl.CostEstimate(
            flops=2 * rows * heads * HEAD_DIM * LATENT,
            bytes_accessed=2 * (queries.size + w_keys.size + w_values.size + w_out.size),
            transcendentals=0,
        ),
        name="prepare",
    )(*[pltpu.with_memory_space_constraint(item, pltpu.HBM) for item in operands])


def place_if(keys_ref, slot, block_ref, condition):
    rows = block_ref.shape[1]

    @pl.when(condition)
    def _():
        keys_ref[:, slot * rows : (slot + 1) * rows] = block_ref[...]


def project(attended_ref, part_ref, share_refs):
    start = 0
    for share_ref in share_refs:
        stop = start + share_ref.shape[1]
        share = jnp.dot(
            attended_ref[...], part_ref[:, start:stop], preferred_element_type=jnp.float32
        )
        share_ref[...] = share.astype(share_ref.dtype)
        start = stop


def attend_kernel(count, paired, folded_ref, bias_ref, values_ref, part_ref, *rest):
    blocks, rest = rest[:count], rest[count:]
    attended_ref, *shares, turned_ref, keys_ref, heads_ref = rest
    rows = bias_ref.shape[1]
    certain = count - 2 if paired else count
    for slot in range(certain):
        turned_ref[:, slot * rows : (slot + 1) * rows] = blocks[slot][...]
    if paired:
        direct = (lax.axis_index("ctx") ^ lax.axis_index("head")) & 1 == 0
        place_if(turned_ref, certain, blocks[certain], direct)
        place_if(turned_ref, certain, blocks[certain + 1], jnp.logical_not(direct))
    for slot in range(keys_ref.shape[0] // rows):
        here = slice(slot * rows, (slot + 1) * rows)
        keys_ref[here, :] = turned_ref[:, here].T
    stacked = COLUMNS_AT_ONCE // rows
    bias = jnp.concatenate([bias_ref[...]] * stacked, axis=1)
    for group in range(folded_ref.shape[1] // COLUMNS_AT_ONCE):
        columns = slice(group * COLUMNS_AT_ONCE, (group + 1) * COLUMNS_AT_ONCE)
        scores = jnp.dot(keys_ref[...], folded_ref[:, columns], preferred_element_type=jnp.float32)
        scores = scores + bias
        peak = jnp.max(scores, axis=0, keepdims=True)
        weights = jnp.exp2((scores - peak) * jnp.float32(EXPONENT))
        inverse = 1.0 / jnp.sum(weights, axis=0, keepdims=True)
        mixed = jnp.dot(
            turned_ref[:LATENT, :], weights.astype(jnp.bfloat16), preferred_element_type=jnp.float32
        ).astype(jnp.bfloat16)
        for inner in range(stacked):
            head = group * stacked + inner
            lines = slice(head * HEAD_DIM, (head + 1) * HEAD_DIM)
            columns = slice(inner * rows, (inner + 1) * rows)
            value = jnp.dot(
                values_ref[lines, :], mixed[:, columns], preferred_element_type=jnp.float32
            )
            heads_ref[lines, :] = (value * inverse[:, columns]).astype(jnp.bfloat16)
    attended_ref[...] = heads_ref[...].T
    project(attended_ref, part_ref, shares)


def share_shapes(rows, widths, kind):
    return [jax.ShapeDtypeStruct((rows, width), kind) for width in widths]


def attend(folded, bias, values, part, blocks, widths):
    keys, rows = bias.shape
    heads = values.shape[0] // HEAD_DIM
    flops = 2 * heads * rows * (keys * (2 * LATENT + ROPE) + LATENT * HEAD_DIM)
    return pl.pallas_call(
        functools.partial(attend_kernel, len(blocks), is_paired()),
        out_shape=share_shapes(rows, [values.shape[0]] + widths, jnp.bfloat16),
        in_specs=[VMEM] * (4 + len(blocks)),
        out_specs=[VMEM] * (1 + len(widths)),
        scratch_shapes=[
            pltpu.VMEM((LATENT + ROPE, keys), jnp.bfloat16),
            pltpu.VMEM((keys, LATENT + ROPE), jnp.bfloat16),
            pltpu.VMEM((values.shape[0], rows), jnp.bfloat16),
        ],
        compiler_params=PARAMS,
        cost_estimate=pl.CostEstimate(
            flops=flops + 2 * rows * part.size,
            bytes_accessed=2 * (folded.size + values.size + part.size),
            transcendentals=heads * rows * keys,
        ),
        name="attend",
    )(folded, bias, values, part, *blocks)


def project_kernel(pieces, attended_ref, *refs):
    parts, shares = refs[: len(pieces)], list(refs[len(pieces) :])
    for part_ref, count in zip(parts, pieces):
        project(attended_ref, part_ref, shares[:count])
        shares = shares[count:]


def project_parts(attended, parts, outs):
    flat = [out for group in outs for out in group]
    return pl.pallas_call(
        functools.partial(project_kernel, [len(group) for group in outs]),
        out_shape=flat,
        in_specs=[VMEM] * (1 + len(parts)),
        out_specs=[VMEM] * len(flat),
        compiler_params=PARAMS,
        cost_estimate=SHORT,
        name="project_parts",
    )(attended, *parts)


def next_to(ctx, head):
    return (ctx + 1 + 2 * (head & 1)) & 3, head


def two_away(ctx, head):
    return (ctx ^ 2 if (ctx ^ head) & 1 == 0 else ctx), head


def other_core(ctx, head):
    return ctx, head ^ 1


def other_chip(ctx, head):
    return ctx, head ^ 2


def shards(queries, latent, w_keys, w_values, w_out, block_order, valid_lengths):
    ctx_count = lax.axis_size("ctx")
    rows = queries.shape[0]
    width = w_out.shape[1] // PARTS
    block = latent.T
    prepared = prepare(block_order, valid_lengths, queries, w_keys, w_values, w_out)
    narrow, wide = jnp.bfloat16, jnp.float32

    if not is_paired():
        blocks = [block]
        for step in range(1, ctx_count):
            blocks.append(routed(block, lambda ctx, head: ((ctx + step) % ctx_count, head)))
        folded, bias, values, *parts = prepared
        attended, share = attend(folded, bias, values, parts[0], blocks, [width])
        outs = [share_shapes(rows, [width], narrow)] * (PARTS - 1)
        shares = [share] + list(project_parts(attended, parts[1:], outs))
        whole = jnp.concatenate(shares, axis=1)
        return lax.psum_scatter(whole, "head", scatter_dimension=1, tiled=True)

    near = routed(block, next_to)
    far = routed(block, two_away)
    near, prepared = lax.optimization_barrier((near, prepared))
    near_swapped = routed(near, other_core)
    far, near_swapped = lax.optimization_barrier((far, near_swapped))
    far_swapped = routed(far, other_core)
    folded, bias, values, *parts = prepared
    blocks = [block, near, near_swapped, far, far_swapped]

    attended, across = attend(folded, bias, values, parts[0], blocks, [width])
    received = routed(across, other_core)
    outs = [share_shapes(rows, [width], kind) for kind in (wide, narrow, wide)]
    far_part, beside, own = project_parts(attended, parts[1:], outs)
    far_part = (far_part + received.astype(wide)).astype(narrow)
    far_part = routed(far_part, other_chip).astype(wide)
    beside = routed(beside, other_core).astype(wide)
    return (own + beside + far_part).astype(narrow)


def solution(mesh):
    in_specs = (
        P(("groups", "ctx"), "head"),
        P(("groups", "ctx"), None),
        P(None, "head"),
        P(None, "head"),
        P("head", None),
        P("groups"),
        P("groups"),
    )
    out_specs = P(("groups", "ctx"), "head")
    return jax.shard_map(shards, mesh=mesh, in_specs=in_specs, out_specs=out_specs, check_vma=False)
```

```python
import functools

import jax
import jax.numpy as jnp
from jax import lax
from jax.experimental import pallas as pl
from jax.experimental.pallas import tpu as pltpu
from jax.sharding import PartitionSpec as P

LATENT = 512
ROPE = 64
HEAD_DIM = 128
QUERY = HEAD_DIM + ROPE
PARTS = 4
PADDED = 256
NT = (((1,), (1,)), ((), ()))
VMEM_BYTES = 32 * 1024 * 1024
HIDDEN = -1e30


def routed(value, route):
    ctx_count = lax.axis_size("ctx")
    head_count = lax.axis_size("head")
    pairs = []
    for ctx in range(ctx_count):
        for head in range(head_count):
            target = route(ctx, head)
            if target is not None:
                pairs.append((ctx * head_count + head, target[0] * head_count + target[1]))
    return lax.ppermute(value, ("ctx", "head"), pairs)


def is_paired():
    return lax.axis_size("ctx") == 4 and lax.axis_size("head") == 4


def key_sources():
    count = lax.axis_size("ctx")
    ctx = lax.axis_index("ctx")
    if is_paired():
        step = 1 + 2 * (lax.axis_index("head") & 1)
        return [ctx, (ctx - step) & 3, (ctx + step) & 3, ctx ^ 2]
    return [ctx] + [lax.rem(ctx + (count - step), count) for step in range(1, count)]


def part_order():
    if is_paired():
        head = lax.axis_index("head")
        return [head ^ 3, head ^ 2, head ^ 1, head]
    return list(range(PARTS))


VMEM = pl.BlockSpec(memory_space=pltpu.VMEM)
HBM = pl.BlockSpec(memory_space=pltpu.HBM)
PARAMS = pltpu.CompilerParams(vmem_limit_bytes=VMEM_BYTES)
SHORT = pl.CostEstimate(flops=1024, bytes_accessed=1024, transcendentals=0)
EXPONENT = QUERY**-0.5 * 1.4426950408889634


def expand(turned, w_keys_ref, w_values_ref, keys_ref, values_ref):
    rows = turned.shape[1]
    latents = turned.T
    compressed = latents[:, :LATENT]
    rope = jnp.concatenate(
        [latents[:, LATENT:], jnp.zeros((rows, PADDED - QUERY), jnp.bfloat16)], axis=1
    )
    nope = jnp.dot(compressed, w_keys_ref[...], preferred_element_type=jnp.float32)
    nope = nope.astype(jnp.bfloat16)
    for head in range(w_keys_ref.shape[1] // HEAD_DIM):
        middle = head * PADDED + HEAD_DIM
        keys_ref[:, head * PADDED : middle] = nope[:, head * HEAD_DIM : (head + 1) * HEAD_DIM]
        keys_ref[:, middle : (head + 1) * PADDED] = rope
    values = jnp.dot(compressed, w_values_ref[...], preferred_element_type=jnp.float32)
    values_ref[...] = values.astype(jnp.bfloat16)


def prepare_kernel(half, *refs):
    order_hbm, lens_hbm, queries_ref, block_ref, w_keys_ref, w_values_ref, w_out_ref = refs[:7]
    padded_ref, bias_ref, keys_ref, values_ref, key_weight, value_weight = refs[7:13]
    part_refs = refs[13 : 13 + PARTS]
    order_ref, lens_ref, query_buffer, block_buffer, sems = refs[13 + PARTS :]
    width = w_out_ref.shape[1] // PARTS
    heads = w_keys_ref.shape[1] // HEAD_DIM
    rows = 2 * half
    scalars = [
        pltpu.make_async_copy(order_hbm, order_ref, sems.at[0]),
        pltpu.make_async_copy(lens_hbm, lens_ref, sems.at[1]),
    ]
    query_copy = pltpu.make_async_copy(queries_ref, query_buffer, sems.at[2])
    first = [
        pltpu.make_async_copy(block_ref, block_buffer, sems.at[3]),
        pltpu.make_async_copy(w_keys_ref, key_weight, sems.at[4]),
        pltpu.make_async_copy(w_values_ref, value_weight, sems.at[5]),
    ]
    later = []
    for slot, part in enumerate(part_order()):
        start = pl.multiple_of(part * width, 128)
        source = w_out_ref.at[:, pl.ds(start, width)]
        later.append(pltpu.make_async_copy(source, part_refs[slot], sems.at[6 + slot]))
    for copy in scalars + [query_copy] + first + later:
        copy.start()

    for copy in scalars:
        copy.wait()
    ctx = lax.axis_index("ctx")
    row = lax.broadcasted_iota(jnp.int32, (rows, rows), 0)
    lane = lax.broadcasted_iota(jnp.int32, (rows, rows), 1)
    query_pos = jnp.where(row < half, order_ref[2 * ctx], order_ref[2 * ctx + 1]) * half + row % half
    offset = lane % half
    for step, source in enumerate(key_sources()):
        key_place = jnp.where(lane < half, order_ref[2 * source], order_ref[2 * source + 1])
        length = jnp.where(lane < half, lens_ref[2 * source], lens_ref[2 * source + 1])
        visible = (key_place * half + offset <= query_pos) & (offset < length)
        bias_ref[:, step * rows : (step + 1) * rows] = jnp.where(visible, 0.0, HIDDEN)

    query_copy.wait()
    nothing = jnp.zeros((rows, PADDED - QUERY), jnp.bfloat16)
    for head in range(heads):
        query = query_buffer[:, head * QUERY : (head + 1) * QUERY]
        padded_ref[:, head * PADDED : (head + 1) * PADDED] = jnp.concatenate(
            [query, nothing], axis=1
        )
    for copy in first:
        copy.wait()
    expand(block_buffer[...], key_weight, value_weight, keys_ref, values_ref)
    for copy in later:
        copy.wait()


def narrow_shape(*shape):
    return jax.ShapeDtypeStruct(shape, jnp.bfloat16)


def prepare(*operands):
    order, lens, queries, block, w_keys, w_values, w_out = operands
    rows = queries.shape[0]
    count = lax.axis_size("ctx")
    heads = w_keys.shape[1] // HEAD_DIM
    return pl.pallas_call(
        functools.partial(prepare_kernel, rows // 2),
        out_shape=[
            narrow_shape(rows, heads * PADDED),
            jax.ShapeDtypeStruct((rows, count * rows), jnp.float32),
            narrow_shape(rows, heads * PADDED),
            narrow_shape(rows, heads * HEAD_DIM),
            narrow_shape(*w_keys.shape),
            narrow_shape(*w_values.shape),
        ]
        + [narrow_shape(w_out.shape[0], w_out.shape[1] // PARTS)] * PARTS,
        in_specs=[HBM] * 7,
        out_specs=[VMEM] * (6 + PARTS),
        scratch_shapes=[
            pltpu.SMEM(order.shape, jnp.int32),
            pltpu.SMEM(lens.shape, jnp.int32),
            pltpu.VMEM(queries.shape, jnp.bfloat16),
            pltpu.VMEM(block.shape, jnp.bfloat16),
            pltpu.SemaphoreType.DMA((6 + PARTS,)),
        ],
        compiler_params=PARAMS,
        cost_estimate=pl.CostEstimate(
            flops=4 * rows * heads * HEAD_DIM * LATENT,
            bytes_accessed=2 * (queries.size + w_keys.size + w_values.size + w_out.size),
            transcendentals=0,
        ),
        name="prepare",
    )(*[pltpu.with_memory_space_constraint(item, pltpu.HBM) for item in operands])


def expand_kernel(block_ref, w_keys_ref, w_values_ref, keys_ref, values_ref):
    expand(block_ref[...], w_keys_ref, w_values_ref, keys_ref, values_ref)


def expand_block(block, w_keys, w_values):
    rows = block.shape[1]
    heads = w_keys.shape[1] // HEAD_DIM
    return pl.pallas_call(
        expand_kernel,
        out_shape=[narrow_shape(rows, heads * PADDED), narrow_shape(rows, heads * HEAD_DIM)],
        in_specs=[VMEM] * 3,
        out_specs=[VMEM] * 2,
        compiler_params=PARAMS,
        cost_estimate=pl.CostEstimate(
            flops=4 * rows * w_keys.size, bytes_accessed=2 * w_keys.size, transcendentals=0
        ),
        name="expand_block",
    )(block, w_keys, w_values)


def project(attended_ref, part_ref, share_refs):
    start = 0
    for share_ref in share_refs:
        stop = start + share_ref.shape[1]
        share = jnp.dot(
            attended_ref[...], part_ref[:, start:stop], preferred_element_type=jnp.float32
        )
        share_ref[...] = share.astype(share_ref.dtype)
        start = stop


def take_if(target_ref, block_ref, condition):
    @pl.when(condition)
    def _():
        target_ref[...] = block_ref[...]


def attend_kernel(count, padded_ref, bias_ref, key_weight, value_weight, part_ref, *refs):
    direct_ref, swapped_ref = refs[:2]
    keys, values = list(refs[2 : 2 + count]), list(refs[2 + count : 2 + 2 * count])
    attended_ref, *shares, turned_ref, last_keys, last_values = refs[2 + 2 * count :]
    rows = bias_ref.shape[0]
    heads = value_weight.shape[1] // HEAD_DIM
    direct = (lax.axis_index("ctx") ^ lax.axis_index("head")) & 1 == 0
    take_if(turned_ref, direct_ref, direct)
    take_if(turned_ref, swapped_ref, jnp.logical_not(direct))
    expand(turned_ref[...], key_weight, value_weight, last_keys, last_values)
    keys.append(last_keys)
    values.append(last_values)
    for head in range(heads):
        wide = slice(head * PADDED, (head + 1) * PADDED)
        columns = slice(head * HEAD_DIM, (head + 1) * HEAD_DIM)
        query = padded_ref[:, wide]
        pieces = []
        for start in range(0, count + 1, 2):
            pair = jnp.concatenate([ref[:, wide] for ref in keys[start : start + 2]], axis=0)
            pieces.append(lax.dot_general(query, pair, NT, preferred_element_type=jnp.float32))
        scores = jnp.concatenate(pieces, axis=1) + bias_ref[...]
        peak = jnp.max(scores, axis=1, keepdims=True)
        weights = jnp.exp2((scores - peak) * jnp.float32(EXPONENT))
        inverse = 1.0 / jnp.sum(weights, axis=1, keepdims=True)
        value = jnp.dot(
            weights.astype(jnp.bfloat16),
            jnp.concatenate([ref[:, columns] for ref in values], axis=0),
            preferred_element_type=jnp.float32,
        )
        attended_ref[:, columns] = (value * inverse).astype(jnp.bfloat16)
    project(attended_ref, part_ref, shares)


def share_shapes(rows, widths, kind):
    return [jax.ShapeDtypeStruct((rows, width), kind) for width in widths]


def attend(padded, bias, weights, part, last, keys, values, widths):
    rows, key_count = bias.shape
    heads = values[0].shape[1] // HEAD_DIM
    flops = 4 * heads * rows * key_count * PADDED + 4 * rows * weights[0].size
    return pl.pallas_call(
        functools.partial(attend_kernel, len(keys)),
        out_shape=share_shapes(rows, [heads * HEAD_DIM] + widths, jnp.bfloat16),
        in_specs=[VMEM] * (7 + 2 * len(keys)),
        out_specs=[VMEM] * (1 + len(widths)),
        scratch_shapes=[
            pltpu.VMEM(last[0].shape, jnp.bfloat16),
            pltpu.VMEM(keys[0].shape, jnp.bfloat16),
            pltpu.VMEM(values[0].shape, jnp.bfloat16),
        ],
        compiler_params=PARAMS,
        cost_estimate=pl.CostEstimate(
            flops=flops + 2 * rows * part.size,
            bytes_accessed=2 * (weights[0].size + weights[1].size + part.size),
            transcendentals=heads * rows * key_count,
        ),
        name="attend",
    )(padded, bias, *weights, part, *last, *keys, *values)


def project_kernel(pieces, attended_ref, *refs):
    parts, shares = refs[: len(pieces)], list(refs[len(pieces) :])
    for part_ref, count in zip(parts, pieces):
        project(attended_ref, part_ref, shares[:count])
        shares = shares[count:]


def project_parts(attended, parts, outs):
    flat = [out for group in outs for out in group]
    return pl.pallas_call(
        functools.partial(project_kernel, [len(group) for group in outs]),
        out_shape=flat,
        in_specs=[VMEM] * (1 + len(parts)),
        out_specs=[VMEM] * len(flat),
        compiler_params=PARAMS,
        cost_estimate=SHORT,
        name="project_parts",
    )(attended, *parts)


def next_to(ctx, head):
    return (ctx + 1 + 2 * (head & 1)) & 3, head


def two_away(ctx, head):
    return (ctx ^ 2 if (ctx ^ head) & 1 == 0 else ctx), head


def other_core(ctx, head):
    return ctx, head ^ 1


def other_chip(ctx, head):
    return ctx, head ^ 2


def shards(queries, latent, w_keys, w_values, w_out, block_order, valid_lengths):
    ctx_count = lax.axis_size("ctx")
    rows = queries.shape[0]
    width = w_out.shape[1] // PARTS
    block = latent.T
    prepared = prepare(block_order, valid_lengths, queries, block, w_keys, w_values, w_out)
    narrow, wide = jnp.bfloat16, jnp.float32

    if not is_paired():
        blocks = []
        for step in range(1, ctx_count):
            blocks.append(routed(block, lambda ctx, head: ((ctx + step) % ctx_count, head)))
        padded, bias, own_keys, own_values, *weights = prepared
        weights, parts = weights[:2], weights[2:]
        expanded = [(own_keys, own_values)]
        expanded += [expand_block(piece, *weights) for piece in blocks[:-1]]
        keys, values = zip(*expanded)
        last = [blocks[-1], blocks[-1]]
        attended, share = attend(padded, bias, weights, parts[0], last, keys, values, [width])
        outs = [share_shapes(rows, [width], narrow)] * (PARTS - 1)
        shares = [share] + list(project_parts(attended, parts[1:], outs))
        whole = jnp.concatenate(shares, axis=1)
        return lax.psum_scatter(whole, "head", scatter_dimension=1, tiled=True)

    near = routed(block, next_to)
    far = routed(block, two_away)
    near, prepared = lax.optimization_barrier((near, prepared))
    padded, bias, own_keys, own_values, *weights = prepared
    weights, parts = weights[:2], weights[2:]
    near_swapped = routed(near, other_core)
    far, near_swapped = lax.optimization_barrier((far, near_swapped))
    far_swapped = routed(far, other_core)
    expanded = [(own_keys, own_values)]
    expanded += [expand_block(piece, *weights) for piece in (near, near_swapped)]
    keys, values = zip(*expanded)
    last = [far, far_swapped]

    attended, across = attend(padded, bias, weights, parts[0], last, keys, values, [width])
    received = routed(across, other_core)
    outs = [share_shapes(rows, [width], kind) for kind in (wide, narrow, wide)]
    far_part, beside, own = project_parts(attended, parts[1:], outs)
    far_part = (far_part + received.astype(wide)).astype(narrow)
    far_part = routed(far_part, other_chip).astype(wide)
    beside = routed(beside, other_core).astype(wide)
    return (own + beside + far_part).astype(narrow)


def solution(mesh):
    in_specs = (
        P(("groups", "ctx"), "head"),
        P(("groups", "ctx"), None),
        P(None, "head"),
        P(None, "head"),
        P("head", None),
        P("groups"),
        P("groups"),
    )
    out_specs = P(("groups", "ctx"), "head")
    return jax.shard_map(shards, mesh=mesh, in_specs=in_specs, out_specs=out_specs, check_vma=False)
```

```python
import functools

import jax
import jax.numpy as jnp
from jax import lax
from jax.experimental import pallas as pl
from jax.experimental.pallas import tpu as pltpu
from jax.sharding import PartitionSpec as P

LATENT = 512
ROPE = 64
HEAD_DIM = 128
QUERY = HEAD_DIM + ROPE
PARTS = 4
PADDED = 256
NT = (((1,), (1,)), ((), ()))
VMEM_BYTES = 32 * 1024 * 1024
HIDDEN = -1e30


def routed(value, route):
    ctx_count = lax.axis_size("ctx")
    head_count = lax.axis_size("head")
    pairs = []
    for ctx in range(ctx_count):
        for head in range(head_count):
            target = route(ctx, head)
            if target is not None:
                pairs.append((ctx * head_count + head, target[0] * head_count + target[1]))
    return lax.ppermute(value, ("ctx", "head"), pairs)


def is_paired():
    return lax.axis_size("ctx") == 4 and lax.axis_size("head") == 4


def key_sources():
    count = lax.axis_size("ctx")
    ctx = lax.axis_index("ctx")
    if is_paired():
        step = 1 + 2 * (lax.axis_index("head") & 1)
        return [ctx, (ctx - step) & 3, (ctx + step) & 3, ctx ^ 2]
    return [ctx] + [lax.rem(ctx + (count - step), count) for step in range(1, count)]


def part_order():
    if is_paired():
        head = lax.axis_index("head")
        return [head ^ 3, head ^ 2, head ^ 1, head]
    return list(range(PARTS))


VMEM = pl.BlockSpec(memory_space=pltpu.VMEM)
HBM = pl.BlockSpec(memory_space=pltpu.HBM)
PARAMS = pltpu.CompilerParams(vmem_limit_bytes=VMEM_BYTES)
SHORT = pl.CostEstimate(flops=1024, bytes_accessed=1024, transcendentals=0)
EXPONENT = QUERY**-0.5 * 1.4426950408889634


def expand(turned, w_keys_ref, w_values_ref, keys_ref, values_ref):
    rows = turned.shape[1]
    latents = turned.T
    compressed = latents[:, :LATENT]
    rope = jnp.concatenate(
        [latents[:, LATENT:], jnp.zeros((rows, PADDED - QUERY), jnp.bfloat16)], axis=1
    )
    nope = jnp.dot(compressed, w_keys_ref[...], preferred_element_type=jnp.float32)
    nope = nope.astype(jnp.bfloat16)
    for head in range(w_keys_ref.shape[1] // HEAD_DIM):
        middle = head * PADDED + HEAD_DIM
        keys_ref[:, head * PADDED : middle] = nope[:, head * HEAD_DIM : (head + 1) * HEAD_DIM]
        keys_ref[:, middle : (head + 1) * PADDED] = rope
    values = jnp.dot(compressed, w_values_ref[...], preferred_element_type=jnp.float32)
    values_ref[...] = values.astype(jnp.bfloat16)


def prepare_kernel(half, *refs):
    order_hbm, lens_hbm, queries_ref, block_ref, w_keys_ref, w_values_ref = refs[:6]
    padded_ref, bias_ref, keys_ref, values_ref, key_weight, value_weight = refs[6:12]
    order_ref, lens_ref, query_buffer, block_buffer, sems = refs[12:]
    heads = w_keys_ref.shape[1] // HEAD_DIM
    rows = 2 * half
    scalars = [
        pltpu.make_async_copy(order_hbm, order_ref, sems.at[0]),
        pltpu.make_async_copy(lens_hbm, lens_ref, sems.at[1]),
    ]
    query_copy = pltpu.make_async_copy(queries_ref, query_buffer, sems.at[2])
    first = [
        pltpu.make_async_copy(block_ref, block_buffer, sems.at[3]),
        pltpu.make_async_copy(w_keys_ref, key_weight, sems.at[4]),
        pltpu.make_async_copy(w_values_ref, value_weight, sems.at[5]),
    ]
    for copy in scalars + [query_copy] + first:
        copy.start()

    for copy in scalars:
        copy.wait()
    ctx = lax.axis_index("ctx")
    row = lax.broadcasted_iota(jnp.int32, (rows, rows), 0)
    lane = lax.broadcasted_iota(jnp.int32, (rows, rows), 1)
    query_pos = jnp.where(row < half, order_ref[2 * ctx], order_ref[2 * ctx + 1]) * half + row % half
    offset = lane % half
    for step, source in enumerate(key_sources()):
        key_place = jnp.where(lane < half, order_ref[2 * source], order_ref[2 * source + 1])
        length = jnp.where(lane < half, lens_ref[2 * source], lens_ref[2 * source + 1])
        visible = (key_place * half + offset <= query_pos) & (offset < length)
        bias_ref[:, step * rows : (step + 1) * rows] = jnp.where(visible, 0.0, HIDDEN)

    query_copy.wait()
    nothing = jnp.zeros((rows, PADDED - QUERY), jnp.bfloat16)
    for head in range(heads):
        query = query_buffer[:, head * QUERY : (head + 1) * QUERY]
        padded_ref[:, head * PADDED : (head + 1) * PADDED] = jnp.concatenate(
            [query, nothing], axis=1
        )
    for copy in first:
        copy.wait()
    expand(block_buffer[...], key_weight, value_weight, keys_ref, values_ref)


def narrow_shape(*shape):
    return jax.ShapeDtypeStruct(shape, jnp.bfloat16)


def prepare(*operands):
    order, lens, queries, block, w_keys, w_values = operands
    rows = queries.shape[0]
    count = lax.axis_size("ctx")
    heads = w_keys.shape[1] // HEAD_DIM
    return pl.pallas_call(
        functools.partial(prepare_kernel, rows // 2),
        out_shape=[
            narrow_shape(rows, heads * PADDED),
            jax.ShapeDtypeStruct((rows, count * rows), jnp.float32),
            narrow_shape(rows, heads * PADDED),
            narrow_shape(rows, heads * HEAD_DIM),
            narrow_shape(*w_keys.shape),
            narrow_shape(*w_values.shape),
        ],
        in_specs=[HBM] * 6,
        out_specs=[VMEM] * 6,
        scratch_shapes=[
            pltpu.SMEM(order.shape, jnp.int32),
            pltpu.SMEM(lens.shape, jnp.int32),
            pltpu.VMEM(queries.shape, jnp.bfloat16),
            pltpu.VMEM(block.shape, jnp.bfloat16),
            pltpu.SemaphoreType.DMA((6,)),
        ],
        compiler_params=PARAMS,
        cost_estimate=pl.CostEstimate(
            flops=4 * rows * heads * HEAD_DIM * LATENT,
            bytes_accessed=2 * (queries.size + w_keys.size + w_values.size),
            transcendentals=0,
        ),
        name="prepare",
    )(*[pltpu.with_memory_space_constraint(item, pltpu.HBM) for item in operands])


def expand_kernel(block_ref, w_keys_ref, w_values_ref, keys_ref, values_ref):
    expand(block_ref[...], w_keys_ref, w_values_ref, keys_ref, values_ref)


def expand_block(block, w_keys, w_values):
    rows = block.shape[1]
    heads = w_keys.shape[1] // HEAD_DIM
    return pl.pallas_call(
        expand_kernel,
        out_shape=[narrow_shape(rows, heads * PADDED), narrow_shape(rows, heads * HEAD_DIM)],
        in_specs=[VMEM] * 3,
        out_specs=[VMEM] * 2,
        compiler_params=PARAMS,
        cost_estimate=pl.CostEstimate(
            flops=4 * rows * w_keys.size, bytes_accessed=2 * w_keys.size, transcendentals=0
        ),
        name="expand_block",
    )(block, w_keys, w_values)


def project(attended_ref, part_ref, share_refs):
    start = 0
    for share_ref in share_refs:
        stop = start + share_ref.shape[1]
        share = jnp.dot(
            attended_ref[...], part_ref[:, start:stop], preferred_element_type=jnp.float32
        )
        share_ref[...] = share.astype(share_ref.dtype)
        start = stop


def take_if(target_ref, block_ref, condition):
    @pl.when(condition)
    def _():
        target_ref[...] = block_ref[...]


def attend_kernel(count, padded_ref, bias_ref, key_weight, value_weight, w_out_ref, *refs):
    direct_ref, swapped_ref = refs[:2]
    keys, values = list(refs[2 : 2 + count]), list(refs[2 + count : 2 + 2 * count])
    attended_ref, share_ref, *parts = refs[2 + 2 * count : 3 + 2 * count + PARTS]
    first_part, turned_ref, last_keys, last_values, scores_ref, weights_ref, sems = refs[
        3 + 2 * count + PARTS :
    ]
    rows = bias_ref.shape[0]
    heads = value_weight.shape[1] // HEAD_DIM
    copies = []
    for slot, part in enumerate(part_order()):
        target = parts[slot - 1] if slot else first_part
        start = pl.multiple_of(part * target.shape[1], 128)
        source = w_out_ref.at[:, pl.ds(start, target.shape[1])]
        copies.append(pltpu.make_async_copy(source, target, sems.at[slot]))
        copies[-1].start()
    direct = (lax.axis_index("ctx") ^ lax.axis_index("head")) & 1 == 0
    take_if(turned_ref, direct_ref, direct)
    take_if(turned_ref, swapped_ref, jnp.logical_not(direct))
    keys.append(last_keys)
    values.append(last_values)

    def lines(head):
        return slice(head * rows, (head + 1) * rows)

    for start in range(0, count + 1, 2):
        if start + 2 > count:
            expand(turned_ref[...], key_weight, value_weight, last_keys, last_values)
        chosen = keys[start : start + 2]
        stretch = slice(start * rows, (start + len(chosen)) * rows)
        for head in range(heads):
            wide = slice(head * PADDED, (head + 1) * PADDED)
            pair = jnp.concatenate([ref[:, wide] for ref in chosen], axis=0)
            product = lax.dot_general(
                padded_ref[:, wide], pair, NT, preferred_element_type=jnp.float32
            )
            scores_ref[lines(head), stretch] = product + bias_ref[:, stretch]
    peaks = [jnp.max(scores_ref[lines(head), :], axis=1, keepdims=True) for head in range(heads)]
    inverses = []
    for head in range(heads):
        weights = jnp.exp2((scores_ref[lines(head), :] - peaks[head]) * jnp.float32(EXPONENT))
        weights_ref[lines(head), :] = weights.astype(jnp.bfloat16)
        inverses.append(1.0 / jnp.sum(weights, axis=1, keepdims=True))
    for head in range(heads):
        columns = slice(head * HEAD_DIM, (head + 1) * HEAD_DIM)
        value = jnp.dot(
            weights_ref[lines(head), :],
            jnp.concatenate([ref[:, columns] for ref in values], axis=0),
            preferred_element_type=jnp.float32,
        )
        attended_ref[:, columns] = (value * inverses[head]).astype(jnp.bfloat16)
    copies[0].wait()
    project(attended_ref, first_part, [share_ref])
    for copy in copies[1:]:
        copy.wait()


def share_shapes(rows, widths, kind):
    return [jax.ShapeDtypeStruct((rows, width), kind) for width in widths]


def attend(padded, bias, weights, w_out, last, keys, values):
    rows, key_count = bias.shape
    heads = values[0].shape[1] // HEAD_DIM
    width = w_out.shape[1] // PARTS
    part = narrow_shape(w_out.shape[0], width)
    flops = 4 * heads * rows * key_count * PADDED + 4 * rows * weights[0].size
    return pl.pallas_call(
        functools.partial(attend_kernel, len(keys)),
        out_shape=[narrow_shape(rows, heads * HEAD_DIM), narrow_shape(rows, width)]
        + [part] * (PARTS - 1),
        in_specs=[VMEM] * 4 + [HBM] + [VMEM] * (2 + 2 * len(keys)),
        out_specs=[VMEM] * (1 + PARTS),
        scratch_shapes=[
            pltpu.VMEM(part.shape, jnp.bfloat16),
            pltpu.VMEM(last[0].shape, jnp.bfloat16),
            pltpu.VMEM(keys[0].shape, jnp.bfloat16),
            pltpu.VMEM(values[0].shape, jnp.bfloat16),
            pltpu.VMEM((heads * rows, key_count), jnp.float32),
            pltpu.VMEM((heads * rows, key_count), jnp.bfloat16),
            pltpu.SemaphoreType.DMA((PARTS,)),
        ],
        compiler_params=PARAMS,
        cost_estimate=pl.CostEstimate(
            flops=flops + 2 * rows * w_out.size // PARTS,
            bytes_accessed=2 * w_out.size,
            transcendentals=heads * rows * key_count,
        ),
        name="attend",
    )(
        padded,
        bias,
        *weights,
        pltpu.with_memory_space_constraint(w_out, pltpu.HBM),
        *last,
        *keys,
        *values,
    )


def project_kernel(pieces, attended_ref, *refs):
    parts, shares = refs[: len(pieces)], list(refs[len(pieces) :])
    for part_ref, count in zip(parts, pieces):
        project(attended_ref, part_ref, shares[:count])
        shares = shares[count:]


def project_parts(attended, parts, outs):
    flat = [out for group in outs for out in group]
    return pl.pallas_call(
        functools.partial(project_kernel, [len(group) for group in outs]),
        out_shape=flat,
        in_specs=[VMEM] * (1 + len(parts)),
        out_specs=[VMEM] * len(flat),
        compiler_params=PARAMS,
        cost_estimate=SHORT,
        name="project_parts",
    )(attended, *parts)


def next_to(ctx, head):
    return (ctx + 1 + 2 * (head & 1)) & 3, head


def two_away(ctx, head):
    return (ctx ^ 2 if (ctx ^ head) & 1 == 0 else ctx), head


def other_core(ctx, head):
    return ctx, head ^ 1


def other_chip(ctx, head):
    return ctx, head ^ 2


def shards(queries, latent, w_keys, w_values, w_out, block_order, valid_lengths):
    ctx_count = lax.axis_size("ctx")
    rows = queries.shape[0]
    width = w_out.shape[1] // PARTS
    block = latent.T
    prepared = prepare(block_order, valid_lengths, queries, block, w_keys, w_values)
    narrow, wide = jnp.bfloat16, jnp.float32

    if not is_paired():
        blocks = []
        for step in range(1, ctx_count):
            blocks.append(routed(block, lambda ctx, head: ((ctx + step) % ctx_count, head)))
        padded, bias, own_keys, own_values, *weights = prepared
        expanded = [(own_keys, own_values)]
        expanded += [expand_block(piece, *weights) for piece in blocks[:-1]]
        keys, values = zip(*expanded)
        last = [blocks[-1], blocks[-1]]
        attended, share, *parts = attend(padded, bias, weights, w_out, last, keys, values)
        outs = [share_shapes(rows, [width], narrow)] * (PARTS - 1)
        shares = [share] + list(project_parts(attended, parts, outs))
        whole = jnp.concatenate(shares, axis=1)
        return lax.psum_scatter(whole, "head", scatter_dimension=1, tiled=True)

    near = routed(block, next_to)
    far = routed(block, two_away)
    near, prepared = lax.optimization_barrier((near, prepared))
    padded, bias, own_keys, own_values, *weights = prepared
    near_swapped = routed(near, other_core)
    near_keys, near_values = expand_block(near, *weights)
    far, near_keys = lax.optimization_barrier((far, near_keys))
    far_swapped = routed(far, other_core)
    other_keys, other_values = expand_block(near_swapped, *weights)
    keys = [own_keys, near_keys, other_keys]
    values = [own_values, near_values, other_values]
    last = [far, far_swapped]

    attended, across, *parts = attend(padded, bias, weights, w_out, last, keys, values)
    received = routed(across, other_core)
    outs = [share_shapes(rows, [width], kind) for kind in (wide, narrow, wide)]
    far_part, beside, own = project_parts(attended, parts, outs)
    far_part = (far_part + received.astype(wide)).astype(narrow)
    far_part = routed(far_part, other_chip).astype(wide)
    beside = routed(beside, other_core).astype(wide)
    return (own + beside + far_part).astype(narrow)


def solution(mesh):
    in_specs = (
        P(("groups", "ctx"), "head"),
        P(("groups", "ctx"), None),
        P(None, "head"),
        P(None, "head"),
        P("head", None),
        P("groups"),
        P("groups"),
    )
    out_specs = P(("groups", "ctx"), "head")
    return jax.shard_map(shards, mesh=mesh, in_specs=in_specs, out_specs=out_specs, check_vma=False)
```

```python
import functools

import jax
import jax.numpy as jnp
from jax import lax
from jax.experimental import pallas as pl
from jax.experimental.pallas import tpu as pltpu
from jax.sharding import PartitionSpec as P

LATENT = 512
ROPE = 64
HEAD_DIM = 128
QUERY = HEAD_DIM + ROPE
PARTS = 4
PADDED = 256
VMEM_BYTES = 32 * 1024 * 1024
HIDDEN = -1e30


def routed(value, route):
    ctx_count = lax.axis_size("ctx")
    head_count = lax.axis_size("head")
    pairs = []
    for ctx in range(ctx_count):
        for head in range(head_count):
            target = route(ctx, head)
            if target is not None:
                pairs.append((ctx * head_count + head, target[0] * head_count + target[1]))
    return lax.ppermute(value, ("ctx", "head"), pairs)


def is_paired():
    return lax.axis_size("ctx") == 4 and lax.axis_size("head") == 4


def key_sources():
    count = lax.axis_size("ctx")
    ctx = lax.axis_index("ctx")
    if is_paired():
        step = 1 + 2 * (lax.axis_index("head") & 1)
        return [ctx, (ctx - step) & 3, (ctx + step) & 3, ctx ^ 2]
    return [ctx] + [lax.rem(ctx + (count - step), count) for step in range(1, count)]


def part_order():
    if is_paired():
        head = lax.axis_index("head")
        return [head ^ 3, head ^ 2, head ^ 1, head]
    return list(range(PARTS))


VMEM = pl.BlockSpec(memory_space=pltpu.VMEM)
HBM = pl.BlockSpec(memory_space=pltpu.HBM)
PARAMS = pltpu.CompilerParams(vmem_limit_bytes=VMEM_BYTES)
SHORT = pl.CostEstimate(flops=1024, bytes_accessed=1024, transcendentals=0)
EXPONENT = QUERY**-0.5 * 1.4426950408889634


def expand(turned, key_weight, value_weight, keys_ref, values_ref):
    rows = turned.shape[1]
    compressed = turned[:LATENT, :]
    rope = turned[LATENT:, :]
    nothing = jnp.zeros((PADDED - QUERY, rows), jnp.bfloat16)
    nope = jnp.dot(key_weight[...], compressed, preferred_element_type=jnp.float32)
    nope = nope.astype(jnp.bfloat16)
    for head in range(key_weight.shape[0] // HEAD_DIM):
        start = head * PADDED
        keys_ref[start : start + HEAD_DIM, :] = nope[head * HEAD_DIM : (head + 1) * HEAD_DIM, :]
        keys_ref[start + HEAD_DIM : start + QUERY, :] = rope
        keys_ref[start + QUERY : start + PADDED, :] = nothing
    values = jnp.dot(compressed.T, value_weight[...], preferred_element_type=jnp.float32)
    values_ref[...] = values.astype(jnp.bfloat16)


def prepare_kernel(half, *refs):
    order_hbm, lens_hbm, queries_ref, block_ref, w_keys_ref, w_values_ref = refs[:6]
    padded_ref, bias_ref, keys_ref, values_ref, key_weight, value_weight = refs[6:12]
    order_ref, lens_ref, query_buffer, block_buffer, weight_buffer, sems = refs[12:]
    heads = w_keys_ref.shape[1] // HEAD_DIM
    rows = 2 * half
    scalars = [
        pltpu.make_async_copy(order_hbm, order_ref, sems.at[0]),
        pltpu.make_async_copy(lens_hbm, lens_ref, sems.at[1]),
    ]
    query_copy = pltpu.make_async_copy(queries_ref, query_buffer, sems.at[2])
    first = [
        pltpu.make_async_copy(block_ref, block_buffer, sems.at[3]),
        pltpu.make_async_copy(w_keys_ref, weight_buffer, sems.at[4]),
        pltpu.make_async_copy(w_values_ref, value_weight, sems.at[5]),
    ]
    for copy in scalars + [query_copy] + first:
        copy.start()

    for copy in scalars:
        copy.wait()
    ctx = lax.axis_index("ctx")
    row = lax.broadcasted_iota(jnp.int32, (rows, rows), 0)
    lane = lax.broadcasted_iota(jnp.int32, (rows, rows), 1)
    query_pos = jnp.where(row < half, order_ref[2 * ctx], order_ref[2 * ctx + 1]) * half + row % half
    offset = lane % half
    for step, source in enumerate(key_sources()):
        key_place = jnp.where(lane < half, order_ref[2 * source], order_ref[2 * source + 1])
        length = jnp.where(lane < half, lens_ref[2 * source], lens_ref[2 * source + 1])
        visible = (key_place * half + offset <= query_pos) & (offset < length)
        bias_ref[:, step * rows : (step + 1) * rows] = jnp.where(visible, 0.0, HIDDEN)

    query_copy.wait()
    nothing = jnp.zeros((rows, PADDED - QUERY), jnp.bfloat16)
    for head in range(heads):
        query = query_buffer[:, head * QUERY : (head + 1) * QUERY]
        padded_ref[:, head * PADDED : (head + 1) * PADDED] = jnp.concatenate(
            [query, nothing], axis=1
        )
    for copy in first:
        copy.wait()
    key_weight[...] = weight_buffer[...].T
    expand(block_buffer[...], key_weight, value_weight, keys_ref, values_ref)


def narrow_shape(*shape):
    return jax.ShapeDtypeStruct(shape, jnp.bfloat16)


def prepare(*operands):
    order, lens, queries, block, w_keys, w_values = operands
    rows = queries.shape[0]
    count = lax.axis_size("ctx")
    heads = w_keys.shape[1] // HEAD_DIM
    return pl.pallas_call(
        functools.partial(prepare_kernel, rows // 2),
        out_shape=[
            narrow_shape(rows, heads * PADDED),
            jax.ShapeDtypeStruct((rows, count * rows), jnp.float32),
            narrow_shape(heads * PADDED, rows),
            narrow_shape(rows, heads * HEAD_DIM),
            narrow_shape(*w_keys.shape[::-1]),
            narrow_shape(*w_values.shape),
        ],
        in_specs=[HBM] * 6,
        out_specs=[VMEM] * 6,
        scratch_shapes=[
            pltpu.SMEM(order.shape, jnp.int32),
            pltpu.SMEM(lens.shape, jnp.int32),
            pltpu.VMEM(queries.shape, jnp.bfloat16),
            pltpu.VMEM(block.shape, jnp.bfloat16),
            pltpu.VMEM(w_keys.shape, jnp.bfloat16),
            pltpu.SemaphoreType.DMA((6,)),
        ],
        compiler_params=PARAMS,
        cost_estimate=pl.CostEstimate(
            flops=4 * rows * heads * HEAD_DIM * LATENT,
            bytes_accessed=2 * (queries.size + w_keys.size + w_values.size),
            transcendentals=0,
        ),
        name="prepare",
    )(*[pltpu.with_memory_space_constraint(item, pltpu.HBM) for item in operands])


def expand_kernel(block_ref, key_weight, value_weight, keys_ref, values_ref):
    expand(block_ref[...], key_weight, value_weight, keys_ref, values_ref)


def expand_block(block, key_weight, value_weight):
    rows = block.shape[1]
    heads = value_weight.shape[1] // HEAD_DIM
    return pl.pallas_call(
        expand_kernel,
        out_shape=[narrow_shape(heads * PADDED, rows), narrow_shape(rows, heads * HEAD_DIM)],
        in_specs=[VMEM] * 3,
        out_specs=[VMEM] * 2,
        compiler_params=PARAMS,
        cost_estimate=pl.CostEstimate(
            flops=4 * rows * value_weight.size,
            bytes_accessed=2 * value_weight.size,
            transcendentals=0,
        ),
        name="expand_block",
    )(block, key_weight, value_weight)


def project(attended_ref, part_ref, share_refs):
    start = 0
    for share_ref in share_refs:
        stop = start + share_ref.shape[1]
        share = jnp.dot(
            attended_ref[...], part_ref[:, start:stop], preferred_element_type=jnp.float32
        )
        share_ref[...] = share.astype(share_ref.dtype)
        start = stop


def take_if(target_ref, block_ref, condition):
    @pl.when(condition)
    def _():
        target_ref[...] = block_ref[...]


def attend_kernel(count, padded_ref, bias_ref, key_weight, value_weight, w_out_ref, *refs):
    direct_ref, swapped_ref = refs[:2]
    keys, values = list(refs[2 : 2 + count]), list(refs[2 + count : 2 + 2 * count])
    attended_ref, share_ref, *parts = refs[2 + 2 * count : 3 + 2 * count + PARTS]
    first_part, turned_ref, last_keys, last_values, scores_ref, weights_ref, sems = refs[
        3 + 2 * count + PARTS :
    ]
    rows = bias_ref.shape[0]
    heads = value_weight.shape[1] // HEAD_DIM
    copies = []
    for slot, part in enumerate(part_order()):
        target = parts[slot - 1] if slot else first_part
        start = pl.multiple_of(part * target.shape[1], 128)
        source = w_out_ref.at[:, pl.ds(start, target.shape[1])]
        copies.append(pltpu.make_async_copy(source, target, sems.at[slot]))
        copies[-1].start()
    direct = (lax.axis_index("ctx") ^ lax.axis_index("head")) & 1 == 0
    take_if(turned_ref, direct_ref, direct)
    take_if(turned_ref, swapped_ref, jnp.logical_not(direct))
    keys.append(last_keys)
    values.append(last_values)

    def lines(head):
        return slice(head * rows, (head + 1) * rows)

    for start in range(0, count + 1, 2):
        if start + 2 > count:
            expand(turned_ref[...], key_weight, value_weight, last_keys, last_values)
        chosen = keys[start : start + 2]
        stretch = slice(start * rows, (start + len(chosen)) * rows)
        for head in range(heads):
            wide = slice(head * PADDED, (head + 1) * PADDED)
            pair = jnp.concatenate([ref[wide, :] for ref in chosen], axis=1)
            product = jnp.dot(padded_ref[:, wide], pair, preferred_element_type=jnp.float32)
            scores_ref[lines(head), stretch] = product + bias_ref[:, stretch]
    peaks = [jnp.max(scores_ref[lines(head), :], axis=1, keepdims=True) for head in range(heads)]
    inverses = []
    for head in range(heads):
        weights = jnp.exp2((scores_ref[lines(head), :] - peaks[head]) * jnp.float32(EXPONENT))
        weights_ref[lines(head), :] = weights.astype(jnp.bfloat16)
        inverses.append(1.0 / jnp.sum(weights, axis=1, keepdims=True))
    for head in range(heads):
        columns = slice(head * HEAD_DIM, (head + 1) * HEAD_DIM)
        value = jnp.dot(
            weights_ref[lines(head), :],
            jnp.concatenate([ref[:, columns] for ref in values], axis=0),
            preferred_element_type=jnp.float32,
        )
        attended_ref[:, columns] = (value * inverses[head]).astype(jnp.bfloat16)
    copies[0].wait()
    project(attended_ref, first_part, [share_ref])
    for copy in copies[1:]:
        copy.wait()


def share_shapes(rows, widths, kind):
    return [jax.ShapeDtypeStruct((rows, width), kind) for width in widths]


def attend(padded, bias, weights, w_out, last, keys, values):
    rows, key_count = bias.shape
    heads = values[0].shape[1] // HEAD_DIM
    width = w_out.shape[1] // PARTS
    part = narrow_shape(w_out.shape[0], width)
    flops = 4 * heads * rows * key_count * PADDED + 4 * rows * weights[0].size
    return pl.pallas_call(
        functools.partial(attend_kernel, len(keys)),
        out_shape=[narrow_shape(rows, heads * HEAD_DIM), narrow_shape(rows, width)]
        + [part] * (PARTS - 1),
        in_specs=[VMEM] * 4 + [HBM] + [VMEM] * (2 + 2 * len(keys)),
        out_specs=[VMEM] * (1 + PARTS),
        scratch_shapes=[
            pltpu.VMEM(part.shape, jnp.bfloat16),
            pltpu.VMEM(last[0].shape, jnp.bfloat16),
            pltpu.VMEM(keys[0].shape, jnp.bfloat16),
            pltpu.VMEM(values[0].shape, jnp.bfloat16),
            pltpu.VMEM((heads * rows, key_count), jnp.float32),
            pltpu.VMEM((heads * rows, key_count), jnp.bfloat16),
            pltpu.SemaphoreType.DMA((PARTS,)),
        ],
        compiler_params=PARAMS,
        cost_estimate=pl.CostEstimate(
            flops=flops + 2 * rows * w_out.size // PARTS,
            bytes_accessed=2 * w_out.size,
            transcendentals=heads * rows * key_count,
        ),
        name="attend",
    )(
        padded,
        bias,
        *weights,
        pltpu.with_memory_space_constraint(w_out, pltpu.HBM),
        *last,
        *keys,
        *values,
    )


def project_kernel(pieces, attended_ref, *refs):
    parts, shares = refs[: len(pieces)], list(refs[len(pieces) :])
    for part_ref, count in zip(parts, pieces):
        project(attended_ref, part_ref, shares[:count])
        shares = shares[count:]


def project_parts(attended, parts, outs):
    flat = [out for group in outs for out in group]
    return pl.pallas_call(
        functools.partial(project_kernel, [len(group) for group in outs]),
        out_shape=flat,
        in_specs=[VMEM] * (1 + len(parts)),
        out_specs=[VMEM] * len(flat),
        compiler_params=PARAMS,
        cost_estimate=SHORT,
        name="project_parts",
    )(attended, *parts)


def next_to(ctx, head):
    return (ctx + 1 + 2 * (head & 1)) & 3, head


def two_away(ctx, head):
    return (ctx ^ 2 if (ctx ^ head) & 1 == 0 else ctx), head


def other_core(ctx, head):
    return ctx, head ^ 1


def other_chip(ctx, head):
    return ctx, head ^ 2


def shards(queries, latent, w_keys, w_values, w_out, block_order, valid_lengths):
    ctx_count = lax.axis_size("ctx")
    rows = queries.shape[0]
    width = w_out.shape[1] // PARTS
    block = latent.T
    prepared = prepare(block_order, valid_lengths, queries, block, w_keys, w_values)
    narrow, wide = jnp.bfloat16, jnp.float32

    if not is_paired():
        blocks = []
        for step in range(1, ctx_count):
            blocks.append(routed(block, lambda ctx, head: ((ctx + step) % ctx_count, head)))
        padded, bias, own_keys, own_values, *weights = prepared
        expanded = [(own_keys, own_values)]
        expanded += [expand_block(piece, *weights) for piece in blocks[:-1]]
        keys, values = zip(*expanded)
        last = [blocks[-1], blocks[-1]]
        attended, share, *parts = attend(padded, bias, weights, w_out, last, keys, values)
        outs = [share_shapes(rows, [width], narrow)] * (PARTS - 1)
        shares = [share] + list(project_parts(attended, parts, outs))
        whole = jnp.concatenate(shares, axis=1)
        return lax.psum_scatter(whole, "head", scatter_dimension=1, tiled=True)

    near = routed(block, next_to)
    far = routed(block, two_away)
    near, prepared = lax.optimization_barrier((near, prepared))
    padded, bias, own_keys, own_values, *weights = prepared
    near_swapped = routed(near, other_core)
    near_keys, near_values = expand_block(near, *weights)
    far, near_keys = lax.optimization_barrier((far, near_keys))
    far_swapped = routed(far, other_core)
    other_keys, other_values = expand_block(near_swapped, *weights)
    keys = [own_keys, near_keys, other_keys]
    values = [own_values, near_values, other_values]
    last = [far, far_swapped]

    attended, across, *parts = attend(padded, bias, weights, w_out, last, keys, values)
    received = routed(across, other_core)
    outs = [share_shapes(rows, [width], kind) for kind in (wide, narrow, wide)]
    far_part, beside, own = project_parts(attended, parts, outs)
    far_part = (far_part + received.astype(wide)).astype(narrow)
    far_part = routed(far_part, other_chip).astype(wide)
    beside = routed(beside, other_core).astype(wide)
    return (own + beside + far_part).astype(narrow)


def solution(mesh):
    in_specs = (
        P(("groups", "ctx"), "head"),
        P(("groups", "ctx"), None),
        P(None, "head"),
        P(None, "head"),
        P("head", None),
        P("groups"),
        P("groups"),
    )
    out_specs = P(("groups", "ctx"), "head")
    return jax.shard_map(shards, mesh=mesh, in_specs=in_specs, out_specs=out_specs, check_vma=False)
```

```python
import functools

import jax
import jax.numpy as jnp
from jax import lax
from jax.experimental import pallas as pl
from jax.experimental.pallas import tpu as pltpu
from jax.sharding import PartitionSpec as P

LATENT = 512
ROPE = 64
HEAD_DIM = 128
QUERY = HEAD_DIM + ROPE
PARTS = 4
PADDED = 256
VMEM_BYTES = 32 * 1024 * 1024
HIDDEN = -1e30


def routed(value, route):
    ctx_count = lax.axis_size("ctx")
    head_count = lax.axis_size("head")
    pairs = []
    for ctx in range(ctx_count):
        for head in range(head_count):
            target = route(ctx, head)
            if target is not None:
                pairs.append((ctx * head_count + head, target[0] * head_count + target[1]))
    return lax.ppermute(value, ("ctx", "head"), pairs)


def is_paired():
    return lax.axis_size("ctx") == 4 and lax.axis_size("head") == 4


def key_sources():
    count = lax.axis_size("ctx")
    ctx = lax.axis_index("ctx")
    if is_paired():
        step = 1 + 2 * (lax.axis_index("head") & 1)
        return [ctx, (ctx - step) & 3, (ctx + step) & 3, ctx ^ 2]
    return [ctx] + [lax.rem(ctx + (count - step), count) for step in range(1, count)]


def part_order():
    if is_paired():
        head = lax.axis_index("head")
        return [head ^ 3, head ^ 2, head ^ 1, head]
    return list(range(PARTS))


def part_copy(w_out_ref, slot, target, sem):
    width = target.shape[1]
    start = pl.multiple_of(part_order()[slot] * width, 128)
    return pltpu.make_async_copy(w_out_ref.at[:, pl.ds(start, width)], target, sem)


EARLY = 2
VMEM = pl.BlockSpec(memory_space=pltpu.VMEM)
HBM = pl.BlockSpec(memory_space=pltpu.HBM)
PARAMS = pltpu.CompilerParams(vmem_limit_bytes=VMEM_BYTES)
SHORT = pl.CostEstimate(flops=1024, bytes_accessed=1024, transcendentals=0)
EXPONENT = QUERY**-0.5 * 1.4426950408889634


def expand(turned, key_weight, value_weight, keys_ref, values_ref):
    rows = turned.shape[1]
    compressed = turned[:LATENT, :]
    rope = turned[LATENT:, :]
    nothing = jnp.zeros((PADDED - QUERY, rows), jnp.bfloat16)
    nope = jnp.dot(key_weight[...], compressed, preferred_element_type=jnp.float32)
    nope = nope.astype(jnp.bfloat16)
    for head in range(key_weight.shape[0] // HEAD_DIM):
        start = head * PADDED
        keys_ref[start : start + HEAD_DIM, :] = nope[head * HEAD_DIM : (head + 1) * HEAD_DIM, :]
        keys_ref[start + HEAD_DIM : start + QUERY, :] = rope
        keys_ref[start + QUERY : start + PADDED, :] = nothing
    values = jnp.dot(compressed.T, value_weight[...], preferred_element_type=jnp.float32)
    values_ref[...] = values.astype(jnp.bfloat16)


def prepare_kernel(half, *refs):
    order_hbm, lens_hbm, queries_ref, block_ref, w_keys_ref, w_values_ref, w_out_ref = refs[:7]
    padded_ref, bias_ref, keys_ref, values_ref, key_weight, value_weight, *parts = refs[7 : 13 + EARLY]
    order_ref, lens_ref, query_buffer, block_buffer, weight_buffer, sems = refs[13 + EARLY :]
    heads = w_keys_ref.shape[1] // HEAD_DIM
    rows = 2 * half
    scalars = [
        pltpu.make_async_copy(order_hbm, order_ref, sems.at[0]),
        pltpu.make_async_copy(lens_hbm, lens_ref, sems.at[1]),
    ]
    query_copy = pltpu.make_async_copy(queries_ref, query_buffer, sems.at[2])
    first = [
        pltpu.make_async_copy(block_ref, block_buffer, sems.at[3]),
        pltpu.make_async_copy(w_keys_ref, weight_buffer, sems.at[4]),
        pltpu.make_async_copy(w_values_ref, value_weight, sems.at[5]),
    ]
    later = [
        part_copy(w_out_ref, slot, part, sems.at[6 + slot]) for slot, part in enumerate(parts)
    ]
    for copy in scalars + [query_copy] + first + later:
        copy.start()

    for copy in scalars:
        copy.wait()
    ctx = lax.axis_index("ctx")
    row = lax.broadcasted_iota(jnp.int32, (rows, rows), 0)
    lane = lax.broadcasted_iota(jnp.int32, (rows, rows), 1)
    query_pos = jnp.where(row < half, order_ref[2 * ctx], order_ref[2 * ctx + 1]) * half + row % half
    offset = lane % half
    for step, source in enumerate(key_sources()):
        key_place = jnp.where(lane < half, order_ref[2 * source], order_ref[2 * source + 1])
        length = jnp.where(lane < half, lens_ref[2 * source], lens_ref[2 * source + 1])
        visible = (key_place * half + offset <= query_pos) & (offset < length)
        bias_ref[:, step * rows : (step + 1) * rows] = jnp.where(visible, 0.0, HIDDEN)

    query_copy.wait()
    nothing = jnp.zeros((rows, PADDED - QUERY), jnp.bfloat16)
    for head in range(heads):
        query = query_buffer[:, head * QUERY : (head + 1) * QUERY]
        padded_ref[:, head * PADDED : (head + 1) * PADDED] = jnp.concatenate(
            [query, nothing], axis=1
        )
    for copy in first:
        copy.wait()
    key_weight[...] = weight_buffer[...].T
    expand(block_buffer[...], key_weight, value_weight, keys_ref, values_ref)
    for copy in later:
        copy.wait()


def narrow_shape(*shape):
    return jax.ShapeDtypeStruct(shape, jnp.bfloat16)


def prepare(*operands):
    order, lens, queries, block, w_keys, w_values, w_out = operands
    rows = queries.shape[0]
    count = lax.axis_size("ctx")
    heads = w_keys.shape[1] // HEAD_DIM
    return pl.pallas_call(
        functools.partial(prepare_kernel, rows // 2),
        out_shape=[
            narrow_shape(rows, heads * PADDED),
            jax.ShapeDtypeStruct((rows, count * rows), jnp.float32),
            narrow_shape(heads * PADDED, rows),
            narrow_shape(rows, heads * HEAD_DIM),
            narrow_shape(*w_keys.shape[::-1]),
            narrow_shape(*w_values.shape),
        ]
        + [narrow_shape(w_out.shape[0], w_out.shape[1] // PARTS)] * EARLY,
        in_specs=[HBM] * 7,
        out_specs=[VMEM] * (6 + EARLY),
        scratch_shapes=[
            pltpu.SMEM(order.shape, jnp.int32),
            pltpu.SMEM(lens.shape, jnp.int32),
            pltpu.VMEM(queries.shape, jnp.bfloat16),
            pltpu.VMEM(block.shape, jnp.bfloat16),
            pltpu.VMEM(w_keys.shape, jnp.bfloat16),
            pltpu.SemaphoreType.DMA((6 + EARLY,)),
        ],
        compiler_params=PARAMS,
        cost_estimate=pl.CostEstimate(
            flops=4 * rows * heads * HEAD_DIM * LATENT,
            bytes_accessed=2 * (queries.size + w_keys.size + w_values.size) + w_out.size,
            transcendentals=0,
        ),
        name="prepare",
    )(*[pltpu.with_memory_space_constraint(item, pltpu.HBM) for item in operands])


def expand_kernel(block_ref, key_weight, value_weight, keys_ref, values_ref):
    expand(block_ref[...], key_weight, value_weight, keys_ref, values_ref)


def expand_block(block, key_weight, value_weight):
    rows = block.shape[1]
    heads = value_weight.shape[1] // HEAD_DIM
    return pl.pallas_call(
        expand_kernel,
        out_shape=[narrow_shape(heads * PADDED, rows), narrow_shape(rows, heads * HEAD_DIM)],
        in_specs=[VMEM] * 3,
        out_specs=[VMEM] * 2,
        compiler_params=PARAMS,
        cost_estimate=pl.CostEstimate(
            flops=4 * rows * value_weight.size,
            bytes_accessed=2 * value_weight.size,
            transcendentals=0,
        ),
        name="expand_block",
    )(block, key_weight, value_weight)


def project(attended_ref, part_ref, share_refs):
    start = 0
    for share_ref in share_refs:
        stop = start + share_ref.shape[1]
        share = jnp.dot(
            attended_ref[...], part_ref[:, start:stop], preferred_element_type=jnp.float32
        )
        share_ref[...] = share.astype(share_ref.dtype)
        start = stop


def take_if(target_ref, block_ref, condition):
    @pl.when(condition)
    def _():
        target_ref[...] = block_ref[...]


def attend_kernel(count, padded_ref, bias_ref, key_weight, value_weight, part_ref, w_out_ref, *refs):
    direct_ref, swapped_ref = refs[:2]
    keys, values = list(refs[2 : 2 + count]), list(refs[2 + count : 2 + 2 * count])
    attended_ref, share_ref, *parts = refs[2 + 2 * count : 4 + 2 * count + PARTS - EARLY]
    turned_ref, last_keys, last_values, scores_ref, weights_ref, sems = refs[
        4 + 2 * count + PARTS - EARLY :
    ]
    rows = bias_ref.shape[0]
    heads = value_weight.shape[1] // HEAD_DIM
    copies = [
        part_copy(w_out_ref, EARLY + index, part, sems.at[index])
        for index, part in enumerate(parts)
    ]
    for copy in copies:
        copy.start()
    direct = (lax.axis_index("ctx") ^ lax.axis_index("head")) & 1 == 0
    take_if(turned_ref, direct_ref, direct)
    take_if(turned_ref, swapped_ref, jnp.logical_not(direct))
    keys.append(last_keys)
    values.append(last_values)

    def lines(head):
        return slice(head * rows, (head + 1) * rows)

    for start in range(0, count + 1, 2):
        if start + 2 > count:
            expand(turned_ref[...], key_weight, value_weight, last_keys, last_values)
        chosen = keys[start : start + 2]
        stretch = slice(start * rows, (start + len(chosen)) * rows)
        for head in range(heads):
            wide = slice(head * PADDED, (head + 1) * PADDED)
            pair = jnp.concatenate([ref[wide, :] for ref in chosen], axis=1)
            product = jnp.dot(padded_ref[:, wide], pair, preferred_element_type=jnp.float32)
            scores_ref[lines(head), stretch] = product + bias_ref[:, stretch]
    peaks = [jnp.max(scores_ref[lines(head), :], axis=1, keepdims=True) for head in range(heads)]
    inverses = []
    for head in range(heads):
        weights = jnp.exp2((scores_ref[lines(head), :] - peaks[head]) * jnp.float32(EXPONENT))
        weights_ref[lines(head), :] = weights.astype(jnp.bfloat16)
        inverses.append(1.0 / jnp.sum(weights, axis=1, keepdims=True))
    for head in range(heads):
        columns = slice(head * HEAD_DIM, (head + 1) * HEAD_DIM)
        value = jnp.dot(
            weights_ref[lines(head), :],
            jnp.concatenate([ref[:, columns] for ref in values], axis=0),
            preferred_element_type=jnp.float32,
        )
        attended_ref[:, columns] = (value * inverses[head]).astype(jnp.bfloat16)
    project(attended_ref, part_ref, [share_ref])
    for copy in copies:
        copy.wait()


def share_shapes(rows, widths, kind):
    return [jax.ShapeDtypeStruct((rows, width), kind) for width in widths]


def attend(padded, bias, weights, part, w_out, last, keys, values):
    rows, key_count = bias.shape
    heads = values[0].shape[1] // HEAD_DIM
    flops = 4 * heads * rows * key_count * PADDED + 4 * rows * weights[0].size
    return pl.pallas_call(
        functools.partial(attend_kernel, len(keys)),
        out_shape=[narrow_shape(rows, heads * HEAD_DIM), narrow_shape(rows, part.shape[1])]
        + [narrow_shape(*part.shape)] * (PARTS - EARLY),
        in_specs=[VMEM] * 5 + [HBM] + [VMEM] * (2 + 2 * len(keys)),
        out_specs=[VMEM] * (2 + PARTS - EARLY),
        scratch_shapes=[
            pltpu.VMEM(last[0].shape, jnp.bfloat16),
            pltpu.VMEM(keys[0].shape, jnp.bfloat16),
            pltpu.VMEM(values[0].shape, jnp.bfloat16),
            pltpu.VMEM((heads * rows, key_count), jnp.float32),
            pltpu.VMEM((heads * rows, key_count), jnp.bfloat16),
            pltpu.SemaphoreType.DMA((PARTS - EARLY,)),
        ],
        compiler_params=PARAMS,
        cost_estimate=pl.CostEstimate(
            flops=flops + 2 * rows * w_out.size // PARTS,
            bytes_accessed=2 * w_out.size,
            transcendentals=heads * rows * key_count,
        ),
        name="attend",
    )(
        padded,
        bias,
        *weights,
        part,
        pltpu.with_memory_space_constraint(w_out, pltpu.HBM),
        *last,
        *keys,
        *values,
    )


def project_kernel(pieces, attended_ref, *refs):
    parts, shares = refs[: len(pieces)], list(refs[len(pieces) :])
    for part_ref, count in zip(parts, pieces):
        project(attended_ref, part_ref, shares[:count])
        shares = shares[count:]


def project_parts(attended, parts, outs):
    flat = [out for group in outs for out in group]
    return pl.pallas_call(
        functools.partial(project_kernel, [len(group) for group in outs]),
        out_shape=flat,
        in_specs=[VMEM] * (1 + len(parts)),
        out_specs=[VMEM] * len(flat),
        compiler_params=PARAMS,
        cost_estimate=SHORT,
        name="project_parts",
    )(attended, *parts)


def next_to(ctx, head):
    return (ctx + 1 + 2 * (head & 1)) & 3, head


def two_away(ctx, head):
    return (ctx ^ 2 if (ctx ^ head) & 1 == 0 else ctx), head


def other_core(ctx, head):
    return ctx, head ^ 1


def other_chip(ctx, head):
    return ctx, head ^ 2


def shards(queries, latent, w_keys, w_values, w_out, block_order, valid_lengths):
    ctx_count = lax.axis_size("ctx")
    rows = queries.shape[0]
    width = w_out.shape[1] // PARTS
    block = latent.T
    prepared = prepare(block_order, valid_lengths, queries, block, w_keys, w_values, w_out)
    narrow, wide = jnp.bfloat16, jnp.float32

    if not is_paired():
        blocks = []
        for step in range(1, ctx_count):
            blocks.append(routed(block, lambda ctx, head: ((ctx + step) % ctx_count, head)))
        padded, bias, own_keys, own_values, *weights, part, second = prepared
        expanded = [(own_keys, own_values)]
        expanded += [expand_block(piece, *weights) for piece in blocks[:-1]]
        keys, values = zip(*expanded)
        last = [blocks[-1], blocks[-1]]
        attended, share, *parts = attend(
        padded, bias, weights, part, w_out, last, keys, values
    )
        outs = [share_shapes(rows, [width], narrow)] * (PARTS - 1)
        shares = [share] + list(project_parts(attended, [second] + parts, outs))
        whole = jnp.concatenate(shares, axis=1)
        return lax.psum_scatter(whole, "head", scatter_dimension=1, tiled=True)

    near = routed(block, next_to)
    far = routed(block, two_away)
    near, prepared = lax.optimization_barrier((near, prepared))
    padded, bias, own_keys, own_values, *weights, part, second = prepared
    near_swapped = routed(near, other_core)
    near_keys, near_values = expand_block(near, *weights)
    far, near_keys = lax.optimization_barrier((far, near_keys))
    far_swapped = routed(far, other_core)
    other_keys, other_values = expand_block(near_swapped, *weights)
    keys = [own_keys, near_keys, other_keys]
    values = [own_values, near_values, other_values]
    last = [far, far_swapped]

    attended, across, *parts = attend(
        padded, bias, weights, part, w_out, last, keys, values
    )
    received = routed(across, other_core)
    outs = [share_shapes(rows, [width], kind) for kind in (wide, narrow, wide)]
    far_part, beside, own = project_parts(attended, [second] + parts, outs)
    far_part = (far_part + received.astype(wide)).astype(narrow)
    far_part = routed(far_part, other_chip).astype(wide)
    beside = routed(beside, other_core).astype(wide)
    return (own + beside + far_part).astype(narrow)


def solution(mesh):
    in_specs = (
        P(("groups", "ctx"), "head"),
        P(("groups", "ctx"), None),
        P(None, "head"),
        P(None, "head"),
        P("head", None),
        P("groups"),
        P("groups"),
    )
    out_specs = P(("groups", "ctx"), "head")
    return jax.shard_map(shards, mesh=mesh, in_specs=in_specs, out_specs=out_specs, check_vma=False)
```

```python
import functools

import jax
import jax.numpy as jnp
from jax import lax
from jax.experimental import pallas as pl
from jax.experimental.pallas import tpu as pltpu
from jax.sharding import PartitionSpec as P

LATENT = 512
ROPE = 64
HEAD_DIM = 128
QUERY = HEAD_DIM + ROPE
PARTS = 4
PADDED = 256
VMEM_BYTES = 32 * 1024 * 1024
HIDDEN = -1e30


def routed(value, route):
    ctx_count = lax.axis_size("ctx")
    head_count = lax.axis_size("head")
    pairs = []
    for ctx in range(ctx_count):
        for head in range(head_count):
            target = route(ctx, head)
            if target is not None:
                pairs.append((ctx * head_count + head, target[0] * head_count + target[1]))
    return lax.ppermute(value, ("ctx", "head"), pairs)


def is_paired():
    return lax.axis_size("ctx") == 4 and lax.axis_size("head") == 4


def key_sources():
    count = lax.axis_size("ctx")
    ctx = lax.axis_index("ctx")
    if is_paired():
        step = 1 + 2 * (lax.axis_index("head") & 1)
        return [ctx, (ctx - step) & 3, (ctx + step) & 3, ctx ^ 2]
    return [ctx] + [lax.rem(ctx + (count - step), count) for step in range(1, count)]


def part_order():
    if is_paired():
        head = lax.axis_index("head")
        return [head ^ 3, head ^ 2, head ^ 1, head]
    return list(range(PARTS))


def part_copy(w_out_ref, slot, target, sem):
    width = target.shape[1]
    start = pl.multiple_of(part_order()[slot] * width, 128)
    return pltpu.make_async_copy(w_out_ref.at[:, pl.ds(start, width)], target, sem)


EARLY = 2
VMEM = pl.BlockSpec(memory_space=pltpu.VMEM)
HBM = pl.BlockSpec(memory_space=pltpu.HBM)
PARAMS = pltpu.CompilerParams(vmem_limit_bytes=VMEM_BYTES)
SHORT = pl.CostEstimate(flops=1024, bytes_accessed=1024, transcendentals=0)
EXPONENT = QUERY**-0.5 * 1.4426950408889634


def expand(turned, key_weight, value_weight, keys_ref, values_ref):
    rows = turned.shape[1]
    compressed = turned[:LATENT, :]
    rope = turned[LATENT:, :]
    nothing = jnp.zeros((PADDED - QUERY, rows), jnp.bfloat16)
    nope = jnp.dot(key_weight[...], compressed, preferred_element_type=jnp.float32)
    nope = nope.astype(jnp.bfloat16)
    for head in range(key_weight.shape[0] // HEAD_DIM):
        start = head * PADDED
        keys_ref[start : start + HEAD_DIM, :] = nope[head * HEAD_DIM : (head + 1) * HEAD_DIM, :]
        keys_ref[start + HEAD_DIM : start + QUERY, :] = rope
        keys_ref[start + QUERY : start + PADDED, :] = nothing
    values = jnp.dot(compressed.T, value_weight[...], preferred_element_type=jnp.float32)
    values_ref[...] = values.astype(jnp.bfloat16)


def prepare_kernel(half, *refs):
    order_hbm, lens_hbm, queries_ref, block_ref, w_keys_ref, w_values_ref, w_out_ref = refs[:7]
    padded_ref, bias_ref, keys_ref, values_ref, key_weight, value_weight, *parts = refs[7 : 13 + EARLY]
    order_ref, lens_ref, query_buffer, block_buffer, weight_buffer, sems = refs[13 + EARLY :]
    heads = w_keys_ref.shape[1] // HEAD_DIM
    rows = 2 * half
    scalars = [
        pltpu.make_async_copy(order_hbm, order_ref, sems.at[0]),
        pltpu.make_async_copy(lens_hbm, lens_ref, sems.at[1]),
    ]
    query_copy = pltpu.make_async_copy(queries_ref, query_buffer, sems.at[2])
    first = [
        pltpu.make_async_copy(block_ref, block_buffer, sems.at[3]),
        pltpu.make_async_copy(w_keys_ref, weight_buffer, sems.at[4]),
        pltpu.make_async_copy(w_values_ref, value_weight, sems.at[5]),
    ]
    later = [
        part_copy(w_out_ref, slot, part, sems.at[6 + slot]) for slot, part in enumerate(parts)
    ]
    for copy in scalars + [query_copy] + first + later:
        copy.start()

    for copy in scalars:
        copy.wait()
    ctx = lax.axis_index("ctx")
    row = lax.broadcasted_iota(jnp.int32, (rows, rows), 0)
    lane = lax.broadcasted_iota(jnp.int32, (rows, rows), 1)
    query_pos = jnp.where(row < half, order_ref[2 * ctx], order_ref[2 * ctx + 1]) * half + row % half
    offset = lane % half
    for step, source in enumerate(key_sources()):
        key_place = jnp.where(lane < half, order_ref[2 * source], order_ref[2 * source + 1])
        length = jnp.where(lane < half, lens_ref[2 * source], lens_ref[2 * source + 1])
        visible = (key_place * half + offset <= query_pos) & (offset < length)
        bias_ref[:, step * rows : (step + 1) * rows] = jnp.where(visible, 0.0, HIDDEN)

    query_copy.wait()
    nothing = jnp.zeros((rows, PADDED - QUERY), jnp.bfloat16)
    for head in range(heads):
        query = query_buffer[:, head * QUERY : (head + 1) * QUERY]
        padded_ref[:, head * PADDED : (head + 1) * PADDED] = jnp.concatenate(
            [query, nothing], axis=1
        )
    for copy in first:
        copy.wait()
    key_weight[...] = weight_buffer[...].T
    expand(block_buffer[...], key_weight, value_weight, keys_ref, values_ref)
    for copy in later:
        copy.wait()


def narrow_shape(*shape):
    return jax.ShapeDtypeStruct(shape, jnp.bfloat16)


def prepare(*operands):
    order, lens, queries, block, w_keys, w_values, w_out = operands
    rows = queries.shape[0]
    count = lax.axis_size("ctx")
    heads = w_keys.shape[1] // HEAD_DIM
    return pl.pallas_call(
        functools.partial(prepare_kernel, rows // 2),
        out_shape=[
            narrow_shape(rows, heads * PADDED),
            jax.ShapeDtypeStruct((rows, count * rows), jnp.float32),
            narrow_shape(heads * PADDED, rows),
            narrow_shape(rows, heads * HEAD_DIM),
            narrow_shape(*w_keys.shape[::-1]),
            narrow_shape(*w_values.shape),
        ]
        + [narrow_shape(w_out.shape[0], w_out.shape[1] // PARTS)] * EARLY,
        in_specs=[HBM] * 7,
        out_specs=[VMEM] * (6 + EARLY),
        scratch_shapes=[
            pltpu.SMEM(order.shape, jnp.int32),
            pltpu.SMEM(lens.shape, jnp.int32),
            pltpu.VMEM(queries.shape, jnp.bfloat16),
            pltpu.VMEM(block.shape, jnp.bfloat16),
            pltpu.VMEM(w_keys.shape, jnp.bfloat16),
            pltpu.SemaphoreType.DMA((6 + EARLY,)),
        ],
        compiler_params=PARAMS,
        cost_estimate=pl.CostEstimate(
            flops=4 * rows * heads * HEAD_DIM * LATENT,
            bytes_accessed=2 * (queries.size + w_keys.size + w_values.size) + w_out.size,
            transcendentals=0,
        ),
        name="prepare",
    )(*[pltpu.with_memory_space_constraint(item, pltpu.HBM) for item in operands])


def score(padded_ref, bias_ref, first_ref, second_ref, scores_ref, at, into):
    rows = bias_ref.shape[0]
    bias = bias_ref[:, at : at + 2 * rows]
    for head in range(padded_ref.shape[1] // PADDED):
        wide = slice(head * PADDED, (head + 1) * PADDED)
        pair = jnp.concatenate([first_ref[wide, :], second_ref[wide, :]], axis=1)
        product = jnp.dot(padded_ref[:, wide], pair, preferred_element_type=jnp.float32)
        scores_ref[head * rows : (head + 1) * rows, into : into + 2 * rows] = product + bias


def expand_and_score_kernel(
    block_ref, key_weight, value_weight, padded_ref, bias_ref, first_ref, second_ref, *outs
):
    keys_ref, values_ref, scores_ref = outs
    score(padded_ref, bias_ref, first_ref, second_ref, scores_ref, 0, 0)
    expand(block_ref[...], key_weight, value_weight, keys_ref, values_ref)


def expand_and_score(block, key_weight, value_weight, padded, bias, first, second):
    rows = block.shape[1]
    heads = value_weight.shape[1] // HEAD_DIM
    return pl.pallas_call(
        expand_and_score_kernel,
        out_shape=[
            narrow_shape(heads * PADDED, rows),
            narrow_shape(rows, heads * HEAD_DIM),
            jax.ShapeDtypeStruct((heads * rows, 2 * rows), jnp.float32),
        ],
        in_specs=[VMEM] * 7,
        out_specs=[VMEM] * 3,
        compiler_params=PARAMS,
        cost_estimate=pl.CostEstimate(
            flops=4 * rows * value_weight.size + 4 * heads * rows * rows * PADDED,
            bytes_accessed=2 * value_weight.size,
            transcendentals=0,
        ),
        name="expand_and_score",
    )(block, key_weight, value_weight, padded, bias, first, second)


def expand_kernel(block_ref, key_weight, value_weight, keys_ref, values_ref):
    expand(block_ref[...], key_weight, value_weight, keys_ref, values_ref)


def expand_block(block, key_weight, value_weight):
    rows = block.shape[1]
    heads = value_weight.shape[1] // HEAD_DIM
    return pl.pallas_call(
        expand_kernel,
        out_shape=[narrow_shape(heads * PADDED, rows), narrow_shape(rows, heads * HEAD_DIM)],
        in_specs=[VMEM] * 3,
        out_specs=[VMEM] * 2,
        compiler_params=PARAMS,
        cost_estimate=pl.CostEstimate(
            flops=4 * rows * value_weight.size,
            bytes_accessed=2 * value_weight.size,
            transcendentals=0,
        ),
        name="expand_block",
    )(block, key_weight, value_weight)


def project(attended_ref, part_ref, share_refs):
    start = 0
    for share_ref in share_refs:
        stop = start + share_ref.shape[1]
        share = jnp.dot(
            attended_ref[...], part_ref[:, start:stop], preferred_element_type=jnp.float32
        )
        share_ref[...] = share.astype(share_ref.dtype)
        start = stop


def take_if(target_ref, block_ref, condition):
    @pl.when(condition)
    def _():
        target_ref[...] = block_ref[...]


def attend_kernel(count, padded_ref, bias_ref, key_weight, value_weight, part_ref, w_out_ref, *refs):
    direct_ref, swapped_ref, early_ref = refs[:3]
    keys, refs = list(refs[3 : 3 + count]), refs[3 + count :]
    values, refs = list(refs[: count + 2]), refs[count + 2 :]
    attended_ref, share_ref, *parts = refs[: 2 + PARTS - EARLY]
    turned_ref, last_keys, last_values, scores_ref, weights_ref, sems = refs[2 + PARTS - EARLY :]
    rows = bias_ref.shape[0]
    heads = value_weight.shape[1] // HEAD_DIM
    copies = [
        part_copy(w_out_ref, EARLY + index, part, sems.at[index])
        for index, part in enumerate(parts)
    ]
    for copy in copies:
        copy.start()
    direct = (lax.axis_index("ctx") ^ lax.axis_index("head")) & 1 == 0
    take_if(turned_ref, direct_ref, direct)
    take_if(turned_ref, swapped_ref, jnp.logical_not(direct))
    keys.append(last_keys)
    values.append(last_values)

    def lines(head):
        return slice(head * rows, (head + 1) * rows)

    for start in range(0, count + 1, 2):
        if start + 2 > count:
            expand(turned_ref[...], key_weight, value_weight, last_keys, last_values)
        first_ref, second_ref = keys[start : start + 2]
        into = start * rows
        score(padded_ref, bias_ref, first_ref, second_ref, scores_ref, into + 2 * rows, into)
    peaks = []
    for head in range(heads):
        early = jnp.max(early_ref[lines(head), :], axis=1, keepdims=True)
        peaks.append(
            jnp.maximum(early, jnp.max(scores_ref[lines(head), :], axis=1, keepdims=True))
        )
    inverses = []
    for head in range(heads):
        scores = jnp.concatenate([early_ref[lines(head), :], scores_ref[lines(head), :]], axis=1)
        weights = jnp.exp2((scores - peaks[head]) * jnp.float32(EXPONENT))
        weights_ref[lines(head), :] = weights.astype(jnp.bfloat16)
        inverses.append(1.0 / jnp.sum(weights, axis=1, keepdims=True))
    for head in range(heads):
        columns = slice(head * HEAD_DIM, (head + 1) * HEAD_DIM)
        value = jnp.dot(
            weights_ref[lines(head), :],
            jnp.concatenate([ref[:, columns] for ref in values], axis=0),
            preferred_element_type=jnp.float32,
        )
        attended_ref[:, columns] = (value * inverses[head]).astype(jnp.bfloat16)
    project(attended_ref, part_ref, [share_ref])
    for copy in copies:
        copy.wait()


def share_shapes(rows, widths, kind):
    return [jax.ShapeDtypeStruct((rows, width), kind) for width in widths]


def attend(padded, bias, weights, part, w_out, last, early, keys, values):
    rows, key_count = bias.shape
    heads = values[0].shape[1] // HEAD_DIM
    flops = 4 * heads * rows * key_count * PADDED + 4 * rows * weights[0].size
    return pl.pallas_call(
        functools.partial(attend_kernel, len(keys)),
        out_shape=[narrow_shape(rows, heads * HEAD_DIM), narrow_shape(rows, part.shape[1])]
        + [narrow_shape(*part.shape)] * (PARTS - EARLY),
        in_specs=[VMEM] * 5 + [HBM] + [VMEM] * (3 + len(keys) + len(values)),
        out_specs=[VMEM] * (2 + PARTS - EARLY),
        scratch_shapes=[
            pltpu.VMEM(last[0].shape, jnp.bfloat16),
            pltpu.VMEM((heads * PADDED, rows), jnp.bfloat16),
            pltpu.VMEM(values[0].shape, jnp.bfloat16),
            pltpu.VMEM((heads * rows, key_count - 2 * rows), jnp.float32),
            pltpu.VMEM((heads * rows, key_count), jnp.bfloat16),
            pltpu.SemaphoreType.DMA((PARTS - EARLY,)),
        ],
        compiler_params=PARAMS,
        cost_estimate=pl.CostEstimate(
            flops=flops + 2 * rows * w_out.size // PARTS,
            bytes_accessed=2 * w_out.size,
            transcendentals=heads * rows * key_count,
        ),
        name="attend",
    )(
        padded,
        bias,
        *weights,
        part,
        pltpu.with_memory_space_constraint(w_out, pltpu.HBM),
        *last,
        early,
        *keys,
        *values,
    )


def project_kernel(pieces, attended_ref, *refs):
    parts, shares = refs[: len(pieces)], list(refs[len(pieces) :])
    for part_ref, count in zip(parts, pieces):
        project(attended_ref, part_ref, shares[:count])
        shares = shares[count:]


def project_parts(attended, parts, outs):
    flat = [out for group in outs for out in group]
    return pl.pallas_call(
        functools.partial(project_kernel, [len(group) for group in outs]),
        out_shape=flat,
        in_specs=[VMEM] * (1 + len(parts)),
        out_specs=[VMEM] * len(flat),
        compiler_params=PARAMS,
        cost_estimate=SHORT,
        name="project_parts",
    )(attended, *parts)


def next_to(ctx, head):
    return (ctx + 1 + 2 * (head & 1)) & 3, head


def two_away(ctx, head):
    return (ctx ^ 2 if (ctx ^ head) & 1 == 0 else ctx), head


def other_core(ctx, head):
    return ctx, head ^ 1


def other_chip(ctx, head):
    return ctx, head ^ 2


def shards(queries, latent, w_keys, w_values, w_out, block_order, valid_lengths):
    ctx_count = lax.axis_size("ctx")
    rows = queries.shape[0]
    width = w_out.shape[1] // PARTS
    block = latent.T
    prepared = prepare(block_order, valid_lengths, queries, block, w_keys, w_values, w_out)
    narrow, wide = jnp.bfloat16, jnp.float32

    if not is_paired():
        blocks = []
        for step in range(1, ctx_count):
            blocks.append(routed(block, lambda ctx, head: ((ctx + step) % ctx_count, head)))
        padded, bias, own_keys, own_values, *weights, part, second = prepared
        next_keys, next_values = expand_block(blocks[0], *weights)
        third_keys, third_values, early = expand_and_score(
            blocks[1], *weights, padded, bias, own_keys, next_keys
        )
        expanded = [expand_block(piece, *weights) for piece in blocks[2:-1]]
        keys = [third_keys] + [pair[0] for pair in expanded]
        values = [own_values, next_values, third_values] + [pair[1] for pair in expanded]
        last = [blocks[-1], blocks[-1]]
        attended, share, *parts = attend(
            padded, bias, weights, part, w_out, last, early, keys, values
        )
        outs = [share_shapes(rows, [width], narrow)] * (PARTS - 1)
        shares = [share] + list(project_parts(attended, [second] + parts, outs))
        whole = jnp.concatenate(shares, axis=1)
        return lax.psum_scatter(whole, "head", scatter_dimension=1, tiled=True)

    near = routed(block, next_to)
    far = routed(block, two_away)
    near, prepared = lax.optimization_barrier((near, prepared))
    padded, bias, own_keys, own_values, *weights, part, second = prepared
    near_swapped = routed(near, other_core)
    near_keys, near_values = expand_block(near, *weights)
    far, near_keys = lax.optimization_barrier((far, near_keys))
    far_swapped = routed(far, other_core)
    other_keys, other_values, early = expand_and_score(
        near_swapped, *weights, padded, bias, own_keys, near_keys
    )
    keys = [other_keys]
    values = [own_values, near_values, other_values]
    last = [far, far_swapped]

    attended, across, *parts = attend(
        padded, bias, weights, part, w_out, last, early, keys, values
    )
    received = routed(across, other_core)
    outs = [share_shapes(rows, [width], kind) for kind in (wide, narrow, wide)]
    far_part, beside, own = project_parts(attended, [second] + parts, outs)
    far_part = (far_part + received.astype(wide)).astype(narrow)
    far_part = routed(far_part, other_chip).astype(wide)
    beside = routed(beside, other_core).astype(wide)
    return (own + beside + far_part).astype(narrow)


def solution(mesh):
    in_specs = (
        P(("groups", "ctx"), "head"),
        P(("groups", "ctx"), None),
        P(None, "head"),
        P(None, "head"),
        P("head", None),
        P("groups"),
        P("groups"),
    )
    out_specs = P(("groups", "ctx"), "head")
    return jax.shard_map(shards, mesh=mesh, in_specs=in_specs, out_specs=out_specs, check_vma=False)
```

```python
import functools

import jax
import jax.numpy as jnp
from jax import lax
from jax.experimental import pallas as pl
from jax.experimental.pallas import tpu as pltpu
from jax.sharding import PartitionSpec as P

LATENT = 512
ROPE = 64
HEAD_DIM = 128
QUERY = HEAD_DIM + ROPE
PARTS = 4
PADDED = 256
VMEM_BYTES = 32 * 1024 * 1024
HIDDEN = -1e30


def routed(value, route):
    ctx_count = lax.axis_size("ctx")
    head_count = lax.axis_size("head")
    pairs = []
    for ctx in range(ctx_count):
        for head in range(head_count):
            target = route(ctx, head)
            if target is not None:
                pairs.append((ctx * head_count + head, target[0] * head_count + target[1]))
    return lax.ppermute(value, ("ctx", "head"), pairs)


def is_paired():
    return lax.axis_size("ctx") == 4 and lax.axis_size("head") == 4


def key_sources():
    count = lax.axis_size("ctx")
    ctx = lax.axis_index("ctx")
    if is_paired():
        step = 1 + 2 * (lax.axis_index("head") & 1)
        return [ctx, (ctx - step) & 3, (ctx + step) & 3, ctx ^ 2]
    return [ctx] + [lax.rem(ctx + (count - step), count) for step in range(1, count)]


def part_order():
    if is_paired():
        head = lax.axis_index("head")
        return [head ^ 3, head ^ 2, head ^ 1, head]
    return list(range(PARTS))


def part_copy(w_out_ref, slot, target, sem):
    width = target.shape[1]
    start = pl.multiple_of(part_order()[slot] * width, 128)
    return pltpu.make_async_copy(w_out_ref.at[:, pl.ds(start, width)], target, sem)


VMEM = pl.BlockSpec(memory_space=pltpu.VMEM)
HBM = pl.BlockSpec(memory_space=pltpu.HBM)
PARAMS = pltpu.CompilerParams(vmem_limit_bytes=VMEM_BYTES)
SHORT = pl.CostEstimate(flops=1024, bytes_accessed=1024, transcendentals=0)
EXPONENT = QUERY**-0.5 * 1.4426950408889634


def expand(turned, key_weight, value_weight, keys_ref, values_ref):
    rows = turned.shape[1]
    compressed = turned[:LATENT, :]
    rope = turned[LATENT:, :]
    nothing = jnp.zeros((PADDED - QUERY, rows), jnp.bfloat16)
    nope = jnp.dot(key_weight[...], compressed, preferred_element_type=jnp.float32)
    nope = nope.astype(jnp.bfloat16)
    for head in range(key_weight.shape[0] // HEAD_DIM):
        start = head * PADDED
        keys_ref[start : start + HEAD_DIM, :] = nope[head * HEAD_DIM : (head + 1) * HEAD_DIM, :]
        keys_ref[start + HEAD_DIM : start + QUERY, :] = rope
        keys_ref[start + QUERY : start + PADDED, :] = nothing
    values = jnp.dot(compressed.T, value_weight[...], preferred_element_type=jnp.float32)
    values_ref[...] = values.astype(jnp.bfloat16)


def prepare_kernel(half, *refs):
    order_hbm, lens_hbm, queries_ref, block_ref, w_keys_ref, w_values_ref, w_out_ref = refs[:7]
    padded_ref, bias_ref, keys_ref, values_ref, key_weight, value_weight, *parts = refs[7 : 13 + PARTS]
    order_ref, lens_ref, query_buffer, block_buffer, weight_buffer, sems = refs[13 + PARTS :]
    heads = w_keys_ref.shape[1] // HEAD_DIM
    rows = 2 * half
    scalars = [
        pltpu.make_async_copy(order_hbm, order_ref, sems.at[0]),
        pltpu.make_async_copy(lens_hbm, lens_ref, sems.at[1]),
    ]
    query_copy = pltpu.make_async_copy(queries_ref, query_buffer, sems.at[2])
    first = [
        pltpu.make_async_copy(block_ref, block_buffer, sems.at[3]),
        pltpu.make_async_copy(w_keys_ref, weight_buffer, sems.at[4]),
        pltpu.make_async_copy(w_values_ref, value_weight, sems.at[5]),
    ]
    later = [
        part_copy(w_out_ref, slot, part, sems.at[6 + slot]) for slot, part in enumerate(parts)
    ]
    for copy in scalars + [query_copy] + first + later:
        copy.start()

    for copy in scalars:
        copy.wait()
    ctx = lax.axis_index("ctx")
    row = lax.broadcasted_iota(jnp.int32, (rows, rows), 0)
    lane = lax.broadcasted_iota(jnp.int32, (rows, rows), 1)
    query_pos = jnp.where(row < half, order_ref[2 * ctx], order_ref[2 * ctx + 1]) * half + row % half
    offset = lane % half
    for step, source in enumerate(key_sources()):
        key_place = jnp.where(lane < half, order_ref[2 * source], order_ref[2 * source + 1])
        length = jnp.where(lane < half, lens_ref[2 * source], lens_ref[2 * source + 1])
        visible = (key_place * half + offset <= query_pos) & (offset < length)
        bias_ref[:, step * rows : (step + 1) * rows] = jnp.where(visible, 0.0, HIDDEN)

    query_copy.wait()
    nothing = jnp.zeros((rows, PADDED - QUERY), jnp.bfloat16)
    for head in range(heads):
        query = query_buffer[:, head * QUERY : (head + 1) * QUERY]
        padded_ref[:, head * PADDED : (head + 1) * PADDED] = jnp.concatenate(
            [query, nothing], axis=1
        )
    for copy in first:
        copy.wait()
    key_weight[...] = weight_buffer[...].T
    expand(block_buffer[...], key_weight, value_weight, keys_ref, values_ref)
    for copy in later:
        copy.wait()


def narrow_shape(*shape):
    return jax.ShapeDtypeStruct(shape, jnp.bfloat16)


def prepare(*operands):
    order, lens, queries, block, w_keys, w_values, w_out = operands
    rows = queries.shape[0]
    count = lax.axis_size("ctx")
    heads = w_keys.shape[1] // HEAD_DIM
    return pl.pallas_call(
        functools.partial(prepare_kernel, rows // 2),
        out_shape=[
            narrow_shape(rows, heads * PADDED),
            jax.ShapeDtypeStruct((rows, count * rows), jnp.float32),
            narrow_shape(heads * PADDED, rows),
            narrow_shape(rows, heads * HEAD_DIM),
            narrow_shape(*w_keys.shape[::-1]),
            narrow_shape(*w_values.shape),
        ]
        + [narrow_shape(w_out.shape[0], w_out.shape[1] // PARTS)] * PARTS,
        in_specs=[HBM] * 7,
        out_specs=[VMEM] * (6 + PARTS),
        scratch_shapes=[
            pltpu.SMEM(order.shape, jnp.int32),
            pltpu.SMEM(lens.shape, jnp.int32),
            pltpu.VMEM(queries.shape, jnp.bfloat16),
            pltpu.VMEM(block.shape, jnp.bfloat16),
            pltpu.VMEM(w_keys.shape, jnp.bfloat16),
            pltpu.SemaphoreType.DMA((6 + PARTS,)),
        ],
        compiler_params=PARAMS,
        cost_estimate=pl.CostEstimate(
            flops=4 * rows * heads * HEAD_DIM * LATENT,
            bytes_accessed=2 * (queries.size + w_keys.size + w_values.size + w_out.size),
            transcendentals=0,
        ),
        name="prepare",
    )(*[pltpu.with_memory_space_constraint(item, pltpu.HBM) for item in operands])


def score(padded_ref, bias_ref, first_ref, second_ref, scores_ref, at, into):
    rows = bias_ref.shape[0]
    bias = bias_ref[:, at : at + 2 * rows]
    for head in range(padded_ref.shape[1] // PADDED):
        wide = slice(head * PADDED, (head + 1) * PADDED)
        pair = jnp.concatenate([first_ref[wide, :], second_ref[wide, :]], axis=1)
        product = jnp.dot(padded_ref[:, wide], pair, preferred_element_type=jnp.float32)
        scores_ref[head * rows : (head + 1) * rows, into : into + 2 * rows] = product + bias


def expand_and_score_kernel(
    block_ref, key_weight, value_weight, padded_ref, bias_ref, first_ref, second_ref, *outs
):
    keys_ref, values_ref, scores_ref = outs
    score(padded_ref, bias_ref, first_ref, second_ref, scores_ref, 0, 0)
    expand(block_ref[...], key_weight, value_weight, keys_ref, values_ref)


def expand_and_score(block, key_weight, value_weight, padded, bias, first, second):
    rows = block.shape[1]
    heads = value_weight.shape[1] // HEAD_DIM
    return pl.pallas_call(
        expand_and_score_kernel,
        out_shape=[
            narrow_shape(heads * PADDED, rows),
            narrow_shape(rows, heads * HEAD_DIM),
            jax.ShapeDtypeStruct((heads * rows, 2 * rows), jnp.float32),
        ],
        in_specs=[VMEM] * 7,
        out_specs=[VMEM] * 3,
        compiler_params=PARAMS,
        cost_estimate=pl.CostEstimate(
            flops=4 * rows * value_weight.size + 4 * heads * rows * rows * PADDED,
            bytes_accessed=2 * value_weight.size,
            transcendentals=0,
        ),
        name="expand_and_score",
    )(block, key_weight, value_weight, padded, bias, first, second)


def expand_kernel(block_ref, key_weight, value_weight, keys_ref, values_ref):
    expand(block_ref[...], key_weight, value_weight, keys_ref, values_ref)


def expand_block(block, key_weight, value_weight):
    rows = block.shape[1]
    heads = value_weight.shape[1] // HEAD_DIM
    return pl.pallas_call(
        expand_kernel,
        out_shape=[narrow_shape(heads * PADDED, rows), narrow_shape(rows, heads * HEAD_DIM)],
        in_specs=[VMEM] * 3,
        out_specs=[VMEM] * 2,
        compiler_params=PARAMS,
        cost_estimate=pl.CostEstimate(
            flops=4 * rows * value_weight.size,
            bytes_accessed=2 * value_weight.size,
            transcendentals=0,
        ),
        name="expand_block",
    )(block, key_weight, value_weight)


def project(attended_ref, part_ref, share_refs):
    start = 0
    for share_ref in share_refs:
        stop = start + share_ref.shape[1]
        share = jnp.dot(
            attended_ref[...], part_ref[:, start:stop], preferred_element_type=jnp.float32
        )
        share_ref[...] = share.astype(share_ref.dtype)
        start = stop


def take_if(target_ref, block_ref, condition):
    @pl.when(condition)
    def _():
        target_ref[...] = block_ref[...]


def attend_kernel(count, padded_ref, bias_ref, key_weight, value_weight, part_ref, *refs):
    direct_ref, swapped_ref, early_ref = refs[:3]
    keys, refs = list(refs[3 : 3 + count]), refs[3 + count :]
    values, refs = list(refs[: count + 2]), refs[count + 2 :]
    attended_ref, share_ref, turned_ref, last_keys, last_values, scores_ref, weights_ref = refs
    rows = bias_ref.shape[0]
    heads = value_weight.shape[1] // HEAD_DIM
    direct = (lax.axis_index("ctx") ^ lax.axis_index("head")) & 1 == 0
    take_if(turned_ref, direct_ref, direct)
    take_if(turned_ref, swapped_ref, jnp.logical_not(direct))
    keys.append(last_keys)
    values.append(last_values)

    def lines(head):
        return slice(head * rows, (head + 1) * rows)

    for start in range(0, count + 1, 2):
        if start + 2 > count:
            expand(turned_ref[...], key_weight, value_weight, last_keys, last_values)
        first_ref, second_ref = keys[start : start + 2]
        into = start * rows
        score(padded_ref, bias_ref, first_ref, second_ref, scores_ref, into + 2 * rows, into)
    peaks = []
    for head in range(heads):
        early = jnp.max(early_ref[lines(head), :], axis=1, keepdims=True)
        peaks.append(
            jnp.maximum(early, jnp.max(scores_ref[lines(head), :], axis=1, keepdims=True))
        )
    inverses = []
    for head in range(heads):
        scores = jnp.concatenate([early_ref[lines(head), :], scores_ref[lines(head), :]], axis=1)
        weights = jnp.exp2((scores - peaks[head]) * jnp.float32(EXPONENT))
        weights_ref[lines(head), :] = weights.astype(jnp.bfloat16)
        inverses.append(1.0 / jnp.sum(weights, axis=1, keepdims=True))
    for head in range(heads):
        columns = slice(head * HEAD_DIM, (head + 1) * HEAD_DIM)
        value = jnp.dot(
            weights_ref[lines(head), :],
            jnp.concatenate([ref[:, columns] for ref in values], axis=0),
            preferred_element_type=jnp.float32,
        )
        attended_ref[:, columns] = (value * inverses[head]).astype(jnp.bfloat16)
    project(attended_ref, part_ref, [share_ref])


def share_shapes(rows, widths, kind):
    return [jax.ShapeDtypeStruct((rows, width), kind) for width in widths]


def attend(padded, bias, weights, part, last, early, keys, values):
    rows, key_count = bias.shape
    heads = values[0].shape[1] // HEAD_DIM
    flops = 4 * heads * rows * key_count * PADDED + 4 * rows * weights[0].size
    return pl.pallas_call(
        functools.partial(attend_kernel, len(keys)),
        out_shape=[narrow_shape(rows, heads * HEAD_DIM), narrow_shape(rows, part.shape[1])],
        in_specs=[VMEM] * (8 + len(keys) + len(values)),
        out_specs=[VMEM] * 2,
        scratch_shapes=[
            pltpu.VMEM(last[0].shape, jnp.bfloat16),
            pltpu.VMEM((heads * PADDED, rows), jnp.bfloat16),
            pltpu.VMEM(values[0].shape, jnp.bfloat16),
            pltpu.VMEM((heads * rows, key_count - 2 * rows), jnp.float32),
            pltpu.VMEM((heads * rows, key_count), jnp.bfloat16),
        ],
        compiler_params=PARAMS,
        cost_estimate=pl.CostEstimate(
            flops=flops + 2 * rows * part.size,
            bytes_accessed=2 * part.size,
            transcendentals=heads * rows * key_count,
        ),
        name="attend",
    )(
        padded,
        bias,
        *weights,
        part,
        *last,
        early,
        *keys,
        *values,
    )


def project_kernel(pieces, attended_ref, *refs):
    parts, shares = refs[: len(pieces)], list(refs[len(pieces) :])
    for part_ref, count in zip(parts, pieces):
        project(attended_ref, part_ref, shares[:count])
        shares = shares[count:]


def project_parts(attended, parts, outs):
    flat = [out for group in outs for out in group]
    return pl.pallas_call(
        functools.partial(project_kernel, [len(group) for group in outs]),
        out_shape=flat,
        in_specs=[VMEM] * (1 + len(parts)),
        out_specs=[VMEM] * len(flat),
        compiler_params=PARAMS,
        cost_estimate=SHORT,
        name="project_parts",
    )(attended, *parts)


def project_onto_kernel(attended_ref, part_ref, other_ref, sum_ref):
    own = jnp.dot(attended_ref[...], part_ref[...], preferred_element_type=jnp.float32)
    sum_ref[...] = own + other_ref[...].astype(jnp.float32)


def project_onto(attended, part, other):
    return pl.pallas_call(
        project_onto_kernel,
        out_shape=jax.ShapeDtypeStruct(other.shape, jnp.float32),
        in_specs=[VMEM] * 3,
        out_specs=VMEM,
        compiler_params=PARAMS,
        cost_estimate=SHORT,
        name="project_onto",
    )(attended, part, other)


def next_to(ctx, head):
    return (ctx + 1 + 2 * (head & 1)) & 3, head


def two_away(ctx, head):
    return (ctx ^ 2 if (ctx ^ head) & 1 == 0 else ctx), head


def other_core(ctx, head):
    return ctx, head ^ 1


def other_chip(ctx, head):
    return ctx, head ^ 2


def shards(queries, latent, w_keys, w_values, w_out, block_order, valid_lengths):
    ctx_count = lax.axis_size("ctx")
    rows = queries.shape[0]
    width = w_out.shape[1] // PARTS
    block = latent.T
    prepared = prepare(block_order, valid_lengths, queries, block, w_keys, w_values, w_out)
    narrow, wide = jnp.bfloat16, jnp.float32

    if not is_paired():
        blocks = []
        for step in range(1, ctx_count):
            blocks.append(routed(block, lambda ctx, head: ((ctx + step) % ctx_count, head)))
        padded, bias, own_keys, own_values, *weights = prepared
        weights, parts = weights[:2], weights[2:]
        next_keys, next_values = expand_block(blocks[0], *weights)
        third_keys, third_values, early = expand_and_score(
            blocks[1], *weights, padded, bias, own_keys, next_keys
        )
        expanded = [expand_block(piece, *weights) for piece in blocks[2:-1]]
        keys = [third_keys] + [pair[0] for pair in expanded]
        values = [own_values, next_values, third_values] + [pair[1] for pair in expanded]
        last = [blocks[-1], blocks[-1]]
        attended, share = attend(padded, bias, weights, parts[0], last, early, keys, values)
        outs = [share_shapes(rows, [width], narrow)] * (PARTS - 1)
        shares = [share] + list(project_parts(attended, parts[1:], outs))
        whole = jnp.concatenate(shares, axis=1)
        return lax.psum_scatter(whole, "head", scatter_dimension=1, tiled=True)

    near = routed(block, next_to)
    far = routed(block, two_away)
    near, prepared = lax.optimization_barrier((near, prepared))
    padded, bias, own_keys, own_values, *weights = prepared
    weights, parts = weights[:2], weights[2:]
    near_swapped = routed(near, other_core)
    near_keys, near_values = expand_block(near, *weights)
    far, near_keys = lax.optimization_barrier((far, near_keys))
    far_swapped = routed(far, other_core)
    other_keys, other_values, early = expand_and_score(
        near_swapped, *weights, padded, bias, own_keys, near_keys
    )
    keys = [other_keys]
    values = [own_values, near_values, other_values]
    last = [far, far_swapped]

    attended, across = attend(padded, bias, weights, parts[0], last, early, keys, values)
    received = routed(across, other_core)
    outs = [share_shapes(rows, [width], kind) for kind in (wide, narrow)]
    far_part, beside = project_parts(attended, parts[1:3], outs)
    far_part = (far_part + received.astype(wide)).astype(narrow)
    far_part = routed(far_part, other_chip).astype(wide)
    beside = routed(beside, other_core)
    return (project_onto(attended, parts[3], beside) + far_part).astype(narrow)


def solution(mesh):
    in_specs = (
        P(("groups", "ctx"), "head"),
        P(("groups", "ctx"), None),
        P(None, "head"),
        P(None, "head"),
        P("head", None),
        P("groups"),
        P("groups"),
    )
    out_specs = P(("groups", "ctx"), "head")
    return jax.shard_map(shards, mesh=mesh, in_specs=in_specs, out_specs=out_specs, check_vma=False)
```

```python
import functools

import jax
import jax.numpy as jnp
from jax import lax
from jax.experimental import pallas as pl
from jax.experimental.pallas import tpu as pltpu
from jax.sharding import PartitionSpec as P

LATENT = 512
ROPE = 64
HEAD_DIM = 128
QUERY = HEAD_DIM + ROPE
PARTS = 4
PADDED = 256
FIRST_PIECE = 512
VMEM_BYTES = 32 * 1024 * 1024
HIDDEN = -1e30


def routed(value, route):
    ctx_count = lax.axis_size("ctx")
    head_count = lax.axis_size("head")
    pairs = []
    for ctx in range(ctx_count):
        for head in range(head_count):
            target = route(ctx, head)
            if target is not None:
                pairs.append((ctx * head_count + head, target[0] * head_count + target[1]))
    return lax.ppermute(value, ("ctx", "head"), pairs)


def is_paired():
    return lax.axis_size("ctx") == 4 and lax.axis_size("head") == 4


def key_sources():
    count = lax.axis_size("ctx")
    ctx = lax.axis_index("ctx")
    if is_paired():
        step = 1 + 2 * (lax.axis_index("head") & 1)
        return [ctx, (ctx - step) & 3, (ctx + step) & 3, ctx ^ 2]
    return [ctx] + [lax.rem(ctx + (count - step), count) for step in range(1, count)]


def part_order():
    if is_paired():
        head = lax.axis_index("head")
        return [head ^ 3, head ^ 2, head ^ 1, head]
    return list(range(PARTS))


def part_copy(w_out_ref, slot, target, sem):
    width = target.shape[1]
    start = pl.multiple_of(part_order()[slot] * width, 128)
    return pltpu.make_async_copy(w_out_ref.at[:, pl.ds(start, width)], target, sem)


VMEM = pl.BlockSpec(memory_space=pltpu.VMEM)
HBM = pl.BlockSpec(memory_space=pltpu.HBM)
PARAMS = pltpu.CompilerParams(vmem_limit_bytes=VMEM_BYTES)
SHORT = pl.CostEstimate(flops=1024, bytes_accessed=1024, transcendentals=0)
EXPONENT = QUERY**-0.5 * 1.4426950408889634


def expand(turned, key_weight, value_weight, keys_ref, values_ref):
    rows = turned.shape[1]
    compressed = turned[:LATENT, :]
    rope = turned[LATENT:, :]
    nothing = jnp.zeros((PADDED - QUERY, rows), jnp.bfloat16)
    nope = jnp.dot(key_weight[...], compressed, preferred_element_type=jnp.float32)
    nope = nope.astype(jnp.bfloat16)
    for head in range(key_weight.shape[0] // HEAD_DIM):
        start = head * PADDED
        keys_ref[start : start + HEAD_DIM, :] = nope[head * HEAD_DIM : (head + 1) * HEAD_DIM, :]
        keys_ref[start + HEAD_DIM : start + QUERY, :] = rope
        keys_ref[start + QUERY : start + PADDED, :] = nothing
    values = jnp.dot(compressed.T, value_weight[...], preferred_element_type=jnp.float32)
    values_ref[...] = values.astype(jnp.bfloat16)


def prepare_kernel(half, *refs):
    order_hbm, lens_hbm, queries_ref, block_ref, w_keys_ref, w_values_ref, w_out_ref = refs[:7]
    padded_ref, bias_ref, keys_ref, values_ref, key_weight, value_weight, *parts = refs[7 : 13 + PARTS]
    order_ref, lens_ref, query_buffer, block_buffer, weight_buffer, sems = refs[13 + PARTS :]
    heads = w_keys_ref.shape[1] // HEAD_DIM
    rows = 2 * half
    scalars = [
        pltpu.make_async_copy(order_hbm, order_ref, sems.at[0]),
        pltpu.make_async_copy(lens_hbm, lens_ref, sems.at[1]),
    ]
    query_copy = pltpu.make_async_copy(queries_ref, query_buffer, sems.at[2])
    first = [
        pltpu.make_async_copy(block_ref, block_buffer, sems.at[3]),
        pltpu.make_async_copy(w_keys_ref, weight_buffer, sems.at[4]),
        pltpu.make_async_copy(w_values_ref, value_weight, sems.at[5]),
    ]
    later = [
        part_copy(w_out_ref, slot, part, sems.at[6 + slot]) for slot, part in enumerate(parts)
    ]
    for copy in scalars + [query_copy] + first + later:
        copy.start()

    for copy in scalars:
        copy.wait()
    ctx = lax.axis_index("ctx")
    row = lax.broadcasted_iota(jnp.int32, (rows, rows), 0)
    lane = lax.broadcasted_iota(jnp.int32, (rows, rows), 1)
    query_pos = jnp.where(row < half, order_ref[2 * ctx], order_ref[2 * ctx + 1]) * half + row % half
    offset = lane % half
    for step, source in enumerate(key_sources()):
        key_place = jnp.where(lane < half, order_ref[2 * source], order_ref[2 * source + 1])
        length = jnp.where(lane < half, lens_ref[2 * source], lens_ref[2 * source + 1])
        visible = (key_place * half + offset <= query_pos) & (offset < length)
        bias_ref[:, step * rows : (step + 1) * rows] = jnp.where(visible, 0.0, HIDDEN)

    query_copy.wait()
    nothing = jnp.zeros((rows, PADDED - QUERY), jnp.bfloat16)
    for head in range(heads):
        query = query_buffer[:, head * QUERY : (head + 1) * QUERY]
        padded_ref[:, head * PADDED : (head + 1) * PADDED] = jnp.concatenate(
            [query, nothing], axis=1
        )
    for copy in first:
        copy.wait()
    key_weight[...] = weight_buffer[...].T
    expand(block_buffer[...], key_weight, value_weight, keys_ref, values_ref)
    for copy in later:
        copy.wait()


def narrow_shape(*shape):
    return jax.ShapeDtypeStruct(shape, jnp.bfloat16)


def prepare(*operands):
    order, lens, queries, block, w_keys, w_values, w_out = operands
    rows = queries.shape[0]
    count = lax.axis_size("ctx")
    heads = w_keys.shape[1] // HEAD_DIM
    return pl.pallas_call(
        functools.partial(prepare_kernel, rows // 2),
        out_shape=[
            narrow_shape(rows, heads * PADDED),
            jax.ShapeDtypeStruct((rows, count * rows), jnp.float32),
            narrow_shape(heads * PADDED, rows),
            narrow_shape(rows, heads * HEAD_DIM),
            narrow_shape(*w_keys.shape[::-1]),
            narrow_shape(*w_values.shape),
        ]
        + [narrow_shape(w_out.shape[0], w_out.shape[1] // PARTS)] * PARTS,
        in_specs=[HBM] * 7,
        out_specs=[VMEM] * (6 + PARTS),
        scratch_shapes=[
            pltpu.SMEM(order.shape, jnp.int32),
            pltpu.SMEM(lens.shape, jnp.int32),
            pltpu.VMEM(queries.shape, jnp.bfloat16),
            pltpu.VMEM(block.shape, jnp.bfloat16),
            pltpu.VMEM(w_keys.shape, jnp.bfloat16),
            pltpu.SemaphoreType.DMA((6 + PARTS,)),
        ],
        compiler_params=PARAMS,
        cost_estimate=pl.CostEstimate(
            flops=4 * rows * heads * HEAD_DIM * LATENT,
            bytes_accessed=2 * (queries.size + w_keys.size + w_values.size + w_out.size),
            transcendentals=0,
        ),
        name="prepare",
    )(*[pltpu.with_memory_space_constraint(item, pltpu.HBM) for item in operands])


def score(padded_ref, bias_ref, first_ref, second_ref, scores_ref, at, into):
    rows = bias_ref.shape[0]
    bias = bias_ref[:, at : at + 2 * rows]
    for head in range(padded_ref.shape[1] // PADDED):
        wide = slice(head * PADDED, (head + 1) * PADDED)
        pair = jnp.concatenate([first_ref[wide, :], second_ref[wide, :]], axis=1)
        product = jnp.dot(padded_ref[:, wide], pair, preferred_element_type=jnp.float32)
        scores_ref[head * rows : (head + 1) * rows, into : into + 2 * rows] = product + bias


def expand_and_score_kernel(
    block_ref, key_weight, value_weight, padded_ref, bias_ref, first_ref, second_ref, *outs
):
    keys_ref, values_ref, scores_ref = outs
    score(padded_ref, bias_ref, first_ref, second_ref, scores_ref, 0, 0)
    expand(block_ref[...], key_weight, value_weight, keys_ref, values_ref)


def expand_and_score(block, key_weight, value_weight, padded, bias, first, second):
    rows = block.shape[1]
    heads = value_weight.shape[1] // HEAD_DIM
    return pl.pallas_call(
        expand_and_score_kernel,
        out_shape=[
            narrow_shape(heads * PADDED, rows),
            narrow_shape(rows, heads * HEAD_DIM),
            jax.ShapeDtypeStruct((heads * rows, 2 * rows), jnp.float32),
        ],
        in_specs=[VMEM] * 7,
        out_specs=[VMEM] * 3,
        compiler_params=PARAMS,
        cost_estimate=pl.CostEstimate(
            flops=4 * rows * value_weight.size + 4 * heads * rows * rows * PADDED,
            bytes_accessed=2 * value_weight.size,
            transcendentals=0,
        ),
        name="expand_and_score",
    )(block, key_weight, value_weight, padded, bias, first, second)


def expand_kernel(block_ref, key_weight, value_weight, keys_ref, values_ref):
    expand(block_ref[...], key_weight, value_weight, keys_ref, values_ref)


def expand_block(block, key_weight, value_weight):
    rows = block.shape[1]
    heads = value_weight.shape[1] // HEAD_DIM
    return pl.pallas_call(
        expand_kernel,
        out_shape=[narrow_shape(heads * PADDED, rows), narrow_shape(rows, heads * HEAD_DIM)],
        in_specs=[VMEM] * 3,
        out_specs=[VMEM] * 2,
        compiler_params=PARAMS,
        cost_estimate=pl.CostEstimate(
            flops=4 * rows * value_weight.size,
            bytes_accessed=2 * value_weight.size,
            transcendentals=0,
        ),
        name="expand_block",
    )(block, key_weight, value_weight)


def project(attended_ref, part_ref, share_refs):
    start = 0
    for share_ref in share_refs:
        stop = start + share_ref.shape[1]
        share = jnp.dot(
            attended_ref[...], part_ref[:, start:stop], preferred_element_type=jnp.float32
        )
        share_ref[...] = share.astype(share_ref.dtype)
        start = stop


def take_if(target_ref, block_ref, condition):
    @pl.when(condition)
    def _():
        target_ref[...] = block_ref[...]


def attend_kernel(count, padded_ref, bias_ref, key_weight, value_weight, part_ref, *refs):
    direct_ref, swapped_ref, early_ref = refs[:3]
    keys, refs = list(refs[3 : 3 + count]), refs[3 + count :]
    values, refs = list(refs[: count + 2]), refs[count + 2 :]
    attended_ref, *shares, turned_ref, last_keys, last_values, scores_ref, weights_ref = refs
    rows = bias_ref.shape[0]
    heads = value_weight.shape[1] // HEAD_DIM
    direct = (lax.axis_index("ctx") ^ lax.axis_index("head")) & 1 == 0
    take_if(turned_ref, direct_ref, direct)
    take_if(turned_ref, swapped_ref, jnp.logical_not(direct))
    keys.append(last_keys)
    values.append(last_values)

    def lines(head):
        return slice(head * rows, (head + 1) * rows)

    for start in range(0, count + 1, 2):
        if start + 2 > count:
            expand(turned_ref[...], key_weight, value_weight, last_keys, last_values)
        first_ref, second_ref = keys[start : start + 2]
        into = start * rows
        score(padded_ref, bias_ref, first_ref, second_ref, scores_ref, into + 2 * rows, into)
    peaks = []
    for head in range(heads):
        early = jnp.max(early_ref[lines(head), :], axis=1, keepdims=True)
        peaks.append(
            jnp.maximum(early, jnp.max(scores_ref[lines(head), :], axis=1, keepdims=True))
        )
    inverses = []
    for head in range(heads):
        scores = jnp.concatenate([early_ref[lines(head), :], scores_ref[lines(head), :]], axis=1)
        weights = jnp.exp2((scores - peaks[head]) * jnp.float32(EXPONENT))
        weights_ref[lines(head), :] = weights.astype(jnp.bfloat16)
        inverses.append(1.0 / jnp.sum(weights, axis=1, keepdims=True))
    for head in range(heads):
        columns = slice(head * HEAD_DIM, (head + 1) * HEAD_DIM)
        value = jnp.dot(
            weights_ref[lines(head), :],
            jnp.concatenate([ref[:, columns] for ref in values], axis=0),
            preferred_element_type=jnp.float32,
        )
        attended_ref[:, columns] = (value * inverses[head]).astype(jnp.bfloat16)
    project(attended_ref, part_ref, shares)


def share_shapes(rows, widths, kind):
    return [jax.ShapeDtypeStruct((rows, width), kind) for width in widths]


def attend(padded, bias, weights, part, last, early, keys, values, widths):
    rows, key_count = bias.shape
    heads = values[0].shape[1] // HEAD_DIM
    flops = 4 * heads * rows * key_count * PADDED + 4 * rows * weights[0].size
    return pl.pallas_call(
        functools.partial(attend_kernel, len(keys)),
        out_shape=share_shapes(rows, [heads * HEAD_DIM] + widths, jnp.bfloat16),
        in_specs=[VMEM] * (8 + len(keys) + len(values)),
        out_specs=[VMEM] * (1 + len(widths)),
        scratch_shapes=[
            pltpu.VMEM(last[0].shape, jnp.bfloat16),
            pltpu.VMEM((heads * PADDED, rows), jnp.bfloat16),
            pltpu.VMEM(values[0].shape, jnp.bfloat16),
            pltpu.VMEM((heads * rows, key_count - 2 * rows), jnp.float32),
            pltpu.VMEM((heads * rows, key_count), jnp.bfloat16),
        ],
        compiler_params=PARAMS,
        cost_estimate=pl.CostEstimate(
            flops=flops + 2 * rows * part.size,
            bytes_accessed=2 * part.size,
            transcendentals=heads * rows * key_count,
        ),
        name="attend",
    )(
        padded,
        bias,
        *weights,
        part,
        *last,
        early,
        *keys,
        *values,
    )


def project_kernel(pieces, attended_ref, *refs):
    parts, shares = refs[: len(pieces)], list(refs[len(pieces) :])
    for part_ref, count in zip(parts, pieces):
        project(attended_ref, part_ref, shares[:count])
        shares = shares[count:]


def project_parts(attended, parts, outs):
    flat = [out for group in outs for out in group]
    return pl.pallas_call(
        functools.partial(project_kernel, [len(group) for group in outs]),
        out_shape=flat,
        in_specs=[VMEM] * (1 + len(parts)),
        out_specs=[VMEM] * len(flat),
        compiler_params=PARAMS,
        cost_estimate=SHORT,
        name="project_parts",
    )(attended, *parts)


def project_onto_kernel(attended_ref, part_ref, other_ref, sum_ref):
    own = jnp.dot(attended_ref[...], part_ref[...], preferred_element_type=jnp.float32)
    sum_ref[...] = own + other_ref[...].astype(jnp.float32)


def project_onto(attended, part, other):
    return pl.pallas_call(
        project_onto_kernel,
        out_shape=jax.ShapeDtypeStruct(other.shape, jnp.float32),
        in_specs=[VMEM] * 3,
        out_specs=VMEM,
        compiler_params=PARAMS,
        cost_estimate=SHORT,
        name="project_onto",
    )(attended, part, other)


def next_to(ctx, head):
    return (ctx + 1 + 2 * (head & 1)) & 3, head


def two_away(ctx, head):
    return (ctx ^ 2 if (ctx ^ head) & 1 == 0 else ctx), head


def other_core(ctx, head):
    return ctx, head ^ 1


def other_chip(ctx, head):
    return ctx, head ^ 2


def shards(queries, latent, w_keys, w_values, w_out, block_order, valid_lengths):
    ctx_count = lax.axis_size("ctx")
    rows = queries.shape[0]
    width = w_out.shape[1] // PARTS
    block = latent.T
    prepared = prepare(block_order, valid_lengths, queries, block, w_keys, w_values, w_out)
    narrow, wide = jnp.bfloat16, jnp.float32

    if not is_paired():
        blocks = []
        for step in range(1, ctx_count):
            blocks.append(routed(block, lambda ctx, head: ((ctx + step) % ctx_count, head)))
        padded, bias, own_keys, own_values, *weights = prepared
        weights, parts = weights[:2], weights[2:]
        next_keys, next_values = expand_block(blocks[0], *weights)
        third_keys, third_values, early = expand_and_score(
            blocks[1], *weights, padded, bias, own_keys, next_keys
        )
        expanded = [expand_block(piece, *weights) for piece in blocks[2:-1]]
        keys = [third_keys] + [pair[0] for pair in expanded]
        values = [own_values, next_values, third_values] + [pair[1] for pair in expanded]
        last = [blocks[-1], blocks[-1]]
        attended, share = attend(
            padded, bias, weights, parts[0], last, early, keys, values, [width]
        )
        outs = [share_shapes(rows, [width], narrow)] * (PARTS - 1)
        shares = [share] + list(project_parts(attended, parts[1:], outs))
        whole = jnp.concatenate(shares, axis=1)
        return lax.psum_scatter(whole, "head", scatter_dimension=1, tiled=True)

    near = routed(block, next_to)
    far = routed(block, two_away)
    near, prepared = lax.optimization_barrier((near, prepared))
    padded, bias, own_keys, own_values, *weights = prepared
    weights, parts = weights[:2], weights[2:]
    near_swapped = routed(near, other_core)
    near_keys, near_values = expand_block(near, *weights)
    far, near_keys = lax.optimization_barrier((far, near_keys))
    far_swapped = routed(far, other_core)
    other_keys, other_values, early = expand_and_score(
        near_swapped, *weights, padded, bias, own_keys, near_keys
    )
    keys = [other_keys]
    values = [own_values, near_values, other_values]
    last = [far, far_swapped]

    widths = [FIRST_PIECE, width - FIRST_PIECE]
    attended, *across = attend(
        padded, bias, weights, parts[0], last, early, keys, values, widths
    )
    received = [routed(piece, other_core) for piece in across]
    outs = [share_shapes(rows, widths, wide), share_shapes(rows, [width], narrow)]
    *sums, beside = project_parts(attended, parts[1:3], outs)
    sums = [(mine + other.astype(wide)).astype(narrow) for mine, other in zip(sums, received)]
    far_part = jnp.concatenate([routed(piece, other_chip) for piece in sums], axis=1)
    beside = routed(beside, other_core)
    return (project_onto(attended, parts[3], beside) + far_part.astype(wide)).astype(narrow)


def solution(mesh):
    in_specs = (
        P(("groups", "ctx"), "head"),
        P(("groups", "ctx"), None),
        P(None, "head"),
        P(None, "head"),
        P("head", None),
        P("groups"),
        P("groups"),
    )
    out_specs = P(("groups", "ctx"), "head")
    return jax.shard_map(shards, mesh=mesh, in_specs=in_specs, out_specs=out_specs, check_vma=False)
```

```python
import functools

import jax
import jax.numpy as jnp
from jax import lax
from jax.experimental import pallas as pl
from jax.experimental.pallas import tpu as pltpu
from jax.sharding import PartitionSpec as P

LATENT = 512
ROPE = 64
HEAD_DIM = 128
QUERY = HEAD_DIM + ROPE
PARTS = 4
PADDED = 256
VMEM_BYTES = 32 * 1024 * 1024
HIDDEN = -1e30


def routed(value, route):
    ctx_count = lax.axis_size("ctx")
    head_count = lax.axis_size("head")
    pairs = []
    for ctx in range(ctx_count):
        for head in range(head_count):
            target = route(ctx, head)
            if target is not None:
                pairs.append((ctx * head_count + head, target[0] * head_count + target[1]))
    return lax.ppermute(value, ("ctx", "head"), pairs)


def is_paired():
    return lax.axis_size("ctx") == 4 and lax.axis_size("head") == 4


def key_sources():
    count = lax.axis_size("ctx")
    ctx = lax.axis_index("ctx")
    if is_paired():
        step = 1 + 2 * (lax.axis_index("head") & 1)
        return [ctx, (ctx - step) & 3, (ctx + step) & 3, ctx ^ 2]
    return [ctx] + [lax.rem(ctx + (count - step), count) for step in range(1, count)]


def part_order():
    if is_paired():
        head = lax.axis_index("head")
        return [head ^ 3, head ^ 2, head ^ 1, head]
    return list(range(PARTS))


def part_copy(w_out_ref, slot, target, sem):
    width = target.shape[1]
    start = pl.multiple_of(part_order()[slot] * width, 128)
    return pltpu.make_async_copy(w_out_ref.at[:, pl.ds(start, width)], target, sem)


VMEM = pl.BlockSpec(memory_space=pltpu.VMEM)
HBM = pl.BlockSpec(memory_space=pltpu.HBM)
PARAMS = pltpu.CompilerParams(vmem_limit_bytes=VMEM_BYTES)
SHORT = pl.CostEstimate(flops=1024, bytes_accessed=1024, transcendentals=0)
EXPONENT = QUERY**-0.5 * 1.4426950408889634


def expand_keys(turned, key_weight, keys_ref):
    rows = turned.shape[1]
    compressed = turned[:LATENT, :]
    rope = turned[LATENT:, :]
    nothing = jnp.zeros((PADDED - QUERY, rows), jnp.bfloat16)
    nope = jnp.dot(key_weight[...], compressed, preferred_element_type=jnp.float32)
    nope = nope.astype(jnp.bfloat16)
    for head in range(key_weight.shape[0] // HEAD_DIM):
        start = head * PADDED
        keys_ref[start : start + HEAD_DIM, :] = nope[head * HEAD_DIM : (head + 1) * HEAD_DIM, :]
        keys_ref[start + HEAD_DIM : start + QUERY, :] = rope
        keys_ref[start + QUERY : start + PADDED, :] = nothing


def expand_values(turned, value_weight, values_ref):
    compressed = turned[:LATENT, :]
    values = jnp.dot(compressed.T, value_weight[...], preferred_element_type=jnp.float32)
    values_ref[...] = values.astype(jnp.bfloat16)


def expand(turned, key_weight, value_weight, keys_ref, values_ref):
    expand_keys(turned, key_weight, keys_ref)
    expand_values(turned, value_weight, values_ref)


def prepare_kernel(half, *refs):
    order_hbm, lens_hbm, queries_ref, block_ref, w_keys_ref, w_values_ref, w_out_ref = refs[:7]
    padded_ref, bias_ref, keys_ref, values_ref, key_weight, value_weight, *parts = refs[7 : 13 + PARTS]
    order_ref, lens_ref, query_buffer, block_buffer, weight_buffer, sems = refs[13 + PARTS :]
    heads = w_keys_ref.shape[1] // HEAD_DIM
    rows = 2 * half
    scalars = [
        pltpu.make_async_copy(order_hbm, order_ref, sems.at[0]),
        pltpu.make_async_copy(lens_hbm, lens_ref, sems.at[1]),
    ]
    query_copy = pltpu.make_async_copy(queries_ref, query_buffer, sems.at[2])
    first = [
        pltpu.make_async_copy(block_ref, block_buffer, sems.at[3]),
        pltpu.make_async_copy(w_keys_ref, weight_buffer, sems.at[4]),
        pltpu.make_async_copy(w_values_ref, value_weight, sems.at[5]),
    ]
    later = [
        part_copy(w_out_ref, slot, part, sems.at[6 + slot]) for slot, part in enumerate(parts)
    ]
    for copy in scalars + [query_copy] + first + later:
        copy.start()

    for copy in scalars:
        copy.wait()
    ctx = lax.axis_index("ctx")
    row = lax.broadcasted_iota(jnp.int32, (rows, rows), 0)
    lane = lax.broadcasted_iota(jnp.int32, (rows, rows), 1)
    query_pos = jnp.where(row < half, order_ref[2 * ctx], order_ref[2 * ctx + 1]) * half + row % half
    offset = lane % half
    for step, source in enumerate(key_sources()):
        key_place = jnp.where(lane < half, order_ref[2 * source], order_ref[2 * source + 1])
        length = jnp.where(lane < half, lens_ref[2 * source], lens_ref[2 * source + 1])
        visible = (key_place * half + offset <= query_pos) & (offset < length)
        bias_ref[:, step * rows : (step + 1) * rows] = jnp.where(visible, 0.0, HIDDEN)

    query_copy.wait()
    nothing = jnp.zeros((rows, PADDED - QUERY), jnp.bfloat16)
    for head in range(heads):
        query = query_buffer[:, head * QUERY : (head + 1) * QUERY]
        padded_ref[:, head * PADDED : (head + 1) * PADDED] = jnp.concatenate(
            [query, nothing], axis=1
        )
    for copy in first:
        copy.wait()
    key_weight[...] = weight_buffer[...].T
    expand(block_buffer[...], key_weight, value_weight, keys_ref, values_ref)
    for copy in later:
        copy.wait()


def narrow_shape(*shape):
    return jax.ShapeDtypeStruct(shape, jnp.bfloat16)


def prepare(*operands):
    order, lens, queries, block, w_keys, w_values, w_out = operands
    rows = queries.shape[0]
    count = lax.axis_size("ctx")
    heads = w_keys.shape[1] // HEAD_DIM
    return pl.pallas_call(
        functools.partial(prepare_kernel, rows // 2),
        out_shape=[
            narrow_shape(rows, heads * PADDED),
            jax.ShapeDtypeStruct((rows, count * rows), jnp.float32),
            narrow_shape(heads * PADDED, rows),
            narrow_shape(rows, heads * HEAD_DIM),
            narrow_shape(*w_keys.shape[::-1]),
            narrow_shape(*w_values.shape),
        ]
        + [narrow_shape(w_out.shape[0], w_out.shape[1] // PARTS)] * PARTS,
        in_specs=[HBM] * 7,
        out_specs=[VMEM] * (6 + PARTS),
        scratch_shapes=[
            pltpu.SMEM(order.shape, jnp.int32),
            pltpu.SMEM(lens.shape, jnp.int32),
            pltpu.VMEM(queries.shape, jnp.bfloat16),
            pltpu.VMEM(block.shape, jnp.bfloat16),
            pltpu.VMEM(w_keys.shape, jnp.bfloat16),
            pltpu.SemaphoreType.DMA((6 + PARTS,)),
        ],
        compiler_params=PARAMS,
        cost_estimate=pl.CostEstimate(
            flops=4 * rows * heads * HEAD_DIM * LATENT,
            bytes_accessed=2 * (queries.size + w_keys.size + w_values.size + w_out.size),
            transcendentals=0,
        ),
        name="prepare",
    )(*[pltpu.with_memory_space_constraint(item, pltpu.HBM) for item in operands])


def score(padded_ref, bias_ref, first_ref, second_ref, scores_ref, at, into):
    rows = bias_ref.shape[0]
    bias = bias_ref[:, at : at + 2 * rows]
    for head in range(padded_ref.shape[1] // PADDED):
        wide = slice(head * PADDED, (head + 1) * PADDED)
        pair = jnp.concatenate([first_ref[wide, :], second_ref[wide, :]], axis=1)
        product = jnp.dot(padded_ref[:, wide], pair, preferred_element_type=jnp.float32)
        scores_ref[head * rows : (head + 1) * rows, into : into + 2 * rows] = product + bias


def expand_and_score_kernel(
    block_ref, key_weight, value_weight, padded_ref, bias_ref, first_ref, second_ref, *outs
):
    keys_ref, values_ref, scores_ref = outs
    score(padded_ref, bias_ref, first_ref, second_ref, scores_ref, 0, 0)
    expand(block_ref[...], key_weight, value_weight, keys_ref, values_ref)


def expand_and_score(block, key_weight, value_weight, padded, bias, first, second):
    rows = block.shape[1]
    heads = value_weight.shape[1] // HEAD_DIM
    return pl.pallas_call(
        expand_and_score_kernel,
        out_shape=[
            narrow_shape(heads * PADDED, rows),
            narrow_shape(rows, heads * HEAD_DIM),
            jax.ShapeDtypeStruct((heads * rows, 2 * rows), jnp.float32),
        ],
        in_specs=[VMEM] * 7,
        out_specs=[VMEM] * 3,
        compiler_params=PARAMS,
        cost_estimate=pl.CostEstimate(
            flops=4 * rows * value_weight.size + 4 * heads * rows * rows * PADDED,
            bytes_accessed=2 * value_weight.size,
            transcendentals=0,
        ),
        name="expand_and_score",
    )(block, key_weight, value_weight, padded, bias, first, second)


def expand_kernel(block_ref, key_weight, value_weight, keys_ref, values_ref):
    expand(block_ref[...], key_weight, value_weight, keys_ref, values_ref)


def expand_block(block, key_weight, value_weight):
    rows = block.shape[1]
    heads = value_weight.shape[1] // HEAD_DIM
    return pl.pallas_call(
        expand_kernel,
        out_shape=[narrow_shape(heads * PADDED, rows), narrow_shape(rows, heads * HEAD_DIM)],
        in_specs=[VMEM] * 3,
        out_specs=[VMEM] * 2,
        compiler_params=PARAMS,
        cost_estimate=pl.CostEstimate(
            flops=4 * rows * value_weight.size,
            bytes_accessed=2 * value_weight.size,
            transcendentals=0,
        ),
        name="expand_block",
    )(block, key_weight, value_weight)


def project(attended_ref, part_ref, share_refs):
    start = 0
    for share_ref in share_refs:
        stop = start + share_ref.shape[1]
        share = jnp.dot(
            attended_ref[...], part_ref[:, start:stop], preferred_element_type=jnp.float32
        )
        share_ref[...] = share.astype(share_ref.dtype)
        start = stop


def take_if(target_ref, block_ref, condition):
    @pl.when(condition)
    def _():
        target_ref[...] = block_ref[...]


def attend_kernel(count, padded_ref, bias_ref, key_weight, value_weight, part_ref, *refs):
    direct_ref, swapped_ref, early_ref = refs[:3]
    keys, refs = list(refs[3 : 3 + count]), refs[3 + count :]
    values, refs = list(refs[: count + 2]), refs[count + 2 :]
    attended_ref, share_ref, turned_ref, last_keys, last_values, scores_ref, weights_ref = refs
    rows = bias_ref.shape[0]
    heads = value_weight.shape[1] // HEAD_DIM
    direct = (lax.axis_index("ctx") ^ lax.axis_index("head")) & 1 == 0
    take_if(turned_ref, direct_ref, direct)
    take_if(turned_ref, swapped_ref, jnp.logical_not(direct))
    keys.append(last_keys)
    values.append(last_values)

    def lines(head):
        return slice(head * rows, (head + 1) * rows)

    for start in range(0, count + 1, 2):
        if start + 2 > count:
            expand_keys(turned_ref[...], key_weight, last_keys)
        first_ref, second_ref = keys[start : start + 2]
        into = start * rows
        score(padded_ref, bias_ref, first_ref, second_ref, scores_ref, into + 2 * rows, into)
    expand_values(turned_ref[...], value_weight, last_values)
    peaks = []
    for head in range(heads):
        early = jnp.max(early_ref[lines(head), :], axis=1, keepdims=True)
        peaks.append(
            jnp.maximum(early, jnp.max(scores_ref[lines(head), :], axis=1, keepdims=True))
        )
    inverses = []
    for head in range(heads):
        scores = jnp.concatenate([early_ref[lines(head), :], scores_ref[lines(head), :]], axis=1)
        weights = jnp.exp2((scores - peaks[head]) * jnp.float32(EXPONENT))
        weights_ref[lines(head), :] = weights.astype(jnp.bfloat16)
        inverses.append(1.0 / jnp.sum(weights, axis=1, keepdims=True))
    for head in range(heads):
        columns = slice(head * HEAD_DIM, (head + 1) * HEAD_DIM)
        value = jnp.dot(
            weights_ref[lines(head), :],
            jnp.concatenate([ref[:, columns] for ref in values], axis=0),
            preferred_element_type=jnp.float32,
        )
        attended_ref[:, columns] = (value * inverses[head]).astype(jnp.bfloat16)
    project(attended_ref, part_ref, [share_ref])


def share_shapes(rows, widths, kind):
    return [jax.ShapeDtypeStruct((rows, width), kind) for width in widths]


def attend(padded, bias, weights, part, last, early, keys, values):
    rows, key_count = bias.shape
    heads = values[0].shape[1] // HEAD_DIM
    flops = 4 * heads * rows * key_count * PADDED + 4 * rows * weights[0].size
    return pl.pallas_call(
        functools.partial(attend_kernel, len(keys)),
        out_shape=[narrow_shape(rows, heads * HEAD_DIM), narrow_shape(rows, part.shape[1])],
        in_specs=[VMEM] * (8 + len(keys) + len(values)),
        out_specs=[VMEM] * 2,
        scratch_shapes=[
            pltpu.VMEM(last[0].shape, jnp.bfloat16),
            pltpu.VMEM((heads * PADDED, rows), jnp.bfloat16),
            pltpu.VMEM(values[0].shape, jnp.bfloat16),
            pltpu.VMEM((heads * rows, key_count - 2 * rows), jnp.float32),
            pltpu.VMEM((heads * rows, key_count), jnp.bfloat16),
        ],
        compiler_params=PARAMS,
        cost_estimate=pl.CostEstimate(
            flops=flops + 2 * rows * part.size,
            bytes_accessed=2 * part.size,
            transcendentals=heads * rows * key_count,
        ),
        name="attend",
    )(
        padded,
        bias,
        *weights,
        part,
        *last,
        early,
        *keys,
        *values,
    )


def project_kernel(pieces, attended_ref, *refs):
    parts, shares = refs[: len(pieces)], list(refs[len(pieces) :])
    for part_ref, count in zip(parts, pieces):
        project(attended_ref, part_ref, shares[:count])
        shares = shares[count:]


def project_parts(attended, parts, outs):
    flat = [out for group in outs for out in group]
    return pl.pallas_call(
        functools.partial(project_kernel, [len(group) for group in outs]),
        out_shape=flat,
        in_specs=[VMEM] * (1 + len(parts)),
        out_specs=[VMEM] * len(flat),
        compiler_params=PARAMS,
        cost_estimate=SHORT,
        name="project_parts",
    )(attended, *parts)


def project_onto_kernel(attended_ref, part_ref, other_ref, sum_ref):
    own = jnp.dot(attended_ref[...], part_ref[...], preferred_element_type=jnp.float32)
    sum_ref[...] = own + other_ref[...].astype(jnp.float32)


def project_onto(attended, part, other):
    return pl.pallas_call(
        project_onto_kernel,
        out_shape=jax.ShapeDtypeStruct(other.shape, jnp.float32),
        in_specs=[VMEM] * 3,
        out_specs=VMEM,
        compiler_params=PARAMS,
        cost_estimate=SHORT,
        name="project_onto",
    )(attended, part, other)


def next_to(ctx, head):
    return (ctx + 1 + 2 * (head & 1)) & 3, head


def two_away(ctx, head):
    return (ctx ^ 2 if (ctx ^ head) & 1 == 0 else ctx), head


def other_core(ctx, head):
    return ctx, head ^ 1


def other_chip(ctx, head):
    return ctx, head ^ 2


def shards(queries, latent, w_keys, w_values, w_out, block_order, valid_lengths):
    ctx_count = lax.axis_size("ctx")
    rows = queries.shape[0]
    width = w_out.shape[1] // PARTS
    block = latent.T
    prepared = prepare(block_order, valid_lengths, queries, block, w_keys, w_values, w_out)
    narrow, wide = jnp.bfloat16, jnp.float32

    if not is_paired():
        blocks = []
        for step in range(1, ctx_count):
            blocks.append(routed(block, lambda ctx, head: ((ctx + step) % ctx_count, head)))
        padded, bias, own_keys, own_values, *weights = prepared
        weights, parts = weights[:2], weights[2:]
        next_keys, next_values = expand_block(blocks[0], *weights)
        third_keys, third_values, early = expand_and_score(
            blocks[1], *weights, padded, bias, own_keys, next_keys
        )
        expanded = [expand_block(piece, *weights) for piece in blocks[2:-1]]
        keys = [third_keys] + [pair[0] for pair in expanded]
        values = [own_values, next_values, third_values] + [pair[1] for pair in expanded]
        last = [blocks[-1], blocks[-1]]
        attended, share = attend(padded, bias, weights, parts[0], last, early, keys, values)
        outs = [share_shapes(rows, [width], narrow)] * (PARTS - 1)
        shares = [share] + list(project_parts(attended, parts[1:], outs))
        whole = jnp.concatenate(shares, axis=1)
        return lax.psum_scatter(whole, "head", scatter_dimension=1, tiled=True)

    near = routed(block, next_to)
    far = routed(block, two_away)
    near, prepared = lax.optimization_barrier((near, prepared))
    padded, bias, own_keys, own_values, *weights = prepared
    weights, parts = weights[:2], weights[2:]
    near_swapped = routed(near, other_core)
    near_keys, near_values = expand_block(near, *weights)
    far, near_keys = lax.optimization_barrier((far, near_keys))
    far_swapped = routed(far, other_core)
    other_keys, other_values, early = expand_and_score(
        near_swapped, *weights, padded, bias, own_keys, near_keys
    )
    keys = [other_keys]
    values = [own_values, near_values, other_values]
    last = [far, far_swapped]

    attended, across = attend(padded, bias, weights, parts[0], last, early, keys, values)
    received = routed(across, other_core)
    outs = [share_shapes(rows, [width], kind) for kind in (wide, narrow)]
    far_part, beside = project_parts(attended, parts[1:3], outs)
    far_part = (far_part + received.astype(wide)).astype(narrow)
    far_part = routed(far_part, other_chip).astype(wide)
    beside = routed(beside, other_core)
    return (project_onto(attended, parts[3], beside) + far_part).astype(narrow)


def solution(mesh):
    in_specs = (
        P(("groups", "ctx"), "head"),
        P(("groups", "ctx"), None),
        P(None, "head"),
        P(None, "head"),
        P("head", None),
        P("groups"),
        P("groups"),
    )
    out_specs = P(("groups", "ctx"), "head")
    return jax.shard_map(shards, mesh=mesh, in_specs=in_specs, out_specs=out_specs, check_vma=False)
```
